512 devices in a mesh: idx: 64 (over z, y), mdl: 8 (over x, core).
Axes of the slice: x: 4, y: 8, z: 8, core: 2. Of those that a mesh axis runs over, the one named last changes fastest.
Arguments:
- index_emb: bfloat16 [8192, 768], P('idx'), may hold values from -6 to 6
- query_emb: bfloat16 [128, 768], P('idx'), may hold values from -6 to 6
- passage_owner: int32 [2560, 1], P('idx'), may hold values from 0 to 63; in each aligned block of 40 rows (0 to 39, 40 to 79, ...) at most 3 rows name the same one
- passage_row: int32 [2560], P('idx'), may hold values from 0 to 127
- token_ids: int32 [2560, 4], P('idx'), may hold values from 0 to 16383
- vocab_table: bfloat16 [16384, 2048], P('idx', 'mdl'), may hold values from -3 to 3
- w_query: bfloat16 [2048, 1024], P(None, 'mdl'), may hold values from -0.125 to 0.125
- w_key: bfloat16 [2048, 1024], P(None, 'mdl'), may hold values from -0.125 to 0.125
- w_value: bfloat16 [2048, 1024], P(None, 'mdl'), may hold values from -0.125 to 0.125
- w_out: bfloat16 [1024, 2048], P('mdl'), may hold values from -0.1875 to 0.1875
- out_grad: bfloat16 [10240, 2048], P('idx', 'mdl'), may hold values from -6 to 6
- slab_emb: bfloat16 [4096, 768], P('idx'), may hold values from -6 to 6
- slab_ids: int32 [4096], P('idx'), may hold values from 0 to 8191, as said below
Outputs:
- relevance: float32 [128, 20], P('idx')
- grad_query: float32 [2048, 1024], P('idx', 'mdl')
- grad_key: float32 [2048, 1024], P('idx', 'mdl')
- grad_value: float32 [2048, 1024], P('idx', 'mdl')
- grad_out: float32 [1024, 2048], P('mdl', 'idx')
- refreshed_index: bfloat16 [8192, 768], P('idx')
The draws below stay inside these ranges and needn't reach their ends.
Inputs may be any that keep to these rules, and one draw needn't show every extreme that they name: `passage_owner`: among the 40 passages of one device's queries no owner appears more than 3 times. `slab_ids`: the ids are distinct; the 64 ids of one device name exactly 2 passages of each of 32 owners, the owner of an id being id // 128.
All inputs are finite; a program needn't handle non-finite values.
Results may differ from the reference program's by a relative error of at most 0.009.
The reference program's roundings to bfloat16 on the way (of `fetched`, `tokens`, `attn`, `context`, `weighted`, `context_grad`, `value_grad` and `score_grad`) count: a program that leaves them out, or rounds other values in their place, can miss the bound.
Values may be sent and summed in bfloat16 or wider, within the bound.
No kernel may reach another device: no remote copies, remote signals or barrier semaphores. Data moves between devices by JAX's collectives and lax.ppermute only.
A program may use at most 64 MiB of HBM per device.

```python
import math
import jax
import jax.numpy as jnp
import numpy as np
from jax import lax

E = 768
D = 2048
HEADS = 16
HEAD_DIM = 64
INNER = 1024
VOCAB = 16384
K = 20
PLEN = 4
Q_DEV = 2
PASS_DEV = 128
CAPS = 2
SLAB_DEV = 64
CAP = 3
QUERIES = 128
NPASS = 8192
SLAB = 4096
TOKENS = 10240
N_IDX = 64


def draw_query_emb(key, part):
    key = jax.random.fold_in(key, 5)
    first = jax.random.fold_in(key, 0)
    base = jnp.clip(jax.random.normal(first, (QUERIES, E)), -6.0, 6.0)
    return (0.15 * base).astype(jnp.bfloat16)


def draw_vocab_table(key, part):
    key = jax.random.fold_in(key, 7)
    first = jax.random.fold_in(key, 0)
    return (0.5 * jnp.clip(jax.random.normal(first, (VOCAB, D)), -6.0, 6.0)).astype(jnp.bfloat16)


def draw_slab_ids(key, part):
    key = jax.random.fold_in(key, 11)
    first, second = jax.random.split(key)
    orders = jax.vmap(lambda sub: jax.random.permutation(sub, N_IDX))(jax.random.split(first, N_IDX))
    slot = jnp.arange(SLAB_DEV, dtype=jnp.int32)
    owner = orders[:, slot // CAPS].astype(jnp.int32)
    offset = jax.random.randint(second, (N_IDX,), 0, PASS_DEV).astype(jnp.int32)
    source = jnp.arange(N_IDX, dtype=jnp.int32)[:, None]
    row = (offset[owner] + source * CAPS + slot[None, :] % CAPS) % PASS_DEV
    return (owner * PASS_DEV + row).reshape(-1).astype(jnp.int32)


def with_ends(array, stream_key, smallest, largest):
    index_at = [jax.random.randint(jax.random.fold_in(stream_key, axis), (), 0, length) for axis, length in enumerate(array.shape)]
    widest = array.shape.index(max(array.shape))
    next_to = index_at[:widest] + [(index_at[widest] + 1) % array.shape[widest]] + index_at[widest + 1:]
    return array.at[tuple(index_at)].set(smallest).at[tuple(next_to)].set(largest)


def block_scale(key, shape, cuts, low, largest):
    factor_of = 1.0
    for position, blocks in cuts:
        steps = jax.random.uniform(jax.random.fold_in(jax.random.fold_in(key, 6), position), (blocks,), jnp.float32, low / len(cuts), largest / len(cuts))
        factor_of = factor_of * jnp.repeat(jnp.exp(steps), shape[position] // blocks).reshape((-1,) + (1,) * (len(shape) - 1 - position))
    return factor_of


def rank_table(number_of, slope):
    loads = [(1 << 20) // math.isqrt(rank ** slope) + 1 for rank in range(1, number_of + 1)]
    scale = 1 + sum(loads) // (1 << 30)
    return np.cumsum(np.array([max(1, weight // scale) for weight in loads]))


def ranked(own_key, shape, count, slope):
    grid = rank_table(count, slope)
    pick = jax.random.randint(jax.random.fold_in(own_key, 1), shape, 0, int(grid[count - 1]))
    grade = jnp.searchsorted(jnp.asarray(grid, jnp.int32), pick, side="right")
    return jax.random.permutation(jax.random.fold_in(own_key, 2), count)[grade].astype(jnp.int32)


def deal_out(key, own, number, rows, count, top, limit, skew):
    sequence = jax.random.permutation(key, count)
    packed, usual = shares(count, rows * top, limit, skew, True), shares(count, rows * top, limit, skew, False)
    places = jnp.arange(count)

    def named(tallies, turn):
        used = int((tallies > 0).sum())
        fixed = max(1, used // 4)
        moved = fixed + (places - fixed + turn * (used - fixed)) % max(1, count - fixed)
        return jnp.zeros((count,), jnp.int32).at[sequence[jnp.where(places < fixed, places, moved)]].set(jnp.asarray(tallies, jnp.int32))

    tallies = jnp.where(number % 4 == 0, named(packed, number // 4), named(usual, number - number // 4 - 1))
    mixed = jax.random.permutation(jax.random.fold_in(own, 3), count)
    donor, receiver = mixed[0:count // 2 * 2:2], mixed[1:count // 2 * 2:2]
    room = jnp.minimum(tallies[donor] - 1, limit - tallies[receiver]) // 2
    room = jnp.where((donor == sequence[0]) | (receiver == sequence[0]) | (tallies[receiver] == 0), 0, jnp.maximum(room, 0))
    moved = jax.random.randint(jax.random.fold_in(own, 4), (count // 2,), 0, 1 << 20) % (room + 1)
    tallies = tallies.at[donor].add(-moved).at[receiver].add(moved)
    members = jnp.searchsorted(jnp.cumsum(tallies), jnp.arange(rows * top), side="right").astype(jnp.int32)
    grid = members.reshape(top, rows).T
    grid = grid[jax.random.permutation(jax.random.fold_in(own, 1), rows)]
    turn = jax.random.randint(jax.random.fold_in(own, 2), (rows, 1), 0, top)
    return jnp.take_along_axis(grid, (jnp.arange(top)[None, :] + turn) % top, axis=1)


def shares(amount, total, most, skew, full):
    loads = [(1 << 20) // math.isqrt(rank ** skew) + 1 for rank in range(1, amount + 1)]
    largest = most if full else min(most, max(-(-total // amount), total * loads[0] // sum(loads)))
    least = 1 if total - largest >= amount - 1 else 0
    holding, rest = [largest] + [least] * (amount - 1), total - largest - least * (amount - 1)
    while rest > 0:
        free = [i for i in range(1, amount) if holding[i] < largest] or [i for i in range(1, amount) if holding[i] < most]
        whole, remaining = sum([loads[i] for i in free]), rest
        for i in free:
            more = min(most - holding[i], max(1, remaining * loads[i] // whole), rest)
            holding[i] = holding[i] + more
            rest = rest - more
    return np.array(holding)


def scatter_about(own_key, dims, deviation, most, cuts=(), kind=jnp.bfloat16):
    array = deviation * jax.random.normal(own_key, dims, jnp.float32)
    if cuts:
        array = array * block_scale(own_key, dims, cuts, -0.22, 0.18)
    return jnp.clip(array, -most, most).astype(kind)


def setup_inputs(seed: int = 0) -> dict:
    keys = jax.random.split(jax.random.key(seed), 14)
    index_emb = scatter_about(keys[0], (NPASS, E), 1.0, 6.0, ((0, 64),))
    query_emb = draw_query_emb(jax.random.fold_in(keys[13], 71), 0)
    passage_owner_keys = jax.random.split(jax.random.fold_in(keys[2], 1), (QUERIES * K) // (Q_DEV * K))
    passage_owner_turns = jax.random.permutation(jax.random.fold_in(keys[2], 3), (QUERIES * K) // (Q_DEV * K))
    passage_owner = jax.vmap(lambda own, number: deal_out(jax.random.fold_in(keys[2], 2), own, number, Q_DEV * K, N_IDX, 1, CAP, 2))(passage_owner_keys, passage_owner_turns).reshape((QUERIES * K, 1))
    passage_row = with_ends(jax.random.randint(keys[3], (QUERIES * K,), 0, PASS_DEV), jax.random.fold_in(keys[3], 1), 0, PASS_DEV - 1).astype(jnp.int32)
    token_ids = with_ends(ranked(keys[4], (QUERIES * K, PLEN), VOCAB, 2), jax.random.fold_in(keys[4], 3), 0, VOCAB - 1).astype(jnp.int32)
    vocab_table = draw_vocab_table(jax.random.fold_in(keys[13], 71), 0)
    w_query = scatter_about(keys[6], (D, INNER), D ** -0.5, 0.125, ((1, 8),))
    w_key = scatter_about(keys[7], (D, INNER), D ** -0.5, 0.125, ((1, 8),))
    w_value = scatter_about(keys[8], (D, INNER), D ** -0.5, 0.125, ((1, 8),))
    w_out = scatter_about(keys[9], (INNER, D), INNER ** -0.5, 0.1875, ((0, 8),))
    out_grad = scatter_about(keys[10], (TOKENS, D), 1.0, 6.0, ((0, 64), (1, 8)))
    slab_emb = scatter_about(keys[11], (SLAB, E), 1.0, 6.0, ((0, 64),))
    slab_ids = draw_slab_ids(jax.random.fold_in(keys[13], 71), 0)
    return dict(index_emb=index_emb, query_emb=query_emb, passage_owner=passage_owner, passage_row=passage_row, token_ids=token_ids, vocab_table=vocab_table, w_query=w_query, w_key=w_key, w_value=w_value, w_out=w_out, out_grad=out_grad, slab_emb=slab_emb, slab_ids=slab_ids)


def reference(index_emb, query_emb, passage_owner, passage_row, token_ids, vocab_table, w_query, w_key, w_value, w_out, out_grad, slab_emb, slab_ids):
    npass = QUERIES * K
    flat_ids = passage_owner[:, 0] * PASS_DEV + passage_row
    fetched = jnp.take(index_emb, flat_ids, axis=0).reshape(QUERIES, K, E)
    scores = jnp.einsum('qke,qe->qk', fetched.astype(jnp.float32), query_emb.astype(jnp.float32))
    relevance = jax.nn.softmax(scores, axis=-1)
    tokens = jnp.take(vocab_table, token_ids.reshape(-1), axis=0)

    def project(weight):
        states = jnp.dot(tokens, weight, preferred_element_type=jnp.float32).astype(jnp.bfloat16)
        return states.reshape(npass, PLEN, HEADS, HEAD_DIM)
    query_states = project(w_query)
    key_states = project(w_key)
    value_states = project(w_value)
    logits = jnp.einsum('pihd,pjhd->phij', query_states.astype(jnp.float32), key_states.astype(jnp.float32))
    probs = jax.nn.softmax(logits, axis=-1)
    attn = probs.astype(jnp.bfloat16)
    context = jnp.einsum('phij,pjhd->pihd', attn.astype(jnp.float32), value_states.astype(jnp.float32)).astype(jnp.bfloat16)
    flat_context = context.reshape(npass * PLEN, INNER)
    weighted = (out_grad.reshape(npass, PLEN, D).astype(jnp.float32) * relevance.reshape(npass, 1, 1)).astype(jnp.bfloat16).reshape(npass * PLEN, D)
    grad_out = jnp.dot(flat_context.T, weighted, preferred_element_type=jnp.float32)
    context_grad = jnp.dot(weighted, w_out.T, preferred_element_type=jnp.float32).astype(jnp.bfloat16).reshape(npass, PLEN, HEADS, HEAD_DIM)
    attn_grad = jnp.einsum('pihd,pjhd->phij', context_grad.astype(jnp.float32), value_states.astype(jnp.float32))
    value_grad = jnp.einsum('phij,pihd->pjhd', attn.astype(jnp.float32), context_grad.astype(jnp.float32)).astype(jnp.bfloat16)
    score_grad = (probs * (attn_grad - lax.optimization_barrier(jnp.sum(attn_grad * probs, axis=-1, keepdims=True)))).astype(jnp.bfloat16)
    query_grad = jnp.einsum('phij,pjhd->pihd', score_grad.astype(jnp.float32), key_states.astype(jnp.float32)).astype(jnp.bfloat16)
    key_grad = jnp.einsum('phij,pihd->pjhd', score_grad.astype(jnp.float32), query_states.astype(jnp.float32)).astype(jnp.bfloat16)

    def weight_grad(states):
        return jnp.dot(tokens.T, states.reshape(npass * PLEN, INNER), preferred_element_type=jnp.float32)
    grad_query = weight_grad(query_grad)
    grad_key = weight_grad(key_grad)
    grad_value = weight_grad(value_grad)
    refreshed_index = index_emb.at[slab_ids].set(slab_emb)
    return (relevance, grad_query, grad_key, grad_value, grad_out, refreshed_index)
```

```python
import jax
import jax.numpy as jnp
from jax import lax
from jax.experimental import pallas as pl
from jax.experimental.pallas import tpu as pltpu
from jax.sharding import Mesh
from jax.sharding import PartitionSpec as P

HEAD_DIM = 64
K = 20
PLEN = 4
CAPS = 2
LANES = 128
IDX = ("z", "y")
F32 = jnp.float32
BF16 = jnp.bfloat16
ROWS = (((0,), (0,)), ((), ()))
COLS = (((1,), (1,)), ((), ()))


def dot(a, b, dims=None):
    if dims is None:
        return jnp.dot(a, b, preferred_element_type=F32)
    return lax.dot_general(a, b, dims, preferred_element_type=F32)


def reader_kernel(tokens_ref, grad_ref, rel_ref, wq_ref, wk_ref, wv_ref, wo_ref, out_ref):
    tokens = tokens_ref[...]
    count, inner = tokens.shape[0], wq_ref.shape[1]
    owners = out_ref.shape[0]
    rows = out_ref.shape[1] // 4
    query = dot(tokens, wq_ref[...]).astype(BF16)
    key = dot(tokens, wk_ref[...]).astype(BF16)
    value = dot(tokens, wv_ref[...]).astype(BF16)
    weighted = (grad_ref[...].astype(F32) * rel_ref[...]).astype(BF16)
    context_grad = dot(weighted, wo_ref[...], COLS).astype(BF16)
    passage_i = lax.broadcasted_iota(jnp.int32, (count, count), 0) // PLEN
    passage_j = lax.broadcasted_iota(jnp.int32, (count, count), 1) // PLEN
    same = passage_i == passage_j
    parts = [], [], [], []
    for head in range(inner // HEAD_DIM):
        cols = slice(head * HEAD_DIM, (head + 1) * HEAD_DIM)
        q, k, v, c = query[:, cols], key[:, cols], value[:, cols], context_grad[:, cols]
        logits = jnp.where(same, dot(q, k, COLS), -jnp.inf)
        exps = jnp.exp(logits - jnp.max(logits, axis=1, keepdims=True))
        probs = exps / jnp.sum(exps, axis=1, keepdims=True)
        attn = probs.astype(BF16)
        attn_grad = dot(c, v, COLS)
        mean = jnp.sum(attn_grad * probs, axis=1, keepdims=True)
        score_grad = (probs * (attn_grad - mean)).astype(BF16)
        parts[0].append(dot(score_grad, k).astype(BF16))
        parts[1].append(dot(score_grad, q, ROWS).astype(BF16))
        parts[2].append(dot(attn, c, ROWS).astype(BF16))
        parts[3].append(dot(attn, v).astype(BF16))
    query_grad, key_grad, value_grad, context = (jnp.concatenate(p, axis=1) for p in parts)
    for place, (left, right) in enumerate(
        ((tokens, query_grad), (tokens, key_grad), (tokens, value_grad), (weighted, context))
    ):
        term = dot(left, right, ROWS).astype(BF16)
        out_ref[:, place * rows : (place + 1) * rows, :] = term.reshape(owners, rows, inner)


def reader(tokens, out_grad, rel, w_query, w_key, w_value, w_out, owners):
    width, inner = w_query.shape
    return pl.pallas_call(
        reader_kernel,
        out_shape=jax.ShapeDtypeStruct((owners, 4 * width // owners, inner), BF16),
        compiler_params=pltpu.CompilerParams(vmem_limit_bytes=40 * 1024 * 1024),
        name="reader",
    )(tokens, out_grad, rel, w_query, w_key, w_value, w_out)


def shards(
    index_emb,
    query_emb,
    passage_owner,
    passage_row,
    token_ids,
    vocab_table,
    w_query,
    w_key,
    w_value,
    w_out,
    out_grad,
    slab_emb,
    slab_ids,
):
    nz, ny = lax.axis_size("z"), lax.axis_size("y")
    owners = nz * ny
    my_z, my_y = lax.axis_index("z"), lax.axis_index("y")
    pass_rows, width = index_emb.shape
    queries = query_emb.shape[0]
    npass = token_ids.shape[0]
    count = npass * PLEN
    vocab_rows = vocab_table.shape[0]
    slab = slab_ids.shape[0]

    vocab = lax.all_gather(vocab_table, "z", axis=0, tiled=True)
    full_grad = lax.all_gather(out_grad, "m", axis=1, tiled=True)

    flat_ids = token_ids.reshape(-1)
    slab_owner, slab_row = slab_ids // pass_rows, slab_ids % pass_rows
    earlier = (slab_owner[:, None] == slab_owner[None, :]) & (
        jnp.arange(slab)[:, None] > jnp.arange(slab)[None, :]
    )
    slot = slab_owner * CAPS + jnp.sum(earlier.astype(jnp.int32), axis=1)
    select = (jnp.arange(owners * CAPS)[:, None] == slot[None, :]).astype(BF16)
    slab_wide = jnp.concatenate(
        [slab_emb, jnp.broadcast_to((slab_row + 1).astype(BF16)[:, None], (slab, LANES))], axis=1
    )
    slab_out = dot(select, slab_wide).astype(BF16).reshape(owners, CAPS, width + LANES)
    ids_part = jnp.stack([flat_ids // LANES, flat_ids % LANES]).astype(BF16)
    common = jnp.concatenate([query_emb, ids_part], axis=1)
    message = jnp.concatenate(
        [slab_out, jnp.broadcast_to(common[None], (owners, *common.shape))], axis=2
    )
    got = lax.all_to_all(message, IDX, 0, 0, tiled=True)

    all_queries = got[:, :, width + LANES : 2 * width + LANES].reshape(-1, width)
    scores_out = dot(all_queries, index_emb, COLS).reshape(owners, queries, pass_rows)
    scores_in = lax.all_to_all(scores_out, IDX, 0, 0, tiled=True)

    got_rows = got[:, :, :width].reshape(-1, width)
    got_place = got[:, :, width].reshape(-1).astype(jnp.int32) - 1
    put = jnp.arange(pass_rows)[:, None] == got_place[None, :]
    refreshed = jnp.where(
        jnp.any(put, axis=1)[:, None], dot(put.astype(BF16), got_rows).astype(BF16), index_emb
    )

    ids_all = got[:, :, 2 * width + LANES :].astype(jnp.int32)
    ids_all = ids_all[:, 0] * LANES + ids_all[:, 1]
    ids = lax.dynamic_slice_in_dim(ids_all, my_z * ny, ny, axis=0).reshape(-1)
    id_owner = ids // vocab_rows
    local = jnp.where(id_owner % ny == my_y, (id_owner // ny) * vocab_rows + ids % vocab_rows, -1)
    one_hot = (local[:, None] == jnp.arange(nz * vocab_rows)[None, :]).astype(BF16)
    served = dot(one_hot, vocab).astype(BF16).reshape(ny, count, -1)
    token_in = lax.all_to_all(served, "y", 0, 0, tiled=True)
    token_part = jnp.sum(token_in.astype(F32), axis=0).astype(BF16)
    tokens = lax.all_gather(token_part, "m", axis=1, tiled=True)

    at = (passage_owner[:, 0][:, None, None] == jnp.arange(owners)[None, :, None]) & (
        passage_row[:, None, None] == jnp.arange(pass_rows)[None, None, :]
    )
    table = jnp.repeat(scores_in.transpose(1, 0, 2), K, axis=0)
    scores = jnp.sum(jnp.where(at, table, 0.0), axis=(1, 2)).reshape(queries, K)
    relevance = jax.nn.softmax(scores, axis=-1)
    rel = jnp.repeat(relevance.reshape(-1), PLEN)[:, None]

    terms = reader(tokens, full_grad, rel, w_query, w_key, w_value, w_out, owners)
    sums = jnp.sum(lax.all_to_all(terms, IDX, 0, 0, tiled=True).astype(F32), axis=0)
    rows = sums.shape[0] // 4
    grad_query, grad_key, grad_value = (sums[i * rows : (i + 1) * rows] for i in range(3))
    grad_out = sums[3 * rows :].T
    return (relevance, grad_query, grad_key, grad_value, grad_out, refreshed)


def solution(mesh):
    owners, columns = mesh.devices.shape
    side = 1
    while side * side < owners:
        side *= 2
    fine = Mesh(mesh.devices.reshape(owners // side, side, columns), ("z", "y", "m"))
    return jax.shard_map(
        shards,
        mesh=fine,
        in_specs=(
            P(IDX, None),
            P(IDX, None),
            P(IDX, None),
            P(IDX),
            P(IDX, None),
            P(IDX, "m"),
            P(None, "m"),
            P(None, "m"),
            P(None, "m"),
            P("m", None),
            P(IDX, "m"),
            P(IDX, None),
            P(IDX),
        ),
        out_specs=(
            P(IDX, None),
            P(IDX, "m"),
            P(IDX, "m"),
            P(IDX, "m"),
            P("m", IDX),
            P(IDX, None),
        ),
        check_vma=False,
    )
```

```python
import functools

import jax
import jax.numpy as jnp
from jax import lax
from jax.experimental import pallas as pl
from jax.experimental.pallas import tpu as pltpu
from jax.sharding import Mesh
from jax.sharding import PartitionSpec as P

HEAD_DIM = 64
K = 20
PLEN = 4
CAPS = 2
LANES = 128
IDX = ("z", "h", "p", "q")
F32 = jnp.float32
BF16 = jnp.bfloat16
ROWS = (((0,), (0,)), ((), ()))
COLS = (((1,), (1,)), ((), ()))


def dot(a, b, dims=None):
    if dims is None:
        return jnp.dot(a, b, preferred_element_type=F32)
    return lax.dot_general(a, b, dims, preferred_element_type=F32)


def reader_kernel(
    heads, half_ref, tokens_ref, grad_ref, rel_ref, wq_ref, wk_ref, wv_ref, wo_ref, out_ref
):
    blocks, count, deep = tokens_ref.shape
    rows = out_ref.shape[1] // 2
    mine = half_ref[0]
    rel = rel_ref[...]

    def projected(weight_ref):
        total = dot(tokens_ref[0], weight_ref[:deep])
        for b in range(1, blocks):
            total += dot(tokens_ref[b], weight_ref[b * deep : (b + 1) * deep])
        return total.astype(BF16)

    def own(states):
        kept = states[:, :HEAD_DIM]
        for head in range(1, heads):
            kept = jnp.where(mine == head, states[:, head * HEAD_DIM : (head + 1) * HEAD_DIM], kept)
        return kept

    q, k, v = own(projected(wq_ref)), own(projected(wk_ref)), own(projected(wv_ref))
    weighted = [(grad_ref[b].astype(F32) * rel).astype(BF16) for b in range(blocks)]
    total = dot(weighted[0], wo_ref[:, :deep], COLS)
    for b in range(1, blocks):
        total += dot(weighted[b], wo_ref[:, b * deep : (b + 1) * deep], COLS)
    c = own(total.astype(BF16))
    passage_i = lax.broadcasted_iota(jnp.int32, (count, count), 0) // PLEN
    passage_j = lax.broadcasted_iota(jnp.int32, (count, count), 1) // PLEN
    logits = jnp.where(passage_i == passage_j, dot(q, k, COLS), -jnp.inf)
    exps = jnp.exp(logits - jnp.max(logits, axis=1, keepdims=True))
    probs = exps / jnp.sum(exps, axis=1, keepdims=True)
    attn = probs.astype(BF16)
    attn_grad = dot(c, v, COLS)
    mean = jnp.sum(attn_grad * probs, axis=1, keepdims=True)
    score_grad = (probs * (attn_grad - mean)).astype(BF16)
    query_grad = dot(score_grad, k).astype(BF16)
    key_grad = dot(score_grad, q, ROWS).astype(BF16)
    value_grad = dot(attn, c, ROWS).astype(BF16)
    context = dot(attn, v).astype(BF16)
    query_key = jnp.concatenate([query_grad, key_grad], axis=1)
    each = deep // rows
    for b in range(blocks):
        first = dot(tokens_ref[b], query_key, ROWS).astype(BF16)
        second = jnp.concatenate(
            [dot(tokens_ref[b], value_grad, ROWS), dot(weighted[b], context, ROWS)], axis=1
        ).astype(BF16)
        out_ref[b * each : (b + 1) * each, :rows, :] = first.reshape(each, rows, -1)
        out_ref[b * each : (b + 1) * each, rows:, :] = second.reshape(each, rows, -1)


def reader(half, tokens, out_grad, rel, w_query, w_key, w_value, w_out, owners):
    width, inner = w_query.shape
    vmem = pl.BlockSpec(memory_space=pltpu.VMEM)
    return pl.pallas_call(
        functools.partial(reader_kernel, inner // HEAD_DIM),
        out_shape=jax.ShapeDtypeStruct((owners, 2 * width // owners, 2 * HEAD_DIM), BF16),
        in_specs=[pl.BlockSpec(memory_space=pltpu.SMEM)] + [vmem] * 7,
        out_specs=vmem,
        compiler_params=pltpu.CompilerParams(vmem_limit_bytes=40 * 1024 * 1024),
        name="reader",
    )(half, tokens, out_grad, rel, w_query, w_key, w_value, w_out)


def all_features(part):
    along_x = lax.all_gather(part, "x", axis=0)
    count = part.shape[0]
    halves = [
        lax.all_gather(along_x[:, i * count // 2 : (i + 1) * count // 2], "c", axis=1)
        for i in range(2)
    ]
    whole = jnp.concatenate(halves, axis=2)
    return whole.reshape(-1, *part.shape)


def shards(
    index_emb,
    query_emb,
    passage_owner,
    passage_row,
    token_ids,
    vocab_table,
    w_query,
    w_key,
    w_value,
    w_out,
    out_grad,
    slab_emb,
    slab_ids,
):
    nq = lax.axis_size("q")
    group = lax.axis_size("p") * nq
    outer = lax.axis_size("z") * lax.axis_size("h")
    owners = outer * group
    my_outer = lax.axis_index(("z", "h"))
    my_inner = lax.axis_index(("p", "q"))
    my_pair = lax.axis_index(("z", "h", "p"))
    my_half = lax.axis_index("q")
    pass_rows, width = index_emb.shape
    queries = query_emb.shape[0]
    npass, plen = token_ids.shape
    count = npass * plen
    vocab_rows = vocab_table.shape[0]
    slab = slab_ids.shape[0]

    vocab = lax.all_gather(vocab_table, ("z", "h"), axis=0, tiled=True)
    full_grad = all_features(lax.all_gather(out_grad, "q", axis=0, tiled=True))

    slab_owner, slab_row = slab_ids // pass_rows, slab_ids % pass_rows
    earlier = (slab_owner[:, None] == slab_owner[None, :]) & (
        jnp.arange(slab)[:, None] > jnp.arange(slab)[None, :]
    )
    slot = slab_owner * CAPS + jnp.sum(earlier.astype(jnp.int32), axis=1)
    select = (jnp.arange(owners * CAPS)[:, None] == slot[None, :]).astype(BF16)
    slab_wide = jnp.concatenate(
        [slab_emb, jnp.broadcast_to((slab_row + 1).astype(BF16)[:, None], (slab, LANES))], axis=1
    )
    slab_out = dot(select, slab_wide).astype(BF16).reshape(owners, CAPS, width + LANES)
    flat_ids = token_ids.reshape(-1)
    ids_part = jnp.stack([flat_ids // LANES, flat_ids % LANES]).astype(BF16)
    place_part = jnp.stack([passage_owner[:, 0], passage_row]).astype(BF16)
    common = jnp.concatenate([query_emb, ids_part, place_part], axis=1)
    message = jnp.concatenate(
        [slab_out, jnp.broadcast_to(common[None], (owners, *common.shape))], axis=2
    )
    got = lax.all_to_all(message, IDX, 0, 0, tiled=True)
    got_slab, got_common = got[:, :, : width + LANES], got[:, :, width + LANES :]

    scores_out = dot(got_common[:, :, :width].reshape(-1, width), index_emb, COLS)
    scores_out = jnp.repeat(
        scores_out.reshape(owners // nq, nq * queries, pass_rows), nq, axis=0
    )
    scores_in = lax.all_to_all(scores_out, IDX, 0, 0, tiled=True)

    got_rows = got_slab[:, :, :width].reshape(-1, width)
    got_place = got_slab[:, :, width].reshape(-1).astype(jnp.int32) - 1
    put = jnp.arange(pass_rows)[:, None] == got_place[None, :]
    refreshed = jnp.where(
        jnp.any(put, axis=1)[:, None], dot(put.astype(BF16), got_rows).astype(BF16), index_emb
    )

    ids = lax.dynamic_slice_in_dim(
        got_common[:, :, width : width + count], my_outer * group, group, axis=0
    ).astype(jnp.int32)
    ids = (ids[:, 0] * LANES + ids[:, 1]).reshape(-1)
    id_owner = ids // vocab_rows
    local = jnp.where(
        id_owner % group == my_inner, (id_owner // group) * vocab_rows + ids % vocab_rows, -1
    )
    one_hot = (local[:, None] == jnp.arange(outer * vocab_rows)[None, :]).astype(BF16)
    served = dot(one_hot, vocab).astype(BF16).reshape(group // nq, nq * count, -1)
    token_in = lax.all_to_all(jnp.repeat(served, nq, axis=0), ("p", "q"), 0, 0, tiled=True)
    token_part = jnp.sum(token_in.astype(F32), axis=0).astype(BF16)
    tokens = all_features(token_part)

    places = lax.dynamic_slice_in_dim(
        got_common[:, :, width + count :], my_pair * nq, nq, axis=0
    ).astype(jnp.int32)
    pair_owner, pair_row = places[:, 0].reshape(-1), places[:, 1].reshape(-1)
    at = (pair_owner[:, None, None] == jnp.arange(owners)[None, :, None]) & (
        pair_row[:, None, None] == jnp.arange(pass_rows)[None, None, :]
    )
    table = jnp.repeat(scores_in.transpose(1, 0, 2), K, axis=0)
    scores = jnp.sum(jnp.where(at, table, 0.0), axis=(1, 2)).reshape(nq * queries, K)
    pair_relevance = jax.nn.softmax(scores, axis=-1)
    relevance = lax.dynamic_slice_in_dim(pair_relevance, my_half * queries, queries, axis=0)
    rel = jnp.repeat(pair_relevance.reshape(-1), plen)[:, None]

    terms = reader(
        my_half.reshape(1), tokens, full_grad, rel, w_query, w_key, w_value, w_out, owners
    )
    terms = lax.all_to_all(terms, IDX, 0, 0, tiled=True)
    rows = terms.shape[1] // 2
    sums = jnp.sum(terms.astype(F32).reshape(owners // nq, nq, 2, rows, 2, HEAD_DIM), axis=0)
    parts = sums.transpose(1, 3, 2, 0, 4).reshape(2, 2, rows, nq * HEAD_DIM)
    return (relevance, parts[0, 0], parts[0, 1], parts[1, 0], parts[1, 1].T, refreshed)


def solution(mesh):
    devices = mesh.devices
    owners, columns = devices.shape
    fine = Mesh(
        devices.reshape(owners // 8, 2, 2, 2, columns // 2, 2), ("z", "h", "p", "q", "x", "c")
    )
    m = ("x", "c")
    return jax.shard_map(
        shards,
        mesh=fine,
        in_specs=(
            P(IDX, None),
            P(IDX, None),
            P(IDX, None),
            P(IDX),
            P(IDX, None),
            P(IDX, m),
            P(None, m),
            P(None, m),
            P(None, m),
            P(m, None),
            P(IDX, m),
            P(IDX, None),
            P(IDX),
        ),
        out_specs=(
            P(IDX, None),
            P(IDX, m),
            P(IDX, m),
            P(IDX, m),
            P(m, IDX),
            P(IDX, None),
        ),
        check_vma=False,
    )
```

```python
import functools

import jax
import jax.numpy as jnp
from jax import lax
from jax.experimental import pallas as pl
from jax.experimental.pallas import tpu as pltpu
from jax.sharding import Mesh
from jax.sharding import PartitionSpec as P

HEAD_DIM = 64
K = 20
PLEN = 4
CAPS = 2
LANES = 128
IDX = ("z", "p", "q")
M = ("x", "c")
F32 = jnp.float32
BF16 = jnp.bfloat16
ROWS = (((0,), (0,)), ((), ()))
COLS = (((1,), (1,)), ((), ()))


def dot(a, b, dims=None):
    if dims is None:
        return jnp.dot(a, b, preferred_element_type=F32)
    return lax.dot_general(a, b, dims, preferred_element_type=F32)


def reader_kernel(
    heads, half_ref, tokens_ref, grad_ref, rel_ref, wq_ref, wk_ref, wv_ref, wo_ref, out_ref
):
    blocks, count, deep = tokens_ref.shape
    rows = out_ref.shape[1] // 2
    mine = half_ref[0]
    rel = rel_ref[...]

    def projected(weight_ref):
        total = dot(tokens_ref[0], weight_ref[:deep])
        for b in range(1, blocks):
            total += dot(tokens_ref[b], weight_ref[b * deep : (b + 1) * deep])
        return total.astype(BF16)

    def own(states):
        kept = states[:, :HEAD_DIM]
        for head in range(1, heads):
            kept = jnp.where(mine == head, states[:, head * HEAD_DIM : (head + 1) * HEAD_DIM], kept)
        return kept

    q, k, v = own(projected(wq_ref)), own(projected(wk_ref)), own(projected(wv_ref))
    weighted = [(grad_ref[b].astype(F32) * rel).astype(BF16) for b in range(blocks)]
    total = dot(weighted[0], wo_ref[:, :deep], COLS)
    for b in range(1, blocks):
        total += dot(weighted[b], wo_ref[:, b * deep : (b + 1) * deep], COLS)
    c = own(total.astype(BF16))
    passage_i = lax.broadcasted_iota(jnp.int32, (count, count), 0) // PLEN
    passage_j = lax.broadcasted_iota(jnp.int32, (count, count), 1) // PLEN
    logits = jnp.where(passage_i == passage_j, dot(q, k, COLS), -jnp.inf)
    exps = jnp.exp(logits - jnp.max(logits, axis=1, keepdims=True))
    probs = exps / jnp.sum(exps, axis=1, keepdims=True)
    attn = probs.astype(BF16)
    attn_grad = dot(c, v, COLS)
    mean = jnp.sum(attn_grad * probs, axis=1, keepdims=True)
    score_grad = (probs * (attn_grad - mean)).astype(BF16)
    query_grad = dot(score_grad, k).astype(BF16)
    key_grad = dot(score_grad, q, ROWS).astype(BF16)
    value_grad = dot(attn, c, ROWS).astype(BF16)
    context = dot(attn, v).astype(BF16)
    query_key = jnp.concatenate([query_grad, key_grad], axis=1)
    each = deep // rows
    for b in range(blocks):
        first = dot(tokens_ref[b], query_key, ROWS).astype(BF16)
        second = jnp.concatenate(
            [dot(tokens_ref[b], value_grad, ROWS), dot(weighted[b], context, ROWS)], axis=1
        ).astype(BF16)
        out_ref[b * each : (b + 1) * each, :rows, :] = first.reshape(each, rows, -1)
        out_ref[b * each : (b + 1) * each, rows:, :] = second.reshape(each, rows, -1)


def reader(half, tokens, out_grad, rel, w_query, w_key, w_value, w_out, owners):
    width, inner = w_query.shape
    vmem = pl.BlockSpec(memory_space=pltpu.VMEM)
    return pl.pallas_call(
        functools.partial(reader_kernel, inner // HEAD_DIM),
        out_shape=jax.ShapeDtypeStruct((owners, 2 * width // owners, 2 * HEAD_DIM), BF16),
        in_specs=[pl.BlockSpec(memory_space=pltpu.SMEM)] + [vmem] * 7,
        out_specs=vmem,
        compiler_params=pltpu.CompilerParams(vmem_limit_bytes=40 * 1024 * 1024),
        name="reader",
    )(half, tokens, out_grad, rel, w_query, w_key, w_value, w_out)


def all_features(part):
    along_x = lax.all_gather(part, "x", axis=0)
    count = part.shape[0]
    halves = [
        lax.all_gather(along_x[:, i * count // 2 : (i + 1) * count // 2], "c", axis=1)
        for i in range(2)
    ]
    whole = jnp.concatenate(halves, axis=2)
    return whole.reshape(-1, *part.shape)


def shards(
    index_emb,
    query_emb,
    passage_owner,
    passage_row,
    token_ids,
    vocab_table,
    w_query,
    w_key,
    w_value,
    w_out,
    out_grad,
    slab_emb,
    slab_ids,
):
    nz, nq = lax.axis_size("z"), lax.axis_size("q")
    ny = lax.axis_size("p") * nq
    owners = nz * ny
    swap = [(0, 1), (1, 0)]
    my_z = lax.axis_index("z")
    my_y = lax.axis_index(("p", "q"))
    my_idx = lax.axis_index(IDX)
    my_half = lax.axis_index("q")
    pass_rows, width = index_emb.shape
    queries = query_emb.shape[0]
    npass, plen = token_ids.shape
    count = npass * plen
    vocab_rows = vocab_table.shape[0]
    slab = slab_ids.shape[0]
    strips = width // LANES
    strip = lax.rem(lax.axis_index(M), strips)

    def my_strip(array):
        return lax.dynamic_slice_in_dim(array, strip * LANES, LANES, axis=1)

    vocab = lax.all_gather(vocab_table, "z", axis=0, tiled=True)
    pair_grad = jnp.concatenate([out_grad, lax.ppermute(out_grad, "q", swap)], axis=0)
    full_grad = lax.all_gather(pair_grad, M, axis=0)

    slab_owner, slab_row = slab_ids // pass_rows, slab_ids % pass_rows
    earlier = (slab_owner[:, None] == slab_owner[None, :]) & (
        jnp.arange(slab)[:, None] > jnp.arange(slab)[None, :]
    )
    slot = slab_owner * CAPS + jnp.sum(earlier.astype(jnp.int32), axis=1)
    select = (jnp.arange(owners * CAPS)[:, None] == slot[None, :]).astype(BF16)
    slab_wide = jnp.concatenate(
        [
            my_strip(slab_emb),
            jnp.broadcast_to((slab_row + 1).astype(BF16)[:, None], (slab, LANES)),
        ],
        axis=1,
    )
    slab_out = dot(select, slab_wide).astype(BF16).reshape(owners, CAPS, 2 * LANES)
    flat_ids = token_ids.reshape(-1)
    ids_part = jnp.stack([flat_ids // LANES, flat_ids % LANES]).astype(BF16)
    place_part = jnp.stack([passage_owner[:, 0], passage_row]).astype(BF16)
    common = jnp.concatenate([query_emb, ids_part, place_part], axis=1)
    message = jnp.concatenate(
        [slab_out, jnp.broadcast_to(common[None], (owners, *common.shape))], axis=2
    )
    got = lax.all_to_all(message, IDX, 0, 0, tiled=True)
    got_slab, got_common = got[:, :, : 2 * LANES], got[:, :, 2 * LANES :]

    scores_out = dot(got_common[:, :, :width].reshape(-1, width), index_emb, COLS)
    scores_out = scores_out.reshape(owners // nq, nq, queries, pass_rows)
    scores_out = jnp.concatenate([scores_out, scores_out[:, ::-1]], axis=2)
    scores_in = lax.all_to_all(
        scores_out.reshape(owners, nq * queries, pass_rows), IDX, 0, 0, tiled=True
    )

    got_place = got_slab[:, :, LANES].reshape(-1).astype(jnp.int32) - 1
    put = jnp.arange(pass_rows)[:, None] == got_place[None, :]
    placed = dot(put.astype(BF16), got_slab[:, :, :LANES].reshape(-1, LANES)).astype(BF16)
    refreshed = jnp.where(jnp.any(put, axis=1)[:, None], placed, my_strip(index_emb))
    refreshed = lax.all_gather(refreshed, M, axis=0)
    refreshed = jnp.concatenate([refreshed[i] for i in range(strips)], axis=1)

    ids = lax.dynamic_slice_in_dim(
        got_common[:, :, width : width + count], my_z * ny, ny, axis=0
    ).astype(jnp.int32)
    ids = (ids[:, 0] * LANES + ids[:, 1]).reshape(-1)
    id_owner = ids // vocab_rows
    local = jnp.where(id_owner % ny == my_y, (id_owner // ny) * vocab_rows + ids % vocab_rows, -1)
    one_hot = (local[:, None] == jnp.arange(nz * vocab_rows)[None, :]).astype(BF16)
    served = dot(one_hot, vocab).astype(BF16).reshape(ny, count, -1)
    token_in = lax.all_to_all(served, ("p", "q"), 0, 0, tiled=True)
    token_part = jnp.sum(token_in.astype(F32), axis=0).astype(BF16)
    tokens = all_features(
        jnp.concatenate([token_part, lax.ppermute(token_part, "q", swap)], axis=0)
    )

    other = my_idx + 1 - 2 * my_half
    other_place = lax.dynamic_index_in_dim(
        got_common[:, :, width + count :], other, axis=0, keepdims=False
    ).astype(jnp.int32)
    pair_owner = jnp.concatenate([passage_owner[:, 0], other_place[0]])
    pair_row = jnp.concatenate([passage_row, other_place[1]])
    at = (pair_owner[:, None, None] == jnp.arange(owners)[None, :, None]) & (
        pair_row[:, None, None] == jnp.arange(pass_rows)[None, None, :]
    )
    table = jnp.repeat(scores_in.transpose(1, 0, 2), K, axis=0)
    scores = jnp.sum(jnp.where(at, table, 0.0), axis=(1, 2)).reshape(nq * queries, K)
    pair_relevance = jax.nn.softmax(scores, axis=-1)
    rel = jnp.repeat(pair_relevance.reshape(-1), plen)[:, None]

    terms = reader(
        my_half.reshape(1), tokens, full_grad, rel, w_query, w_key, w_value, w_out, owners
    )
    terms = lax.all_to_all(terms, IDX, 0, 0, tiled=True)
    rows = terms.shape[1] // 2
    sums = jnp.sum(terms.reshape(owners // nq, nq, *terms.shape[1:]).astype(F32), axis=0)

    def whole(top, left):
        return jnp.concatenate(
            [
                sums[h, top * rows : (top + 1) * rows, left * HEAD_DIM : (left + 1) * HEAD_DIM]
                for h in range(nq)
            ],
            axis=1,
        )

    return (
        pair_relevance[:queries],
        whole(0, 0),
        whole(0, 1),
        whole(1, 0),
        whole(1, 1).T,
        refreshed,
    )


def solution(mesh):
    devices = mesh.devices
    owners, columns = devices.shape
    fine = Mesh(devices.reshape(owners // 8, 4, 2, columns // 2, 2), (*IDX, *M))
    return jax.shard_map(
        shards,
        mesh=fine,
        in_specs=(
            P(IDX, None),
            P(IDX, None),
            P(IDX, None),
            P(IDX),
            P(IDX, None),
            P(IDX, M),
            P(None, M),
            P(None, M),
            P(None, M),
            P(M, None),
            P(IDX, M),
            P(IDX, None),
            P(IDX),
        ),
        out_specs=(
            P(IDX, None),
            P(IDX, M),
            P(IDX, M),
            P(IDX, M),
            P(M, IDX),
            P(IDX, None),
        ),
        check_vma=False,
    )
```

```python
import functools

import jax
import jax.numpy as jnp
from jax import lax
from jax.experimental import pallas as pl
from jax.experimental.pallas import tpu as pltpu
from jax.sharding import Mesh
from jax.sharding import PartitionSpec as P

HEAD_DIM = 64
K = 20
PLEN = 4
CAPS = 2
LANES = 128
IDX = ("z", "p", "q")
M = ("x", "c")
F32 = jnp.float32
BF16 = jnp.bfloat16
ROWS = (((0,), (0,)), ((), ()))
COLS = (((1,), (1,)), ((), ()))


def dot(a, b, dims=None):
    if dims is None:
        return jnp.dot(a, b, preferred_element_type=F32)
    return lax.dot_general(a, b, dims, preferred_element_type=F32)


def reader_kernel(heads, half_ref, tokens_ref, grad_ref, rel_ref, *refs):
    hbm, out_ref, vmem, sems = refs[:4], refs[4], refs[5:9], refs[9]
    copies = [pltpu.make_async_copy(hbm[i], vmem[i], sems.at[i]) for i in range(4)]
    for copy in copies:
        copy.start()
    wq_ref, wk_ref, wv_ref, wo_ref = vmem
    blocks, count, deep = tokens_ref.shape
    rows = out_ref.shape[1] // 2
    mine = half_ref[0]
    rel = rel_ref[...]

    def projected(weight_ref):
        total = dot(tokens_ref[0], weight_ref[:deep])
        for b in range(1, blocks):
            total += dot(tokens_ref[b], weight_ref[b * deep : (b + 1) * deep])
        return total.astype(BF16)

    def own(states):
        kept = states[:, :HEAD_DIM]
        for head in range(1, heads):
            kept = jnp.where(mine == head, states[:, head * HEAD_DIM : (head + 1) * HEAD_DIM], kept)
        return kept

    weighted = [(grad_ref[b].astype(F32) * rel).astype(BF16) for b in range(blocks)]
    for copy in copies:
        copy.wait()
    q, k, v = own(projected(wq_ref)), own(projected(wk_ref)), own(projected(wv_ref))
    total = dot(weighted[0], wo_ref[:, :deep], COLS)
    for b in range(1, blocks):
        total += dot(weighted[b], wo_ref[:, b * deep : (b + 1) * deep], COLS)
    c = own(total.astype(BF16))
    passage_i = lax.broadcasted_iota(jnp.int32, (count, count), 0) // PLEN
    passage_j = lax.broadcasted_iota(jnp.int32, (count, count), 1) // PLEN
    logits = jnp.where(passage_i == passage_j, dot(q, k, COLS), -jnp.inf)
    exps = jnp.exp(logits - jnp.max(logits, axis=1, keepdims=True))
    probs = exps / jnp.sum(exps, axis=1, keepdims=True)
    attn = probs.astype(BF16)
    attn_grad = dot(c, v, COLS)
    mean = jnp.sum(attn_grad * probs, axis=1, keepdims=True)
    score_grad = (probs * (attn_grad - mean)).astype(BF16)
    query_grad = dot(score_grad, k).astype(BF16)
    key_grad = dot(score_grad, q, ROWS).astype(BF16)
    value_grad = dot(attn, c, ROWS).astype(BF16)
    context = dot(attn, v).astype(BF16)
    query_key = jnp.concatenate([query_grad, key_grad], axis=1)
    each = deep // rows
    for b in range(blocks):
        first = dot(tokens_ref[b], query_key, ROWS).astype(BF16)
        second = jnp.concatenate(
            [dot(tokens_ref[b], value_grad, ROWS), dot(weighted[b], context, ROWS)], axis=1
        ).astype(BF16)
        out_ref[b * each : (b + 1) * each, :rows, :] = first.reshape(each, rows, -1)
        out_ref[b * each : (b + 1) * each, rows:, :] = second.reshape(each, rows, -1)


def reader(half, tokens, out_grad, rel, w_query, w_key, w_value, w_out, owners):
    width, inner = w_query.shape
    vmem = pl.BlockSpec(memory_space=pltpu.VMEM)
    return pl.pallas_call(
        functools.partial(reader_kernel, inner // HEAD_DIM),
        out_shape=jax.ShapeDtypeStruct((owners, 2 * width // owners, 2 * HEAD_DIM), BF16),
        in_specs=[pl.BlockSpec(memory_space=pltpu.SMEM)]
        + [vmem] * 3
        + [pl.BlockSpec(memory_space=pl.ANY)] * 4,
        out_specs=vmem,
        scratch_shapes=[pltpu.VMEM((width, inner), BF16)] * 3
        + [pltpu.VMEM((inner, width), BF16), pltpu.SemaphoreType.DMA((4,))],
        compiler_params=pltpu.CompilerParams(vmem_limit_bytes=40 * 1024 * 1024),
        name="reader",
    )(half, tokens, out_grad, rel, w_query, w_key, w_value, w_out)


def all_features(part):
    along_x = lax.all_gather(part, "x", axis=0)
    count = part.shape[0]
    halves = [
        lax.all_gather(along_x[:, i * count // 2 : (i + 1) * count // 2], "c", axis=1)
        for i in range(2)
    ]
    whole = jnp.concatenate(halves, axis=2)
    return whole.reshape(-1, *part.shape)


def shards(
    index_emb,
    query_emb,
    passage_owner,
    passage_row,
    token_ids,
    vocab_table,
    w_query,
    w_key,
    w_value,
    w_out,
    out_grad,
    slab_emb,
    slab_ids,
):
    nz, nq = lax.axis_size("z"), lax.axis_size("q")
    ny = lax.axis_size("p") * nq
    owners = nz * ny
    swap = [(0, 1), (1, 0)]
    my_y = lax.axis_index(("p", "q"))
    my_half = lax.axis_index("q")
    pass_rows, width = index_emb.shape
    queries = query_emb.shape[0]
    npass, plen = token_ids.shape
    count = npass * plen
    vocab_rows = vocab_table.shape[0]
    slab = slab_ids.shape[0]
    strips = width // LANES
    strip = lax.rem(lax.axis_index(M), strips)

    def my_strip(array):
        return lax.dynamic_slice_in_dim(array, strip * LANES, LANES, axis=1)

    deep = vocab_table.shape[1]
    query_rows = queries * width // deep
    pad = jnp.zeros((-query_rows % 8, deep), BF16)
    message = jnp.concatenate([vocab_table, query_emb.reshape(query_rows, deep), pad], axis=0)
    stride = message.shape[0]
    got_z = lax.all_to_all(
        jnp.broadcast_to(message[None], (nz, *message.shape)), "z", 0, 0, tiled=True
    )
    ids = jnp.pad(token_ids.reshape(1, -1), ((0, 0), (0, -count % LANES)))
    ids = lax.all_gather(ids, ("p", "q"), axis=0, tiled=True)[:, :count].reshape(-1)

    places = jnp.concatenate([passage_owner[:, 0], passage_row]).astype(BF16)
    places = jnp.pad(places[None], ((0, 15), (0, deep - 2 * npass)))
    other = lax.ppermute(jnp.concatenate([out_grad, places], axis=0), "q", swap)
    full_grad = lax.all_gather(jnp.concatenate([out_grad, other[:count]], axis=0), M, axis=0)
    other_place = other[count, : 2 * npass].astype(jnp.int32)
    pair_owner = jnp.concatenate([passage_owner[:, 0], other_place[:npass]])
    pair_row = jnp.concatenate([passage_row, other_place[npass:]])

    id_owner = ids // vocab_rows
    local = jnp.where(id_owner % ny == my_y, (id_owner // ny) * stride + ids % vocab_rows, -1)
    one_hot = (local[:, None] == jnp.arange(nz * stride)[None, :]).astype(BF16)
    served = dot(one_hot, got_z.reshape(nz * stride, deep)).astype(BF16).reshape(ny, count, deep)
    z_queries = got_z[:, vocab_rows : vocab_rows + query_rows].reshape(1, nz * query_rows, deep)
    got_y = lax.all_to_all(
        jnp.concatenate(
            [served, jnp.broadcast_to(z_queries, (ny, nz * query_rows, deep))], axis=1
        ),
        ("p", "q"),
        0,
        0,
        tiled=True,
    )
    token_part = jnp.sum(got_y[:, :count].astype(F32), axis=0).astype(BF16)
    tokens = all_features(
        jnp.concatenate([token_part, lax.ppermute(token_part, "q", swap)], axis=0)
    )

    slab_owner, slab_row = slab_ids // pass_rows, slab_ids % pass_rows
    earlier = (slab_owner[:, None] == slab_owner[None, :]) & (
        jnp.arange(slab)[:, None] > jnp.arange(slab)[None, :]
    )
    slot = slab_owner * CAPS + jnp.sum(earlier.astype(jnp.int32), axis=1)
    select = (jnp.arange(owners * CAPS)[:, None] == slot[None, :]).astype(BF16)
    slab_out = dot(select, my_strip(slab_emb)).reshape(owners, CAPS, LANES)
    place_out = jnp.sum(jnp.where(select > 0, (slab_row + 1)[None, :], 0), axis=1)
    place_out = jnp.broadcast_to(
        place_out.astype(F32).reshape(owners, CAPS, 1), (owners, CAPS, LANES)
    )

    all_queries = got_y[:, count:].reshape(ny, nz, queries, width).transpose(1, 0, 2, 3)
    scores_out = dot(all_queries.reshape(-1, width), index_emb, COLS)
    scores_out = scores_out.reshape(owners // nq, nq, queries, pass_rows)
    scores_out = jnp.concatenate([scores_out, scores_out[:, ::-1]], axis=2)
    back = jnp.concatenate(
        [scores_out.reshape(owners, nq * queries, pass_rows), slab_out, place_out], axis=1
    )
    got = lax.all_to_all(back, IDX, 0, 0, tiled=True)
    scores_in = got[:, : nq * queries]
    got_slab = got[:, nq * queries : nq * queries + CAPS].reshape(-1, LANES).astype(BF16)
    got_place = got[:, nq * queries + CAPS :, 0].reshape(-1).astype(jnp.int32) - 1

    put = jnp.arange(pass_rows)[:, None] == got_place[None, :]
    placed = dot(put.astype(BF16), got_slab).astype(BF16)
    refreshed = jnp.where(jnp.any(put, axis=1)[:, None], placed, my_strip(index_emb))
    refreshed = lax.all_gather(refreshed, M, axis=0)
    refreshed = jnp.concatenate([refreshed[i] for i in range(strips)], axis=1)

    at = (pair_owner[:, None, None] == jnp.arange(owners)[None, :, None]) & (
        pair_row[:, None, None] == jnp.arange(pass_rows)[None, None, :]
    )
    table = jnp.repeat(scores_in.transpose(1, 0, 2), K, axis=0)
    scores = jnp.sum(jnp.where(at, table, 0.0), axis=(1, 2)).reshape(nq * queries, K)
    pair_relevance = jax.nn.softmax(scores, axis=-1)
    rel = jnp.repeat(pair_relevance.reshape(-1), plen)[:, None]

    terms = reader(
        my_half.reshape(1), tokens, full_grad, rel, w_query, w_key, w_value, w_out, owners
    )
    terms = lax.all_to_all(terms, IDX, 0, 0, tiled=True)
    rows = terms.shape[1] // 2
    sums = jnp.sum(terms.reshape(owners // nq, nq, *terms.shape[1:]).astype(F32), axis=0)

    def whole(top, left):
        return jnp.concatenate(
            [
                sums[h, top * rows : (top + 1) * rows, left * HEAD_DIM : (left + 1) * HEAD_DIM]
                for h in range(nq)
            ],
            axis=1,
        )

    return (
        pair_relevance[:queries],
        whole(0, 0),
        whole(0, 1),
        whole(1, 0),
        whole(1, 1).T,
        refreshed,
    )


def solution(mesh):
    devices = mesh.devices
    owners, columns = devices.shape
    fine = Mesh(devices.reshape(owners // 8, 4, 2, columns // 2, 2), (*IDX, *M))
    return jax.shard_map(
        shards,
        mesh=fine,
        in_specs=(
            P(IDX, None),
            P(IDX, None),
            P(IDX, None),
            P(IDX),
            P(IDX, None),
            P(IDX, M),
            P(None, M),
            P(None, M),
            P(None, M),
            P(M, None),
            P(IDX, M),
            P(IDX, None),
            P(IDX),
        ),
        out_specs=(
            P(IDX, None),
            P(IDX, M),
            P(IDX, M),
            P(IDX, M),
            P(M, IDX),
            P(IDX, None),
        ),
        check_vma=False,
    )
```

```python
import functools

import jax
import jax.numpy as jnp
from jax import lax
from jax.experimental import pallas as pl
from jax.experimental.pallas import tpu as pltpu
from jax.sharding import Mesh
from jax.sharding import PartitionSpec as P

HEAD_DIM = 64
K = 20
PLEN = 4
LANES = 128
IDX = ("z", "p", "q")
M = ("x", "c")
F32 = jnp.float32
BF16 = jnp.bfloat16
ROWS = (((0,), (0,)), ((), ()))
COLS = (((1,), (1,)), ((), ()))


def dot(a, b, dims=None):
    if dims is None:
        return jnp.dot(a, b, preferred_element_type=F32)
    return lax.dot_general(a, b, dims, preferred_element_type=F32)


def reader_kernel(heads, half_ref, high_ref, query_ref, *refs):
    token_refs, grad_refs, hbm = refs[:2], refs[2:4], refs[4:8]
    out_ref, rel_ref, vmem, sems = refs[8], refs[9], refs[10:14], refs[14]
    copies = [pltpu.make_async_copy(hbm[i], vmem[i], sems.at[i]) for i in range(4)]
    for copy in copies:
        copy.start()
    wq_ref, wk_ref, wv_ref, wo_ref = vmem
    nc, nx, count, deep = grad_refs[0].shape
    blocks = 2 * nx * nc
    strips, passages = query_ref.shape[:2]
    rows = out_ref.shape[1] // 2
    mine = half_ref[0]

    def block(pair, b, low, high):
        x, c = divmod(b, nc)
        return pair[x // nx][c, x % nx, low:high, :]

    acc = jnp.zeros((passages, deep), F32)
    for s in range(strips):
        fetched = block(token_refs, s, count, count + passages)
        acc += fetched.astype(F32) * query_ref[s].astype(F32)
    low = jnp.sum(acc[:, :LANES], axis=1, keepdims=True)
    high = jnp.sum(acc[:, LANES:], axis=1, keepdims=True)
    scores = jnp.where(high_ref[...] > 0, high, low)
    queries = passages // K
    p = lax.broadcasted_iota(jnp.int32, (passages, queries), 0)
    first = lax.broadcasted_iota(jnp.int32, (passages, queries), 1) * K
    group = (p >= first) & (p < first + K)
    top = jnp.max(jnp.where(group, scores, -jnp.inf), axis=0, keepdims=True)
    exps = jnp.where(group, jnp.exp(scores - top), 0.0)
    rel_column = jnp.sum(exps / jnp.sum(exps, axis=0, keepdims=True), axis=1, keepdims=True)
    same = lax.broadcasted_iota(jnp.int32, (passages, passages), 0) == lax.broadcasted_iota(
        jnp.int32, (passages, passages), 1
    )
    rel_row = jnp.sum(jnp.where(same, rel_column, 0.0), axis=0, keepdims=True)
    rel_ref[...] = rel_row
    token = lax.broadcasted_iota(jnp.int32, (count, passages), 0)
    begin = lax.broadcasted_iota(jnp.int32, (count, passages), 1) * PLEN
    of_token = (token >= begin) & (token < begin + PLEN)
    rel = jnp.sum(jnp.where(of_token, rel_row, 0.0), axis=1, keepdims=True)

    tokens = [block(token_refs, b, 0, count) for b in range(blocks)]
    weighted = [
        (block(grad_refs, b, 0, count).astype(F32) * rel).astype(BF16) for b in range(blocks)
    ]
    for copy in copies:
        copy.wait()

    def projected(weight_ref):
        total = dot(tokens[0], weight_ref[:deep])
        for b in range(1, blocks):
            total += dot(tokens[b], weight_ref[b * deep : (b + 1) * deep])
        return total.astype(BF16)

    def own(states):
        kept = states[:, :HEAD_DIM]
        for head in range(1, heads):
            kept = jnp.where(mine == head, states[:, head * HEAD_DIM : (head + 1) * HEAD_DIM], kept)
        return kept

    q, k, v = own(projected(wq_ref)), own(projected(wk_ref)), own(projected(wv_ref))
    total = dot(weighted[0], wo_ref[:, :deep], COLS)
    for b in range(1, blocks):
        total += dot(weighted[b], wo_ref[:, b * deep : (b + 1) * deep], COLS)
    c = own(total.astype(BF16))
    passage_i = lax.broadcasted_iota(jnp.int32, (count, count), 0) // PLEN
    passage_j = lax.broadcasted_iota(jnp.int32, (count, count), 1) // PLEN
    logits = jnp.where(passage_i == passage_j, dot(q, k, COLS), -jnp.inf)
    exps = jnp.exp(logits - jnp.max(logits, axis=1, keepdims=True))
    probs = exps / jnp.sum(exps, axis=1, keepdims=True)
    attn = probs.astype(BF16)
    attn_grad = dot(c, v, COLS)
    mean = jnp.sum(attn_grad * probs, axis=1, keepdims=True)
    score_grad = (probs * (attn_grad - mean)).astype(BF16)
    query_grad = dot(score_grad, k).astype(BF16)
    key_grad = dot(score_grad, q, ROWS).astype(BF16)
    value_grad = dot(attn, c, ROWS).astype(BF16)
    context = dot(attn, v).astype(BF16)
    query_key = jnp.concatenate([query_grad, key_grad], axis=1)
    each = deep // rows
    for b in range(blocks):
        upper = dot(tokens[b], query_key, ROWS).astype(BF16)
        lower = jnp.concatenate(
            [dot(tokens[b], value_grad, ROWS), dot(weighted[b], context, ROWS)], axis=1
        ).astype(BF16)
        out_ref[b * each : (b + 1) * each, :rows, :] = upper.reshape(each, rows, -1)
        out_ref[b * each : (b + 1) * each, rows:, :] = lower.reshape(each, rows, -1)


def reader(half, high, query, tokens, out_grad, weights, owners):
    width, inner = weights[0].shape
    passages = query.shape[1]
    vmem = pl.BlockSpec(memory_space=pltpu.VMEM)
    return pl.pallas_call(
        functools.partial(reader_kernel, inner // HEAD_DIM),
        out_shape=(
            jax.ShapeDtypeStruct((owners, 2 * width // owners, 2 * HEAD_DIM), BF16),
            jax.ShapeDtypeStruct((1, passages), F32),
        ),
        in_specs=[pl.BlockSpec(memory_space=pltpu.SMEM)]
        + [vmem] * 6
        + [pl.BlockSpec(memory_space=pl.ANY)] * 4,
        out_specs=(vmem, vmem),
        scratch_shapes=[pltpu.VMEM((width, inner), BF16)] * 3
        + [pltpu.VMEM((inner, width), BF16), pltpu.SemaphoreType.DMA((4,))],
        compiler_params=pltpu.CompilerParams(vmem_limit_bytes=40 * 1024 * 1024),
        name="reader",
    )(half, high, query, *tokens, *out_grad, *weights)


def all_features(part):
    along_x = lax.all_gather(part, "x", axis=0)
    half = along_x.shape[0] // 2
    return [lax.all_gather(along_x[i * half : (i + 1) * half], "c", axis=0) for i in range(2)]


def shards(
    index_emb,
    query_emb,
    passage_owner,
    passage_row,
    token_ids,
    vocab_table,
    w_query,
    w_key,
    w_value,
    w_out,
    out_grad,
    slab_emb,
    slab_ids,
):
    nz, nq = lax.axis_size("z"), lax.axis_size("q")
    ny = lax.axis_size("p") * nq
    owners = nz * ny
    swap = [(0, 1), (1, 0)]
    my_y = lax.axis_index(("p", "q"))
    my_idx = lax.axis_index(IDX)
    my_half = lax.axis_index("q")
    pass_rows, width = index_emb.shape
    queries = query_emb.shape[0]
    npass, plen = token_ids.shape
    count = npass * plen
    vocab_rows = vocab_table.shape[0]
    slab = slab_ids.shape[0]
    strips = width // LANES
    strip = lax.rem(lax.axis_index(M), strips)

    def my_strip(array):
        return lax.dynamic_slice_in_dim(array, strip * LANES, LANES, axis=1)

    deep = vocab_table.shape[1]
    index_strip = my_strip(index_emb)
    folded = pass_rows // 2
    message = jnp.concatenate(
        [vocab_table, jnp.concatenate([index_strip[:folded], index_strip[folded:]], axis=1)], axis=0
    )
    stride = message.shape[0]
    got_z = lax.all_to_all(
        jnp.broadcast_to(message[None], (nz, *message.shape)), "z", 0, 0, tiled=True
    )
    wanted = jnp.concatenate([token_ids.reshape(-1), passage_owner[:, 0], passage_row])
    wanted = jnp.pad(wanted[None], ((0, 0), (0, -wanted.shape[0] % LANES)))
    wanted = lax.all_gather(wanted, ("p", "q"), axis=0, tiled=True)

    query_strips = query_emb.reshape(queries, strips, LANES).transpose(1, 0, 2)
    extra = jnp.concatenate(
        [
            query_strips.reshape(strips, queries * LANES),
            jnp.pad(passage_row.astype(BF16)[None], ((0, 0), (0, deep - npass))),
        ],
        axis=0,
    )
    extra = jnp.pad(extra, ((0, -extra.shape[0] % 16), (0, 0)))
    other = lax.ppermute(jnp.concatenate([out_grad, extra], axis=0), "q", swap)
    grads = all_features(jnp.concatenate([out_grad, other[:count]], axis=0))
    other_strips = other[count : count + strips].reshape(strips, queries, LANES)
    pair_query = jnp.concatenate([query_strips, other_strips], axis=1)
    pair_query = jnp.repeat(jnp.concatenate([pair_query, pair_query], axis=2), K, axis=1)
    other_row = other[count + strips, :npass].astype(jnp.int32)
    high = (jnp.concatenate([passage_row, other_row])[:, None] >= folded).astype(jnp.int32)

    ids, place_owner, place_row = (
        wanted[:, :count],
        wanted[:, count : count + npass],
        wanted[:, count + npass : count + 2 * npass],
    )
    id_owner = ids // vocab_rows
    token_at = jnp.where(id_owner % ny == my_y, id_owner // ny * stride + ids % vocab_rows, -1)
    place_at = jnp.where(
        place_owner % ny == my_y,
        place_owner // ny * stride + vocab_rows + place_row % folded,
        -1,
    )
    at = jnp.concatenate([token_at, place_at], axis=1).reshape(-1)
    one_hot = (at[:, None] == jnp.arange(nz * stride)[None, :]).astype(BF16)
    served = dot(one_hot, got_z.reshape(nz * stride, deep)).astype(BF16)
    got_y = lax.all_to_all(
        served.reshape(ny, count + npass, deep), ("p", "q"), 0, 0, tiled=True
    )
    got_y, grads = lax.optimization_barrier((got_y, grads))
    part = jnp.sum(got_y.astype(F32), axis=0).astype(BF16)
    other_part = lax.ppermute(part, "q", swap)
    tokens = all_features(
        jnp.concatenate(
            [part[:count], other_part[:count], part[count:], other_part[count:]], axis=0
        )
    )

    slab_ids_row = jnp.concatenate([slab_ids // pass_rows, slab_ids % pass_rows]).astype(BF16)
    slab_part = jnp.concatenate(
        [my_strip(slab_emb), jnp.pad(slab_ids_row[None], ((0, 15), (0, 0)))], axis=0
    )
    slabs = lax.all_gather(slab_part, IDX, axis=0)
    slab_at = slabs[:, slab].astype(jnp.int32)
    slab_at = jnp.where(slab_at[:, :slab] == my_idx, slab_at[:, slab:], -1)
    slab_at = jnp.pad(slab_at, ((0, 0), (0, 16)), constant_values=-1).reshape(-1)
    put = jnp.arange(pass_rows)[:, None] == slab_at[None, :]
    placed = dot(put.astype(BF16), slabs.reshape(-1, LANES)).astype(BF16)
    refreshed = jnp.where(jnp.any(put, axis=1)[:, None], placed, index_strip)
    refreshed = lax.all_gather(refreshed, M, axis=0)
    refreshed = jnp.concatenate([refreshed[i] for i in range(strips)], axis=1)

    terms, pair_relevance = reader(
        my_half.reshape(1), high, pair_query, tokens, grads, (w_query, w_key, w_value, w_out), owners
    )
    relevance = pair_relevance[0, :npass].reshape(queries, K)
    terms = lax.all_to_all(terms, IDX, 0, 0, tiled=True)
    rows = terms.shape[1] // 2
    sums = jnp.sum(terms.reshape(owners // nq, nq, *terms.shape[1:]).astype(F32), axis=0)

    def whole(top, left):
        return jnp.concatenate(
            [
                sums[h, top * rows : (top + 1) * rows, left * HEAD_DIM : (left + 1) * HEAD_DIM]
                for h in range(nq)
            ],
            axis=1,
        )

    return (
        relevance,
        whole(0, 0),
        whole(0, 1),
        whole(1, 0),
        whole(1, 1).T,
        refreshed,
    )


def solution(mesh):
    devices = mesh.devices
    owners, columns = devices.shape
    fine = Mesh(devices.reshape(owners // 8, 4, 2, columns // 2, 2), (*IDX, *M))
    return jax.shard_map(
        shards,
        mesh=fine,
        in_specs=(
            P(IDX, None),
            P(IDX, None),
            P(IDX, None),
            P(IDX),
            P(IDX, None),
            P(IDX, M),
            P(None, M),
            P(None, M),
            P(None, M),
            P(M, None),
            P(IDX, M),
            P(IDX, None),
            P(IDX),
        ),
        out_specs=(
            P(IDX, None),
            P(IDX, M),
            P(IDX, M),
            P(IDX, M),
            P(M, IDX),
            P(IDX, None),
        ),
        check_vma=False,
    )
```

```python
import functools

import jax
import jax.numpy as jnp
from jax import lax
from jax.experimental import pallas as pl
from jax.experimental.pallas import tpu as pltpu
from jax.sharding import Mesh
from jax.sharding import PartitionSpec as P

HEAD_DIM = 64
K = 20
PLEN = 4
CAPS = 2
LANES = 128
IDX = ("z", "p", "q")
M = ("x", "c")
F32 = jnp.float32
BF16 = jnp.bfloat16
ROWS = (((0,), (0,)), ((), ()))
COLS = (((1,), (1,)), ((), ()))


def dot(a, b, dims=None):
    if dims is None:
        return jnp.dot(a, b, preferred_element_type=F32)
    return lax.dot_general(a, b, dims, preferred_element_type=F32)


def reader_kernel(heads, half_ref, high_ref, query_ref, *refs):
    token_refs, grad_refs, hbm = refs[:2], refs[2:4], refs[4:8]
    out_ref, rel_ref, vmem, sems = refs[8], refs[9], refs[10:14], refs[14]
    copies = [pltpu.make_async_copy(hbm[i], vmem[i], sems.at[i]) for i in range(4)]
    for copy in copies:
        copy.start()
    wq_ref, wk_ref, wv_ref, wo_ref = vmem
    nc, nx, count, deep = grad_refs[0].shape
    blocks = 2 * nx * nc
    strips, passages = query_ref.shape[:2]
    rows = out_ref.shape[1] // 2
    mine = half_ref[0]

    def block(pair, b, low, high):
        x, c = divmod(b, nc)
        return pair[x // nx][c, x % nx, low:high, :]

    acc = jnp.zeros((passages, deep), F32)
    for s in range(strips):
        fetched = block(token_refs, s, count, count + passages)
        acc += fetched.astype(F32) * query_ref[s].astype(F32)
    low = jnp.sum(acc[:, :LANES], axis=1, keepdims=True)
    high = jnp.sum(acc[:, LANES:], axis=1, keepdims=True)
    scores = jnp.where(high_ref[...] > 0, high, low)
    queries = passages // K
    p = lax.broadcasted_iota(jnp.int32, (passages, queries), 0)
    first = lax.broadcasted_iota(jnp.int32, (passages, queries), 1) * K
    group = (p >= first) & (p < first + K)
    top = jnp.max(jnp.where(group, scores, -jnp.inf), axis=0, keepdims=True)
    exps = jnp.where(group, jnp.exp(scores - top), 0.0)
    rel_column = jnp.sum(exps / jnp.sum(exps, axis=0, keepdims=True), axis=1, keepdims=True)
    same = lax.broadcasted_iota(jnp.int32, (passages, passages), 0) == lax.broadcasted_iota(
        jnp.int32, (passages, passages), 1
    )
    rel_row = jnp.sum(jnp.where(same, rel_column, 0.0), axis=0, keepdims=True)
    rel_ref[...] = rel_row
    token = lax.broadcasted_iota(jnp.int32, (count, passages), 0)
    begin = lax.broadcasted_iota(jnp.int32, (count, passages), 1) * PLEN
    of_token = (token >= begin) & (token < begin + PLEN)
    rel = jnp.sum(jnp.where(of_token, rel_row, 0.0), axis=1, keepdims=True)

    tokens = [block(token_refs, b, 0, count) for b in range(blocks)]
    weighted = [
        (block(grad_refs, b, 0, count).astype(F32) * rel).astype(BF16) for b in range(blocks)
    ]
    for copy in copies:
        copy.wait()

    def projected(weight_ref):
        total = dot(tokens[0], weight_ref[:deep])
        for b in range(1, blocks):
            total += dot(tokens[b], weight_ref[b * deep : (b + 1) * deep])
        return total.astype(BF16)

    def own(states):
        kept = states[:, :HEAD_DIM]
        for head in range(1, heads):
            kept = jnp.where(mine == head, states[:, head * HEAD_DIM : (head + 1) * HEAD_DIM], kept)
        return kept

    q, k, v = own(projected(wq_ref)), own(projected(wk_ref)), own(projected(wv_ref))
    total = dot(weighted[0], wo_ref[:, :deep], COLS)
    for b in range(1, blocks):
        total += dot(weighted[b], wo_ref[:, b * deep : (b + 1) * deep], COLS)
    c = own(total.astype(BF16))
    passage_i = lax.broadcasted_iota(jnp.int32, (count, count), 0) // PLEN
    passage_j = lax.broadcasted_iota(jnp.int32, (count, count), 1) // PLEN
    logits = jnp.where(passage_i == passage_j, dot(q, k, COLS), -jnp.inf)
    exps = jnp.exp(logits - jnp.max(logits, axis=1, keepdims=True))
    probs = exps / jnp.sum(exps, axis=1, keepdims=True)
    attn = probs.astype(BF16)
    attn_grad = dot(c, v, COLS)
    mean = jnp.sum(attn_grad * probs, axis=1, keepdims=True)
    score_grad = (probs * (attn_grad - mean)).astype(BF16)
    query_grad = dot(score_grad, k).astype(BF16)
    key_grad = dot(score_grad, q, ROWS).astype(BF16)
    value_grad = dot(attn, c, ROWS).astype(BF16)
    context = dot(attn, v).astype(BF16)
    query_key = jnp.concatenate([query_grad, key_grad], axis=1)
    each = deep // rows
    for b in range(blocks):
        upper = dot(tokens[b], query_key, ROWS).astype(BF16)
        lower = jnp.concatenate(
            [dot(tokens[b], value_grad, ROWS), dot(weighted[b], context, ROWS)], axis=1
        ).astype(BF16)
        out_ref[b * each : (b + 1) * each, :rows, :] = upper.reshape(each, rows, -1)
        out_ref[b * each : (b + 1) * each, rows:, :] = lower.reshape(each, rows, -1)


def reader(half, high, query, tokens, out_grad, weights, owners):
    width, inner = weights[0].shape
    passages = query.shape[1]
    vmem = pl.BlockSpec(memory_space=pltpu.VMEM)
    return pl.pallas_call(
        functools.partial(reader_kernel, inner // HEAD_DIM),
        out_shape=(
            jax.ShapeDtypeStruct((owners, 2 * width // owners, 2 * HEAD_DIM), BF16),
            jax.ShapeDtypeStruct((1, passages), F32),
        ),
        in_specs=[pl.BlockSpec(memory_space=pltpu.SMEM)]
        + [vmem] * 6
        + [pl.BlockSpec(memory_space=pl.ANY)] * 4,
        out_specs=(vmem, vmem),
        scratch_shapes=[pltpu.VMEM((width, inner), BF16)] * 3
        + [pltpu.VMEM((inner, width), BF16), pltpu.SemaphoreType.DMA((4,))],
        compiler_params=pltpu.CompilerParams(vmem_limit_bytes=40 * 1024 * 1024),
        name="reader",
    )(half, high, query, *tokens, *out_grad, *weights)


def all_features(part):
    along_x = lax.all_gather(part, "x", axis=0)
    half = along_x.shape[0] // 2
    return [lax.all_gather(along_x[i * half : (i + 1) * half], "c", axis=0) for i in range(2)]


def shards(
    index_emb,
    query_emb,
    passage_owner,
    passage_row,
    token_ids,
    vocab_table,
    w_query,
    w_key,
    w_value,
    w_out,
    out_grad,
    slab_emb,
    slab_ids,
):
    nz, nq = lax.axis_size("z"), lax.axis_size("q")
    ny = lax.axis_size("p") * nq
    owners = nz * ny
    swap = [(0, 1), (1, 0)]
    my_y = lax.axis_index(("p", "q"))
    my_half = lax.axis_index("q")
    pass_rows, width = index_emb.shape
    queries = query_emb.shape[0]
    npass, plen = token_ids.shape
    count = npass * plen
    vocab_rows = vocab_table.shape[0]
    slab = slab_ids.shape[0]
    strips = width // LANES
    strip = lax.rem(lax.axis_index(M), strips)

    def my_strip(array):
        return lax.dynamic_slice_in_dim(array, strip * LANES, LANES, axis=1)

    deep = vocab_table.shape[1]
    index_strip = my_strip(index_emb)
    folded = pass_rows // 2
    message = jnp.concatenate(
        [vocab_table, jnp.concatenate([index_strip[:folded], index_strip[folded:]], axis=1)], axis=0
    )
    stride = message.shape[0]
    got_z = lax.all_to_all(
        jnp.broadcast_to(message[None], (nz, *message.shape)), "z", 0, 0, tiled=True
    )
    wanted = jnp.concatenate([token_ids.reshape(-1), passage_owner[:, 0], passage_row])
    wanted = jnp.pad(wanted[None], ((0, 0), (0, -wanted.shape[0] % LANES)))
    wanted = lax.all_gather(wanted, ("p", "q"), axis=0, tiled=True)

    query_strips = query_emb.reshape(queries, strips, LANES).transpose(1, 0, 2)
    extra = jnp.concatenate(
        [
            query_strips.reshape(strips, queries * LANES),
            jnp.pad(passage_row.astype(BF16)[None], ((0, 0), (0, deep - npass))),
        ],
        axis=0,
    )
    extra = jnp.pad(extra, ((0, -extra.shape[0] % 16), (0, 0)))
    other = lax.ppermute(jnp.concatenate([out_grad, extra], axis=0), "q", swap)
    grads = all_features(jnp.concatenate([out_grad, other[:count]], axis=0))
    other_strips = other[count : count + strips].reshape(strips, queries, LANES)
    pair_query = jnp.concatenate([query_strips, other_strips], axis=1)
    pair_query = jnp.repeat(jnp.concatenate([pair_query, pair_query], axis=2), K, axis=1)
    other_row = other[count + strips, :npass].astype(jnp.int32)
    high = (jnp.concatenate([passage_row, other_row])[:, None] >= folded).astype(jnp.int32)

    ids, place_owner, place_row = (
        wanted[:, :count],
        wanted[:, count : count + npass],
        wanted[:, count + npass : count + 2 * npass],
    )
    id_owner = ids // vocab_rows
    token_at = jnp.where(id_owner % ny == my_y, id_owner // ny * stride + ids % vocab_rows, -1)
    place_at = jnp.where(
        place_owner % ny == my_y,
        place_owner // ny * stride + vocab_rows + place_row % folded,
        -1,
    )
    at = jnp.concatenate([token_at, place_at], axis=1).reshape(-1)
    one_hot = (at[:, None] == jnp.arange(nz * stride)[None, :]).astype(BF16)
    served = dot(one_hot, got_z.reshape(nz * stride, deep)).astype(BF16)
    got_y = lax.all_to_all(
        served.reshape(ny, count + npass, deep), ("p", "q"), 0, 0, tiled=True
    )
    got_y, grads = lax.optimization_barrier((got_y, grads))
    part = jnp.sum(got_y.astype(F32), axis=0).astype(BF16)
    other_part = lax.ppermute(part, "q", swap)
    tokens = all_features(
        jnp.concatenate(
            [part[:count], other_part[:count], part[count:], other_part[count:]], axis=0
        )
    )

    slab_owner, slab_row = slab_ids // pass_rows, slab_ids % pass_rows
    earlier = (slab_owner[:, None] == slab_owner[None, :]) & (
        jnp.arange(slab)[:, None] > jnp.arange(slab)[None, :]
    )
    slot = slab_owner * CAPS + jnp.sum(earlier.astype(jnp.int32), axis=1)
    select = (jnp.arange(owners * CAPS)[:, None] == slot[None, :]).astype(BF16)
    slab_wide = jnp.concatenate(
        [
            my_strip(slab_emb),
            jnp.broadcast_to((slab_row + 1).astype(BF16)[:, None], (slab, LANES)),
        ],
        axis=1,
    )
    slab_out = dot(select, slab_wide).astype(BF16).reshape(owners, CAPS, 2 * LANES)
    slab_out, _ = lax.optimization_barrier((slab_out, part))
    got_slab = lax.all_to_all(slab_out, IDX, 0, 0, tiled=True).reshape(-1, 2 * LANES)
    got_place = got_slab[:, LANES].astype(jnp.int32) - 1
    put = jnp.arange(pass_rows)[:, None] == got_place[None, :]
    placed = dot(put.astype(BF16), got_slab[:, :LANES]).astype(BF16)
    refreshed = jnp.where(jnp.any(put, axis=1)[:, None], placed, index_strip)
    terms, pair_relevance = reader(
        my_half.reshape(1), high, pair_query, tokens, grads, (w_query, w_key, w_value, w_out), owners
    )
    relevance = pair_relevance[0, :npass].reshape(queries, K)
    refreshed, terms = lax.optimization_barrier((refreshed, terms))
    refreshed = lax.all_gather(refreshed, M, axis=0)
    refreshed = jnp.concatenate([refreshed[i] for i in range(strips)], axis=1)
    terms = lax.all_to_all(terms, IDX, 0, 0, tiled=True)
    rows = terms.shape[1] // 2
    sums = jnp.sum(terms.reshape(owners // nq, nq, *terms.shape[1:]).astype(F32), axis=0)

    def whole(top, left):
        return jnp.concatenate(
            [
                sums[h, top * rows : (top + 1) * rows, left * HEAD_DIM : (left + 1) * HEAD_DIM]
                for h in range(nq)
            ],
            axis=1,
        )

    return (
        relevance,
        whole(0, 0),
        whole(0, 1),
        whole(1, 0),
        whole(1, 1).T,
        refreshed,
    )


def solution(mesh):
    devices = mesh.devices
    owners, columns = devices.shape
    fine = Mesh(devices.reshape(owners // 8, 4, 2, columns // 2, 2), (*IDX, *M))
    return jax.shard_map(
        shards,
        mesh=fine,
        in_specs=(
            P(IDX, None),
            P(IDX, None),
            P(IDX, None),
            P(IDX),
            P(IDX, None),
            P(IDX, M),
            P(None, M),
            P(None, M),
            P(None, M),
            P(M, None),
            P(IDX, M),
            P(IDX, None),
            P(IDX),
        ),
        out_specs=(
            P(IDX, None),
            P(IDX, M),
            P(IDX, M),
            P(IDX, M),
            P(M, IDX),
            P(IDX, None),
        ),
        check_vma=False,
    )
```

```python
import functools

import jax
import jax.numpy as jnp
from jax import lax
from jax.experimental import pallas as pl
from jax.experimental.pallas import tpu as pltpu
from jax.sharding import Mesh
from jax.sharding import PartitionSpec as P

HEAD_DIM = 64
K = 20
PLEN = 4
CAPS = 2
LANES = 128
IDX = ("z", "p", "q")
M = ("x", "c")
F32 = jnp.float32
BF16 = jnp.bfloat16
ROWS = (((0,), (0,)), ((), ()))
COLS = (((1,), (1,)), ((), ()))


def dot(a, b, dims=None):
    if dims is None:
        return jnp.dot(a, b, preferred_element_type=F32)
    return lax.dot_general(a, b, dims, preferred_element_type=F32)


def reader_kernel(heads, half_ref, high_ref, query_ref, *refs):
    token_refs, grad_refs, hbm = refs[:2], refs[2:4], refs[4:8]
    out_ref, rel_ref, vmem, sems = refs[8], refs[9], refs[10:14], refs[14]
    copies = [pltpu.make_async_copy(hbm[i], vmem[i], sems.at[i]) for i in range(4)]
    for copy in copies:
        copy.start()
    wq_ref, wk_ref, wv_ref, wo_ref = vmem
    nc, nx, count, deep = grad_refs[0].shape
    blocks = 2 * nx * nc
    strips, passages = query_ref.shape[:2]
    rows = out_ref.shape[1] // 2
    mine = half_ref[0]

    def grad_block(b):
        x, c = divmod(b, nc)
        return grad_refs[x // nx][c, x % nx]

    def token_block(b, low, high):
        x, c = divmod(b, nc)
        both = [ref[c, x, low:high, :] for ref in token_refs]
        ordered = [jnp.where(mine == 0, both[0], both[1]), jnp.where(mine == 0, both[1], both[0])]
        return jnp.concatenate(ordered, axis=0)

    acc = jnp.zeros((passages, deep), F32)
    for s in range(strips):
        fetched = token_block(s, count // 2, (count + passages) // 2)
        acc += fetched.astype(F32) * query_ref[s].astype(F32)
    low = jnp.sum(acc[:, :LANES], axis=1, keepdims=True)
    high = jnp.sum(acc[:, LANES:], axis=1, keepdims=True)
    scores = jnp.where(high_ref[...] > 0, high, low)
    each, valid = passages // 2, count // 2 // PLEN
    queries = valid // K
    p = lax.broadcasted_iota(jnp.int32, (passages, 2 * queries), 0)
    g = lax.broadcasted_iota(jnp.int32, (passages, 2 * queries), 1)
    first = jnp.where(g >= queries, each + (g - queries) * K, g * K)
    group = (p >= first) & (p < first + K)
    top = jnp.max(jnp.where(group, scores, -jnp.inf), axis=0, keepdims=True)
    exps = jnp.where(group, jnp.exp(scores - top), 0.0)
    rel_column = jnp.sum(exps / jnp.sum(exps, axis=0, keepdims=True), axis=1, keepdims=True)
    same = lax.broadcasted_iota(jnp.int32, (passages, passages), 0) == lax.broadcasted_iota(
        jnp.int32, (passages, passages), 1
    )
    rel_row = jnp.sum(jnp.where(same, rel_column, 0.0), axis=0, keepdims=True)
    rel_ref[...] = rel_row
    token = lax.broadcasted_iota(jnp.int32, (count, passages), 0)
    p = lax.broadcasted_iota(jnp.int32, (count, passages), 1)
    at = jnp.where(p >= each, p - each, p)
    begin = jnp.where(p >= each, count // 2, 0) + at * PLEN
    begin = jnp.where(at < valid, begin, count)
    of_token = (token >= begin) & (token < begin + PLEN)
    rel = jnp.sum(jnp.where(of_token, rel_row, 0.0), axis=1, keepdims=True)

    tokens = [token_block(b, 0, count // 2) for b in range(blocks)]
    weighted = [
        (grad_block(b).astype(F32) * rel).astype(BF16) for b in range(blocks)
    ]
    for copy in copies:
        copy.wait()

    def projected(weight_ref):
        total = dot(tokens[0], weight_ref[:deep])
        for b in range(1, blocks):
            total += dot(tokens[b], weight_ref[b * deep : (b + 1) * deep])
        return total.astype(BF16)

    def own(states):
        kept = states[:, :HEAD_DIM]
        for head in range(1, heads):
            kept = jnp.where(mine == head, states[:, head * HEAD_DIM : (head + 1) * HEAD_DIM], kept)
        return kept

    q, k, v = own(projected(wq_ref)), own(projected(wk_ref)), own(projected(wv_ref))
    total = dot(weighted[0], wo_ref[:, :deep], COLS)
    for b in range(1, blocks):
        total += dot(weighted[b], wo_ref[:, b * deep : (b + 1) * deep], COLS)
    c = own(total.astype(BF16))
    passage_i = lax.broadcasted_iota(jnp.int32, (count, count), 0) // PLEN
    passage_j = lax.broadcasted_iota(jnp.int32, (count, count), 1) // PLEN
    logits = jnp.where(passage_i == passage_j, dot(q, k, COLS), -jnp.inf)
    exps = jnp.exp(logits - jnp.max(logits, axis=1, keepdims=True))
    probs = exps / jnp.sum(exps, axis=1, keepdims=True)
    attn = probs.astype(BF16)
    attn_grad = dot(c, v, COLS)
    mean = jnp.sum(attn_grad * probs, axis=1, keepdims=True)
    score_grad = (probs * (attn_grad - mean)).astype(BF16)
    query_grad = dot(score_grad, k).astype(BF16)
    key_grad = dot(score_grad, q, ROWS).astype(BF16)
    value_grad = dot(attn, c, ROWS).astype(BF16)
    context = dot(attn, v).astype(BF16)
    query_key = jnp.concatenate([query_grad, key_grad], axis=1)
    span = deep // rows
    for b in range(blocks):
        upper = dot(tokens[b], query_key, ROWS).astype(BF16)
        lower = jnp.concatenate(
            [dot(tokens[b], value_grad, ROWS), dot(weighted[b], context, ROWS)], axis=1
        ).astype(BF16)
        out_ref[b * span : (b + 1) * span, :rows, :] = upper.reshape(span, rows, -1)
        out_ref[b * span : (b + 1) * span, rows:, :] = lower.reshape(span, rows, -1)


def reader(half, high, query, tokens, out_grad, weights, owners):
    width, inner = weights[0].shape
    passages = query.shape[1]
    vmem = pl.BlockSpec(memory_space=pltpu.VMEM)
    return pl.pallas_call(
        functools.partial(reader_kernel, inner // HEAD_DIM),
        out_shape=(
            jax.ShapeDtypeStruct((owners, 2 * width // owners, 2 * HEAD_DIM), BF16),
            jax.ShapeDtypeStruct((1, passages), F32),
        ),
        in_specs=[pl.BlockSpec(memory_space=pltpu.SMEM)]
        + [vmem] * 6
        + [pl.BlockSpec(memory_space=pl.ANY)] * 4,
        out_specs=(vmem, vmem),
        scratch_shapes=[pltpu.VMEM((width, inner), BF16)] * 3
        + [pltpu.VMEM((inner, width), BF16), pltpu.SemaphoreType.DMA((4,))],
        compiler_params=pltpu.CompilerParams(vmem_limit_bytes=40 * 1024 * 1024),
        name="reader",
    )(half, high, query, *tokens, *out_grad, *weights)


def shards(
    index_emb,
    query_emb,
    passage_owner,
    passage_row,
    token_ids,
    vocab_table,
    w_query,
    w_key,
    w_value,
    w_out,
    out_grad,
    slab_emb,
    slab_ids,
):
    nz, nq = lax.axis_size("z"), lax.axis_size("q")
    ny = lax.axis_size("p") * nq
    owners = nz * ny
    swap = [(0, 1), (1, 0)]
    my_y = lax.axis_index(("p", "q"))
    my_half = lax.axis_index("q")
    pass_rows, width = index_emb.shape
    queries = query_emb.shape[0]
    npass, plen = token_ids.shape
    count = npass * plen
    vocab_rows = vocab_table.shape[0]
    slab = slab_ids.shape[0]
    strips = width // LANES
    strip = lax.rem(lax.axis_index(M), strips)

    def my_strip(array):
        return lax.dynamic_slice_in_dim(array, strip * LANES, LANES, axis=1)

    deep = vocab_table.shape[1]
    flat_ids = token_ids.reshape(-1)
    upper = jnp.concatenate([flat_ids // LANES, passage_owner[:, 0], passage_row])
    lower = jnp.pad(flat_ids % LANES, (0, 2 * npass))
    wanted = jnp.stack([upper, lower]).astype(BF16)
    wanted = jnp.pad(wanted, ((0, 6), (0, deep - wanted.shape[1])))
    slab_owner, slab_row = slab_ids // pass_rows, slab_ids % pass_rows
    earlier = (slab_owner[:, None] == slab_owner[None, :]) & (
        jnp.arange(slab)[:, None] > jnp.arange(slab)[None, :]
    )
    rank = jnp.sum(earlier.astype(jnp.int32), axis=1)
    slot = ((slab_owner % ny) * nz + slab_owner // ny) * CAPS + rank
    select = (jnp.arange(owners * CAPS)[:, None] == slot[None, :]).astype(BF16)
    slab_wide = jnp.concatenate(
        [
            my_strip(slab_emb),
            jnp.broadcast_to((slab_row + 1).astype(BF16)[:, None], (slab, deep - LANES)),
        ],
        axis=1,
    )
    slab_out = dot(select, slab_wide).astype(BF16).reshape(ny, nz * CAPS, deep)
    got_first = lax.all_to_all(
        jnp.concatenate([jnp.broadcast_to(wanted[None], (ny, *wanted.shape)), slab_out], axis=1),
        ("p", "q"),
        0,
        0,
        tiled=True,
    )
    got_wanted = got_first[:, :2].astype(jnp.int32)
    slab_out = got_first[:, wanted.shape[0] :].reshape(ny, nz, CAPS, deep).transpose(1, 0, 2, 3)

    index_strip = my_strip(index_emb)
    folded = pass_rows // 2
    message = jnp.concatenate(
        [vocab_table, jnp.concatenate([index_strip[:folded], index_strip[folded:]], axis=1)], axis=0
    )
    held = message.shape[0]
    stride = held + ny * CAPS
    got_z = lax.all_to_all(
        jnp.concatenate(
            [
                jnp.broadcast_to(message[None], (nz, *message.shape)),
                slab_out.reshape(nz, ny * CAPS, deep),
            ],
            axis=1,
        ),
        "z",
        0,
        0,
        tiled=True,
    )

    query_strips = query_emb.reshape(queries, strips, LANES).transpose(1, 0, 2)
    extra = jnp.concatenate(
        [
            query_strips.reshape(strips, queries * LANES),
            jnp.pad(passage_row.astype(BF16)[None], ((0, 0), (0, deep - npass))),
        ],
        axis=0,
    )
    extra = jnp.pad(extra, ((0, -extra.shape[0] % 8), (0, 0)))
    pair_message, _ = lax.optimization_barrier(
        (jnp.concatenate([out_grad, extra], axis=0), got_wanted)
    )
    other = lax.ppermute(pair_message, "q", swap)
    grads = lax.all_gather(jnp.concatenate([out_grad, other[:count]], axis=0), "x", axis=0)
    grads = [
        lax.all_gather(grads[i * grads.shape[0] // 2 : (i + 1) * grads.shape[0] // 2], "c", axis=0)
        for i in range(2)
    ]
    got_z, grads = lax.optimization_barrier((got_z, grads))
    other_strips = other[count : count + strips].reshape(strips, queries, LANES)
    spare = -npass % 16

    def per_passage(some):
        some = jnp.repeat(jnp.concatenate([some, some], axis=2), K, axis=1)
        return jnp.pad(some, ((0, 0), (0, spare), (0, 0)))

    pair_query = jnp.concatenate([per_passage(query_strips), per_passage(other_strips)], axis=1)
    other_row = other[count + strips, :npass].astype(jnp.int32)
    high = jnp.concatenate([jnp.pad(passage_row, (0, spare)), jnp.pad(other_row, (0, spare))])
    high = (high[:, None] >= folded).astype(jnp.int32)

    ids = got_wanted[:, 0, :count] * LANES + got_wanted[:, 1, :count]
    place_owner = got_wanted[:, 0, count : count + npass]
    place_row = got_wanted[:, 0, count + npass : count + 2 * npass]
    id_owner = ids // vocab_rows
    token_at = jnp.where(id_owner % ny == my_y, id_owner // ny * stride + ids % vocab_rows, -1)
    place_at = jnp.where(
        place_owner % ny == my_y,
        place_owner // ny * stride + vocab_rows + place_row % folded,
        -1,
    )
    at = jnp.concatenate([token_at, place_at, jnp.full((ny, spare), -1, jnp.int32)], axis=1)
    at = at.reshape(-1)
    one_hot = (at[:, None] == jnp.arange(nz * stride)[None, :]).astype(BF16)
    served = dot(one_hot, got_z.reshape(nz * stride, deep)).astype(BF16)
    got_y = lax.all_to_all(
        served.reshape(ny, count + npass + spare, deep), ("p", "q"), 0, 0, tiled=True
    )
    part = jnp.sum(got_y.astype(F32), axis=0).astype(BF16)

    nx = lax.axis_size("x")
    near = lax.all_to_all(
        jnp.broadcast_to(part[None], (nq * nx, *part.shape)), ("q", "x"), 0, 0, tiled=True
    )
    tokens = [lax.all_gather(near[i * nx : (i + 1) * nx], "c", axis=0) for i in range(nq)]

    got_slab = got_z[:, held:].reshape(-1, deep)
    got_place = got_slab[:, LANES].astype(jnp.int32) - 1
    put = jnp.arange(pass_rows)[:, None] == got_place[None, :]
    placed = dot(put.astype(BF16), got_slab[:, :LANES]).astype(BF16)
    refreshed = jnp.where(jnp.any(put, axis=1)[:, None], placed, index_strip)
    refreshed, _ = lax.optimization_barrier((refreshed, served))
    refreshed = lax.all_gather(refreshed, M, axis=0)
    refreshed = jnp.concatenate([refreshed[i] for i in range(strips)], axis=1)

    terms, pair_relevance = reader(
        my_half.reshape(1), high, pair_query, tokens, grads, (w_query, w_key, w_value, w_out), owners
    )
    relevance = pair_relevance[0, :npass].reshape(queries, K)
    terms = lax.all_to_all(terms, IDX, 0, 0, tiled=True)
    rows = terms.shape[1] // 2
    sums = jnp.sum(terms.reshape(owners // nq, nq, *terms.shape[1:]).astype(F32), axis=0)

    def whole(top, left):
        return jnp.concatenate(
            [
                sums[h, top * rows : (top + 1) * rows, left * HEAD_DIM : (left + 1) * HEAD_DIM]
                for h in range(nq)
            ],
            axis=1,
        )

    return (
        relevance,
        whole(0, 0),
        whole(0, 1),
        whole(1, 0),
        whole(1, 1).T,
        refreshed,
    )


def solution(mesh):
    devices = mesh.devices
    owners, columns = devices.shape
    fine = Mesh(devices.reshape(owners // 8, 4, 2, columns // 2, 2), (*IDX, *M))
    return jax.shard_map(
        shards,
        mesh=fine,
        in_specs=(
            P(IDX, None),
            P(IDX, None),
            P(IDX, None),
            P(IDX),
            P(IDX, None),
            P(IDX, M),
            P(None, M),
            P(None, M),
            P(None, M),
            P(M, None),
            P(IDX, M),
            P(IDX, None),
            P(IDX),
        ),
        out_specs=(
            P(IDX, None),
            P(IDX, M),
            P(IDX, M),
            P(IDX, M),
            P(M, IDX),
            P(IDX, None),
        ),
        check_vma=False,
    )
```

```python
import functools

import jax
import jax.numpy as jnp
from jax import lax
from jax.experimental import pallas as pl
from jax.experimental.pallas import tpu as pltpu
from jax.sharding import Mesh
from jax.sharding import PartitionSpec as P

HEAD_DIM = 64
K = 20
PLEN = 4
CAPS = 2
LANES = 128
IDX = ("z", "p", "q")
M = ("x", "c")
ALONG = ("z", "p", "q", "c")
F32 = jnp.float32
BF16 = jnp.bfloat16
ROWS = (((0,), (0,)), ((), ()))
COLS = (((1,), (1,)), ((), ()))


def dot(a, b, dims=None):
    if dims is None:
        return jnp.dot(a, b, preferred_element_type=F32)
    return lax.dot_general(a, b, dims, preferred_element_type=F32)


def reader_kernel(heads, half_ref, high_ref, query_ref, *refs):
    token_refs, grad_refs, hbm = refs[:2], refs[2:4], refs[4:8]
    out_ref, rel_ref, vmem, sems = refs[8], refs[9], refs[10:14], refs[14]
    copies = [pltpu.make_async_copy(hbm[i], vmem[i], sems.at[i]) for i in range(4)]
    for copy in copies:
        copy.start()
    wq_ref, wk_ref, wv_ref, wo_ref = vmem
    nc, nx, count, deep = grad_refs[0].shape
    blocks = 2 * nx * nc
    strips, passages = query_ref.shape[:2]
    rows = out_ref.shape[1] // 2
    mine = half_ref[0]

    def grad_block(b):
        x, c = divmod(b, nc)
        return grad_refs[x // nx][c, x % nx]

    def token_block(b, low, high):
        x, c = divmod(b, nc)
        both = [ref[c, x, low:high, :] for ref in token_refs]
        ordered = [jnp.where(mine == 0, both[0], both[1]), jnp.where(mine == 0, both[1], both[0])]
        return jnp.concatenate(ordered, axis=0)

    acc = jnp.zeros((passages, deep), F32)
    for s in range(strips):
        fetched = token_block(s, count // 2, (count + passages) // 2)
        acc += fetched.astype(F32) * query_ref[s].astype(F32)
    low = jnp.sum(acc[:, :LANES], axis=1, keepdims=True)
    high = jnp.sum(acc[:, LANES:], axis=1, keepdims=True)
    scores = jnp.where(high_ref[...] > 0, high, low)
    each, valid = passages // 2, count // 2 // PLEN
    queries = valid // K
    p = lax.broadcasted_iota(jnp.int32, (passages, 2 * queries), 0)
    g = lax.broadcasted_iota(jnp.int32, (passages, 2 * queries), 1)
    first = jnp.where(g >= queries, each + (g - queries) * K, g * K)
    group = (p >= first) & (p < first + K)
    top = jnp.max(jnp.where(group, scores, -jnp.inf), axis=0, keepdims=True)
    exps = jnp.where(group, jnp.exp(scores - top), 0.0)
    rel_column = jnp.sum(exps / jnp.sum(exps, axis=0, keepdims=True), axis=1, keepdims=True)
    same = lax.broadcasted_iota(jnp.int32, (passages, passages), 0) == lax.broadcasted_iota(
        jnp.int32, (passages, passages), 1
    )
    rel_row = jnp.sum(jnp.where(same, rel_column, 0.0), axis=0, keepdims=True)
    rel_ref[...] = rel_row
    token = lax.broadcasted_iota(jnp.int32, (count, passages), 0)
    p = lax.broadcasted_iota(jnp.int32, (count, passages), 1)
    at = jnp.where(p >= each, p - each, p)
    begin = jnp.where(p >= each, count // 2, 0) + at * PLEN
    begin = jnp.where(at < valid, begin, count)
    of_token = (token >= begin) & (token < begin + PLEN)
    rel = jnp.sum(jnp.where(of_token, rel_row, 0.0), axis=1, keepdims=True)

    tokens = [token_block(b, 0, count // 2) for b in range(blocks)]
    weighted = [
        (grad_block(b).astype(F32) * rel).astype(BF16) for b in range(blocks)
    ]
    for copy in copies:
        copy.wait()

    def projected(weight_ref):
        total = dot(tokens[0], weight_ref[:deep])
        for b in range(1, blocks):
            total += dot(tokens[b], weight_ref[b * deep : (b + 1) * deep])
        return total.astype(BF16)

    def own(states):
        kept = states[:, :HEAD_DIM]
        for head in range(1, heads):
            kept = jnp.where(mine == head, states[:, head * HEAD_DIM : (head + 1) * HEAD_DIM], kept)
        return kept

    q, k, v = own(projected(wq_ref)), own(projected(wk_ref)), own(projected(wv_ref))
    total = dot(weighted[0], wo_ref[:, :deep], COLS)
    for b in range(1, blocks):
        total += dot(weighted[b], wo_ref[:, b * deep : (b + 1) * deep], COLS)
    c = own(total.astype(BF16))
    passage_i = lax.broadcasted_iota(jnp.int32, (count, count), 0) // PLEN
    passage_j = lax.broadcasted_iota(jnp.int32, (count, count), 1) // PLEN
    logits = jnp.where(passage_i == passage_j, dot(q, k, COLS), -jnp.inf)
    exps = jnp.exp(logits - jnp.max(logits, axis=1, keepdims=True))
    probs = exps / jnp.sum(exps, axis=1, keepdims=True)
    attn = probs.astype(BF16)
    attn_grad = dot(c, v, COLS)
    mean = jnp.sum(attn_grad * probs, axis=1, keepdims=True)
    score_grad = (probs * (attn_grad - mean)).astype(BF16)
    query_grad = dot(score_grad, k).astype(BF16)
    key_grad = dot(score_grad, q, ROWS).astype(BF16)
    value_grad = dot(attn, c, ROWS).astype(BF16)
    context = dot(attn, v).astype(BF16)
    query_key = jnp.concatenate([query_grad, key_grad], axis=1)
    span = deep // rows
    for b in range(blocks):
        upper = dot(tokens[b], query_key, ROWS).astype(BF16)
        lower = jnp.concatenate(
            [dot(tokens[b], value_grad, ROWS), dot(weighted[b], context, ROWS)], axis=1
        ).astype(BF16)
        out_ref[b * span : (b + 1) * span, :rows, :] = upper.reshape(span, rows, -1)
        out_ref[b * span : (b + 1) * span, rows:, :] = lower.reshape(span, rows, -1)


def reader(half, high, query, tokens, out_grad, weights, owners):
    width, inner = weights[0].shape
    passages = query.shape[1]
    vmem = pl.BlockSpec(memory_space=pltpu.VMEM)
    return pl.pallas_call(
        functools.partial(reader_kernel, inner // HEAD_DIM),
        out_shape=(
            jax.ShapeDtypeStruct((owners, 2 * width // owners, 2 * HEAD_DIM), BF16),
            jax.ShapeDtypeStruct((1, passages), F32),
        ),
        in_specs=[pl.BlockSpec(memory_space=pltpu.SMEM)]
        + [vmem] * 6
        + [pl.BlockSpec(memory_space=pl.ANY)] * 4,
        out_specs=(vmem, vmem),
        scratch_shapes=[pltpu.VMEM((width, inner), BF16)] * 3
        + [pltpu.VMEM((inner, width), BF16), pltpu.SemaphoreType.DMA((4,))],
        compiler_params=pltpu.CompilerParams(vmem_limit_bytes=40 * 1024 * 1024),
        name="reader",
    )(half, high, query, *tokens, *out_grad, *weights)


def shards(
    index_emb,
    query_emb,
    passage_owner,
    passage_row,
    token_ids,
    vocab_table,
    w_query,
    w_key,
    w_value,
    w_out,
    out_grad,
    slab_emb,
    slab_ids,
):
    nz, nq = lax.axis_size("z"), lax.axis_size("q")
    ny = lax.axis_size("p") * nq
    owners = nz * ny
    swap = [(0, 1), (1, 0)]
    my_z = lax.axis_index("z")
    my_y = lax.axis_index(("p", "q"))
    my_half = lax.axis_index("q")
    pass_rows, width = index_emb.shape
    queries = query_emb.shape[0]
    npass, plen = token_ids.shape
    count = npass * plen
    vocab_rows = vocab_table.shape[0]
    slab = slab_ids.shape[0]
    strips = width // LANES
    strip = lax.rem(lax.axis_index(M), strips)

    def my_strip(array):
        return lax.dynamic_slice_in_dim(array, strip * LANES, LANES, axis=1)

    cores = lax.axis_size("c")
    my_core = lax.axis_index("c")
    at_z = [[(z * ny + y) * cores for z in range(nz)] for y in range(ny)]
    at_y = [[(z * ny + y) * cores for y in range(ny)] for z in range(nz)]
    first_groups = at_z + [[i + 1 for i in group] for group in at_y]
    second_groups = at_y + [[i + 1 for i in group] for group in at_z]
    second = jnp.where(my_core == 0, my_y, my_z)

    def places(owner):
        z, y = owner // ny, owner % ny
        return jnp.where(my_core == 0, z, y), jnp.where(my_core == 0, y, z)

    deep = vocab_table.shape[1]
    index_strip = my_strip(index_emb)
    folded = pass_rows // 2
    message = jnp.concatenate(
        [vocab_table, jnp.concatenate([index_strip[:folded], index_strip[folded:]], axis=1)], axis=0
    )
    held = message.shape[0]
    stride = held + ny * CAPS
    slab_owner, slab_row = slab_ids // pass_rows, slab_ids % pass_rows
    earlier = (slab_owner[:, None] == slab_owner[None, :]) & (
        jnp.arange(slab)[:, None] > jnp.arange(slab)[None, :]
    )
    rank = jnp.sum(earlier.astype(jnp.int32), axis=1)
    slab_first, slab_second = places(slab_owner)
    slot = (slab_first * ny + slab_second) * CAPS + rank
    select = (jnp.arange(owners * CAPS)[:, None] == slot[None, :]).astype(BF16)
    slab_wide = jnp.concatenate(
        [
            my_strip(slab_emb),
            jnp.broadcast_to((slab_row + 1).astype(BF16)[:, None], (slab, deep - LANES)),
        ],
        axis=1,
    )
    slab_out = dot(select, slab_wide).astype(BF16).reshape(nz, ny * CAPS, deep)
    got_first = lax.all_to_all(
        jnp.concatenate([jnp.broadcast_to(message[None], (nz, *message.shape)), slab_out], axis=1),
        ALONG,
        0,
        0,
        axis_index_groups=first_groups,
        tiled=True,
    )
    wanted = jnp.concatenate([token_ids.reshape(-1), passage_owner[:, 0], passage_row])
    wanted = jnp.pad(wanted[None], ((0, 0), (0, -wanted.shape[0] % LANES)))
    wanted = lax.all_gather(
        wanted, ALONG, axis=0, axis_index_groups=second_groups, tiled=True
    )

    query_strips = query_emb.reshape(queries, strips, LANES).transpose(1, 0, 2)
    extra = jnp.concatenate(
        [
            query_strips.reshape(strips, queries * LANES),
            jnp.pad(passage_row.astype(BF16)[None], ((0, 0), (0, deep - npass))),
        ],
        axis=0,
    )
    extra = jnp.pad(extra, ((0, -extra.shape[0] % 8), (0, 0)))
    other = lax.ppermute(jnp.concatenate([out_grad, extra], axis=0), "q", swap)
    grads = lax.all_gather(jnp.concatenate([out_grad, other[:count]], axis=0), "x", axis=0)
    grads = [
        lax.all_gather(grads[i * grads.shape[0] // 2 : (i + 1) * grads.shape[0] // 2], "c", axis=0)
        for i in range(2)
    ]
    other_strips = other[count : count + strips].reshape(strips, queries, LANES)
    spare = -npass % 16

    def per_passage(some):
        some = jnp.repeat(jnp.concatenate([some, some], axis=2), K, axis=1)
        return jnp.pad(some, ((0, 0), (0, spare), (0, 0)))

    pair_query = jnp.concatenate([per_passage(query_strips), per_passage(other_strips)], axis=1)
    other_row = other[count + strips, :npass].astype(jnp.int32)
    high = jnp.concatenate([jnp.pad(passage_row, (0, spare)), jnp.pad(other_row, (0, spare))])
    high = (high[:, None] >= folded).astype(jnp.int32)

    ids, place_owner, place_row = (
        wanted[:, :count],
        wanted[:, count : count + npass],
        wanted[:, count + npass : count + 2 * npass],
    )
    token_first, token_second = places(ids // vocab_rows)
    token_at = jnp.where(token_second == second, token_first * stride + ids % vocab_rows, -1)
    place_first, place_second = places(place_owner)
    place_at = jnp.where(
        place_second == second, place_first * stride + vocab_rows + place_row % folded, -1
    )
    slab_at = (
        held
        + jnp.arange(ny)[:, None, None] * CAPS
        + jnp.arange(nz)[None, :, None] * stride
        + jnp.arange(CAPS)[None, None, :]
    ).reshape(ny, nz * CAPS)
    at = jnp.concatenate(
        [token_at, place_at, jnp.full((ny, spare), -1, jnp.int32), slab_at], axis=1
    )
    one_hot = (at.reshape(-1)[:, None] == jnp.arange(nz * stride)[None, :]).astype(BF16)
    served = dot(one_hot, got_first.reshape(nz * stride, deep)).astype(BF16)
    got_second = lax.all_to_all(
        served.reshape(*at.shape, deep),
        ALONG,
        0,
        0,
        axis_index_groups=second_groups,
        tiled=True,
    )
    got_second, grads = lax.optimization_barrier((got_second, grads))
    rows_here = count + npass + spare
    part = jnp.sum(got_second[:, :rows_here].astype(F32), axis=0).astype(BF16)

    nx = lax.axis_size("x")
    near = lax.all_to_all(
        jnp.broadcast_to(part[None], (nq * nx, *part.shape)), ("q", "x"), 0, 0, tiled=True
    )
    tokens = [lax.all_gather(near[i * nx : (i + 1) * nx], "c", axis=0) for i in range(nq)]

    got_slab = got_second[:, rows_here:].reshape(-1, deep)
    got_place = got_slab[:, LANES].astype(jnp.int32) - 1
    put = jnp.arange(pass_rows)[:, None] == got_place[None, :]
    placed = dot(put.astype(BF16), got_slab[:, :LANES]).astype(BF16)
    refreshed = jnp.where(jnp.any(put, axis=1)[:, None], placed, index_strip)

    terms, pair_relevance = reader(
        my_half.reshape(1), high, pair_query, tokens, grads, (w_query, w_key, w_value, w_out), owners
    )
    relevance = pair_relevance[0, :npass].reshape(queries, K)
    refreshed, terms = lax.optimization_barrier((refreshed, terms))
    refreshed = lax.all_gather(refreshed, M, axis=0)
    refreshed = jnp.concatenate([refreshed[i] for i in range(strips)], axis=1)
    terms = lax.all_to_all(terms, IDX, 0, 0, tiled=True)
    rows = terms.shape[1] // 2
    sums = jnp.sum(terms.reshape(owners // nq, nq, *terms.shape[1:]).astype(F32), axis=0)

    def whole(top, left):
        return jnp.concatenate(
            [
                sums[h, top * rows : (top + 1) * rows, left * HEAD_DIM : (left + 1) * HEAD_DIM]
                for h in range(nq)
            ],
            axis=1,
        )

    return (
        relevance,
        whole(0, 0),
        whole(0, 1),
        whole(1, 0),
        whole(1, 1).T,
        refreshed,
    )


def solution(mesh):
    devices = mesh.devices
    owners, columns = devices.shape
    fine = Mesh(devices.reshape(owners // 8, 4, 2, columns // 2, 2), (*IDX, *M))
    return jax.shard_map(
        shards,
        mesh=fine,
        in_specs=(
            P(IDX, None),
            P(IDX, None),
            P(IDX, None),
            P(IDX),
            P(IDX, None),
            P(IDX, M),
            P(None, M),
            P(None, M),
            P(None, M),
            P(M, None),
            P(IDX, M),
            P(IDX, None),
            P(IDX),
        ),
        out_specs=(
            P(IDX, None),
            P(IDX, M),
            P(IDX, M),
            P(IDX, M),
            P(M, IDX),
            P(IDX, None),
        ),
        check_vma=False,
    )
```

```python
import functools

import jax
import jax.numpy as jnp
from jax import lax
from jax.experimental import pallas as pl
from jax.experimental.pallas import tpu as pltpu
from jax.sharding import Mesh
from jax.sharding import PartitionSpec as P

HEAD_DIM = 64
K = 20
PLEN = 4
CAPS = 2
LANES = 128
REACH = 4096
IDX = ("z", "p", "q")
M = ("x", "c")
ALONG = ("z", "p", "q", "c")
F32 = jnp.float32
BF16 = jnp.bfloat16
ROWS = (((0,), (0,)), ((), ()))
COLS = (((1,), (1,)), ((), ()))


def dot(a, b, dims=None):
    if dims is None:
        return jnp.dot(a, b, preferred_element_type=F32)
    return lax.dot_general(a, b, dims, preferred_element_type=F32)


def reader_kernel(heads, half_ref, high_ref, query_ref, *refs):
    token_refs, grad_refs, hbm = refs[:2], refs[2:4], refs[4:8]
    out_ref, rel_ref, vmem, sems = refs[8], refs[9], refs[10:14], refs[14]
    copies = [pltpu.make_async_copy(hbm[i], vmem[i], sems.at[i]) for i in range(4)]
    for copy in copies:
        copy.start()
    wq_ref, wk_ref, wv_ref, wo_ref = vmem
    nc, nx, count, deep = grad_refs[0].shape
    blocks = 2 * nx * nc
    strips, passages = query_ref.shape[:2]
    rows = out_ref.shape[1] // 2
    mine = half_ref[0]

    def grad_block(b):
        x, c = divmod(b, nc)
        return grad_refs[x // nx][c, x % nx]

    def token_block(b, low, high):
        x, c = divmod(b, nc)
        both = [ref[c, x, low:high, :] for ref in token_refs]
        ordered = [jnp.where(mine == 0, both[0], both[1]), jnp.where(mine == 0, both[1], both[0])]
        return jnp.concatenate(ordered, axis=0)

    acc = jnp.zeros((passages, deep), F32)
    for s in range(strips):
        fetched = token_block(s, count // 2, (count + passages) // 2)
        acc += fetched.astype(F32) * query_ref[s].astype(F32)
    low = jnp.sum(acc[:, :LANES], axis=1, keepdims=True)
    high = jnp.sum(acc[:, LANES:], axis=1, keepdims=True)
    scores = jnp.where(high_ref[...] > 0, high, low)
    each, valid = passages // 2, count // 2 // PLEN
    queries = valid // K
    p = lax.broadcasted_iota(jnp.int32, (passages, 2 * queries), 0)
    g = lax.broadcasted_iota(jnp.int32, (passages, 2 * queries), 1)
    first = jnp.where(g >= queries, each + (g - queries) * K, g * K)
    group = (p >= first) & (p < first + K)
    top = jnp.max(jnp.where(group, scores, -jnp.inf), axis=0, keepdims=True)
    exps = jnp.where(group, jnp.exp(scores - top), 0.0)
    rel_column = jnp.sum(exps / jnp.sum(exps, axis=0, keepdims=True), axis=1, keepdims=True)
    same = lax.broadcasted_iota(jnp.int32, (passages, passages), 0) == lax.broadcasted_iota(
        jnp.int32, (passages, passages), 1
    )
    rel_row = jnp.sum(jnp.where(same, rel_column, 0.0), axis=0, keepdims=True)
    rel_ref[...] = rel_row
    token = lax.broadcasted_iota(jnp.int32, (count, passages), 0)
    p = lax.broadcasted_iota(jnp.int32, (count, passages), 1)
    at = jnp.where(p >= each, p - each, p)
    begin = jnp.where(p >= each, count // 2, 0) + at * PLEN
    begin = jnp.where(at < valid, begin, count)
    of_token = (token >= begin) & (token < begin + PLEN)
    rel = jnp.sum(jnp.where(of_token, rel_row, 0.0), axis=1, keepdims=True)

    tokens = [token_block(b, 0, count // 2) for b in range(blocks)]
    weighted = [
        (grad_block(b).astype(F32) * rel).astype(BF16) for b in range(blocks)
    ]
    for copy in copies:
        copy.wait()

    def projected(weight_ref):
        total = dot(tokens[0], weight_ref[:deep])
        for b in range(1, blocks):
            total += dot(tokens[b], weight_ref[b * deep : (b + 1) * deep])
        return total.astype(BF16)

    def own(states):
        kept = states[:, :HEAD_DIM]
        for head in range(1, heads):
            kept = jnp.where(mine == head, states[:, head * HEAD_DIM : (head + 1) * HEAD_DIM], kept)
        return kept

    q, k, v = own(projected(wq_ref)), own(projected(wk_ref)), own(projected(wv_ref))
    total = dot(weighted[0], wo_ref[:, :deep], COLS)
    for b in range(1, blocks):
        total += dot(weighted[b], wo_ref[:, b * deep : (b + 1) * deep], COLS)
    c = own(total.astype(BF16))
    passage_i = lax.broadcasted_iota(jnp.int32, (count, count), 0) // PLEN
    passage_j = lax.broadcasted_iota(jnp.int32, (count, count), 1) // PLEN
    logits = jnp.where(passage_i == passage_j, dot(q, k, COLS), -jnp.inf)
    exps = jnp.exp(logits - jnp.max(logits, axis=1, keepdims=True))
    probs = exps / jnp.sum(exps, axis=1, keepdims=True)
    attn = probs.astype(BF16)
    attn_grad = dot(c, v, COLS)
    mean = jnp.sum(attn_grad * probs, axis=1, keepdims=True)
    score_grad = (probs * (attn_grad - mean)).astype(BF16)
    query_grad = dot(score_grad, k).astype(BF16)
    key_grad = dot(score_grad, q, ROWS).astype(BF16)
    value_grad = dot(attn, c, ROWS).astype(BF16)
    context = dot(attn, v).astype(BF16)
    query_key = jnp.concatenate([query_grad, key_grad], axis=1)
    span = deep // rows
    for b in range(blocks):
        upper = dot(tokens[b], query_key, ROWS).astype(BF16)
        lower = jnp.concatenate(
            [dot(tokens[b], value_grad, ROWS), dot(weighted[b], context, ROWS)], axis=1
        ).astype(BF16)
        out_ref[b * span : (b + 1) * span, :rows, :] = upper.reshape(span, rows, -1)
        out_ref[b * span : (b + 1) * span, rows:, :] = lower.reshape(span, rows, -1)


def reader(half, high, query, tokens, out_grad, weights, owners):
    width, inner = weights[0].shape
    passages = query.shape[1]
    vmem = pl.BlockSpec(memory_space=pltpu.VMEM)
    return pl.pallas_call(
        functools.partial(reader_kernel, inner // HEAD_DIM),
        out_shape=(
            jax.ShapeDtypeStruct((owners, 2 * width // owners, 2 * HEAD_DIM), BF16),
            jax.ShapeDtypeStruct((1, passages), F32),
        ),
        in_specs=[pl.BlockSpec(memory_space=pltpu.SMEM)]
        + [vmem] * 6
        + [pl.BlockSpec(memory_space=pl.ANY)] * 4,
        out_specs=(vmem, vmem),
        scratch_shapes=[pltpu.VMEM((width, inner), BF16)] * 3
        + [pltpu.VMEM((inner, width), BF16), pltpu.SemaphoreType.DMA((4,))],
        compiler_params=pltpu.CompilerParams(vmem_limit_bytes=40 * 1024 * 1024),
        name="reader",
    )(half, high, query, *tokens, *out_grad, *weights)


def shards(
    index_emb,
    query_emb,
    passage_owner,
    passage_row,
    token_ids,
    vocab_table,
    w_query,
    w_key,
    w_value,
    w_out,
    out_grad,
    slab_emb,
    slab_ids,
):
    nz, nq = lax.axis_size("z"), lax.axis_size("q")
    ny = lax.axis_size("p") * nq
    owners = nz * ny
    swap = [(0, 1), (1, 0)]
    my_z = lax.axis_index("z")
    my_y = lax.axis_index(("p", "q"))
    my_half = lax.axis_index("q")
    pass_rows, width = index_emb.shape
    queries = query_emb.shape[0]
    npass, plen = token_ids.shape
    count = npass * plen
    vocab_rows = vocab_table.shape[0]
    slab = slab_ids.shape[0]
    strips = width // LANES
    strip = lax.rem(lax.axis_index(M), strips)

    def my_strip(array):
        return lax.dynamic_slice_in_dim(array, strip * LANES, LANES, axis=1)

    cores = lax.axis_size("c")
    my_core = lax.axis_index("c")
    at_z = [[(z * ny + y) * cores for z in range(nz)] for y in range(ny)]
    at_y = [[(z * ny + y) * cores for y in range(ny)] for z in range(nz)]
    first_groups = at_z + [[i + 1 for i in group] for group in at_y]
    second_groups = at_y + [[i + 1 for i in group] for group in at_z]
    second = jnp.where(my_core == 0, my_y, my_z)

    def places(owner, core):
        z, y = owner // ny, owner % ny
        return jnp.where(core == 0, z, y), jnp.where(core == 0, y, z)

    deep = vocab_table.shape[1]
    index_strip = my_strip(index_emb)
    folded = pass_rows // 2
    message = jnp.concatenate(
        [vocab_table, jnp.concatenate([index_strip[:folded], index_strip[folded:]], axis=1)], axis=0
    )
    asked = message.shape[0]
    held = asked + 8
    stride = held + ny * CAPS
    spare = -npass % 16
    flat_ids = token_ids.reshape(-1)
    row = jnp.concatenate([flat_ids % vocab_rows, vocab_rows + passage_row % folded])
    row_first, row_second = places(
        jnp.concatenate([flat_ids // vocab_rows, passage_owner[:, 0]]), 1 - my_core
    )
    code = row_second * REACH + row_first * stride + row
    rows_here = count + npass + spare
    code = jnp.pad(code, (0, deep - code.shape[0]), constant_values=ny * REACH - 1)
    code = jnp.pad(jnp.stack([code // LANES, code % LANES]).astype(BF16), ((0, 6), (0, 0)))
    message = jnp.concatenate([message, code], axis=0)
    slab_owner, slab_row = slab_ids // pass_rows, slab_ids % pass_rows
    earlier = (slab_owner[:, None] == slab_owner[None, :]) & (
        jnp.arange(slab)[:, None] > jnp.arange(slab)[None, :]
    )
    rank = jnp.sum(earlier.astype(jnp.int32), axis=1)
    slab_first, slab_second = places(slab_owner, my_core)
    slot = (slab_first * ny + slab_second) * CAPS + rank
    select = (jnp.arange(owners * CAPS)[:, None] == slot[None, :]).astype(BF16)
    slab_wide = jnp.concatenate(
        [
            my_strip(slab_emb),
            jnp.broadcast_to((slab_row + 1).astype(BF16)[:, None], (slab, deep - LANES)),
        ],
        axis=1,
    )
    slab_out = dot(select, slab_wide).astype(BF16).reshape(nz, ny * CAPS, deep)
    got_first = lax.all_to_all(
        jnp.concatenate([jnp.broadcast_to(message[None], (nz, *message.shape)), slab_out], axis=1),
        ALONG,
        0,
        0,
        axis_index_groups=first_groups,
        tiled=True,
    )
    query_strips = query_emb.reshape(queries, strips, LANES).transpose(1, 0, 2)
    extra = jnp.concatenate(
        [
            query_strips.reshape(strips, queries * LANES),
            jnp.pad(passage_row.astype(BF16)[None], ((0, 0), (0, deep - npass))),
        ],
        axis=0,
    )
    extra = jnp.pad(extra, ((0, -extra.shape[0] % 8), (0, 0)))
    other = lax.ppermute(jnp.concatenate([out_grad, extra], axis=0), "q", swap)
    got_first, other = lax.optimization_barrier((got_first, other))
    along_x = lax.all_gather(jnp.concatenate([out_grad, other[:count]], axis=0), "x", axis=0)
    other_strips = other[count : count + strips].reshape(strips, queries, LANES)
    def per_passage(some):
        some = jnp.repeat(jnp.concatenate([some, some], axis=2), K, axis=1)
        return jnp.pad(some, ((0, 0), (0, spare), (0, 0)))

    pair_query = jnp.concatenate([per_passage(query_strips), per_passage(other_strips)], axis=1)
    other_row = other[count + strips, :npass].astype(jnp.int32)
    high = jnp.concatenate([jnp.pad(passage_row, (0, spare)), jnp.pad(other_row, (0, spare))])
    high = (high[:, None] >= folded).astype(jnp.int32)

    wanted = lax.ppermute(got_first[:, asked : asked + 2], "c", [(0, 1), (1, 0)])
    wanted = wanted.astype(jnp.int32)[:, :, :rows_here]
    rows_at = wanted[:, 0] * LANES + wanted[:, 1] - second * REACH
    slab_at = (
        held
        + jnp.arange(ny)[:, None, None] * CAPS
        + jnp.arange(nz)[None, :, None] * stride
        + jnp.arange(CAPS)[None, None, :]
    ).reshape(ny, nz * CAPS)
    at = jnp.concatenate([rows_at, slab_at], axis=1)
    one_hot = (at.reshape(-1)[:, None] == jnp.arange(nz * stride)[None, :]).astype(BF16)
    served = dot(one_hot, got_first.reshape(nz * stride, deep)).astype(BF16)
    got_second = lax.all_to_all(
        served.reshape(*at.shape, deep),
        ALONG,
        0,
        0,
        axis_index_groups=second_groups,
        tiled=True,
    )
    got_second, along_x = lax.optimization_barrier((got_second, along_x))
    part = jnp.sum(got_second[:, :rows_here].astype(F32), axis=0).astype(BF16)

    nx = lax.axis_size("x")
    grads = [
        lax.all_gather(along_x[i * nx // 2 : (i + 1) * nx // 2], "c", axis=0) for i in range(2)
    ]
    near = lax.all_to_all(
        jnp.broadcast_to(part[None], (nq * nx, *part.shape)), ("q", "x"), 0, 0, tiled=True
    )
    near, grads = lax.optimization_barrier((near, grads))
    tokens = [lax.all_gather(near[i * nx : (i + 1) * nx], "c", axis=0) for i in range(nq)]

    got_slab = got_second[:, rows_here:].reshape(-1, deep)
    got_place = got_slab[:, LANES].astype(jnp.int32) - 1
    put = jnp.arange(pass_rows)[:, None] == got_place[None, :]
    placed = dot(put.astype(BF16), got_slab[:, :LANES]).astype(BF16)
    refreshed = jnp.where(jnp.any(put, axis=1)[:, None], placed, index_strip)

    terms, pair_relevance = reader(
        my_half.reshape(1), high, pair_query, tokens, grads, (w_query, w_key, w_value, w_out), owners
    )
    relevance = pair_relevance[0, :npass].reshape(queries, K)
    refreshed, terms = lax.optimization_barrier((refreshed, terms))
    refreshed = lax.all_gather(refreshed, M, axis=0)
    refreshed = jnp.concatenate([refreshed[i] for i in range(strips)], axis=1)
    terms = lax.all_to_all(terms, IDX, 0, 0, tiled=True)
    rows = terms.shape[1] // 2
    sums = jnp.sum(terms.reshape(owners // nq, nq, *terms.shape[1:]).astype(F32), axis=0)

    def whole(top, left):
        return jnp.concatenate(
            [
                sums[h, top * rows : (top + 1) * rows, left * HEAD_DIM : (left + 1) * HEAD_DIM]
                for h in range(nq)
            ],
            axis=1,
        )

    return (
        relevance,
        whole(0, 0),
        whole(0, 1),
        whole(1, 0),
        whole(1, 1).T,
        refreshed,
    )


def solution(mesh):
    devices = mesh.devices
    owners, columns = devices.shape
    fine = Mesh(devices.reshape(owners // 8, 4, 2, columns // 2, 2), (*IDX, *M))
    return jax.shard_map(
        shards,
        mesh=fine,
        in_specs=(
            P(IDX, None),
            P(IDX, None),
            P(IDX, None),
            P(IDX),
            P(IDX, None),
            P(IDX, M),
            P(None, M),
            P(None, M),
            P(None, M),
            P(M, None),
            P(IDX, M),
            P(IDX, None),
            P(IDX),
        ),
        out_specs=(
            P(IDX, None),
            P(IDX, M),
            P(IDX, M),
            P(IDX, M),
            P(M, IDX),
            P(IDX, None),
        ),
        check_vma=False,
    )
```

```python
import functools

import jax
import jax.numpy as jnp
from jax import lax
from jax.experimental import pallas as pl
from jax.experimental.pallas import tpu as pltpu
from jax.sharding import Mesh
from jax.sharding import PartitionSpec as P

HEAD_DIM = 64
K = 20
PLEN = 4
CAPS = 2
LANES = 128
REACH = 4096
IDX = ("z", "p", "q")
M = ("x", "c")
ALONG = ("z", "p", "q", "c")
F32 = jnp.float32
BF16 = jnp.bfloat16
ROWS = (((0,), (0,)), ((), ()))
COLS = (((1,), (1,)), ((), ()))


def dot(a, b, dims=None):
    if dims is None:
        return jnp.dot(a, b, preferred_element_type=F32)
    return lax.dot_general(a, b, dims, preferred_element_type=F32)


def reader_kernel(heads, half_ref, high_ref, query_ref, *refs):
    token_refs, grad_refs, hbm = refs[:2], refs[2:4], refs[4:8]
    out_ref, rel_ref, vmem, sems = refs[8], refs[9], refs[10:12], refs[12]
    states_ref, wo_ref = vmem
    inner = wo_ref.shape[0]
    targets = [states_ref.at[:, i * inner : (i + 1) * inner] for i in range(3)] + [wo_ref]
    copies = [pltpu.make_async_copy(hbm[i], targets[i], sems.at[i]) for i in range(4)]
    for copy in copies:
        copy.start()
    nc, nx, count, deep = grad_refs[0].shape
    blocks = 2 * nx * nc
    strips, passages = query_ref.shape[:2]
    rows = out_ref.shape[1] // 2
    mine = half_ref[0]

    def grad_block(b):
        x, c = divmod(b, nc)
        return grad_refs[x // nx][c, x % nx]

    def token_block(b, low, high):
        x, c = divmod(b, nc)
        both = [ref[c, x, low:high, :] for ref in token_refs]
        ordered = [jnp.where(mine == 0, both[0], both[1]), jnp.where(mine == 0, both[1], both[0])]
        return jnp.concatenate(ordered, axis=0)

    acc = jnp.zeros((passages, deep), F32)
    for s in range(strips):
        fetched = token_block(s, count // 2, (count + passages) // 2)
        acc += fetched.astype(F32) * query_ref[s].astype(F32)
    low = jnp.sum(acc[:, :LANES], axis=1, keepdims=True)
    high = jnp.sum(acc[:, LANES:], axis=1, keepdims=True)
    scores = jnp.where(high_ref[...] > 0, high, low)
    each, valid = passages // 2, count // 2 // PLEN
    queries = valid // K
    p = lax.broadcasted_iota(jnp.int32, (passages, 2 * queries), 0)
    g = lax.broadcasted_iota(jnp.int32, (passages, 2 * queries), 1)
    first = jnp.where(g >= queries, each + (g - queries) * K, g * K)
    group = (p >= first) & (p < first + K)
    top = jnp.max(jnp.where(group, scores, -jnp.inf), axis=0, keepdims=True)
    exps = jnp.where(group, jnp.exp(scores - top), 0.0)
    rel_column = jnp.sum(exps / jnp.sum(exps, axis=0, keepdims=True), axis=1, keepdims=True)
    same = lax.broadcasted_iota(jnp.int32, (passages, passages), 0) == lax.broadcasted_iota(
        jnp.int32, (passages, passages), 1
    )
    rel_row = jnp.sum(jnp.where(same, rel_column, 0.0), axis=0, keepdims=True)
    rel_ref[...] = rel_row
    token = lax.broadcasted_iota(jnp.int32, (count, passages), 0)
    p = lax.broadcasted_iota(jnp.int32, (count, passages), 1)
    at = jnp.where(p >= each, p - each, p)
    begin = jnp.where(p >= each, count // 2, 0) + at * PLEN
    begin = jnp.where(at < valid, begin, count)
    of_token = (token >= begin) & (token < begin + PLEN)
    rel = jnp.sum(jnp.where(of_token, rel_row, 0.0), axis=1, keepdims=True)

    tokens = [token_block(b, 0, count // 2) for b in range(blocks)]
    weighted = [
        (grad_block(b).astype(F32) * rel).astype(BF16) for b in range(blocks)
    ]
    for copy in copies:
        copy.wait()

    def own(states):
        kept = states[:, :HEAD_DIM]
        for head in range(1, heads):
            kept = jnp.where(mine == head, states[:, head * HEAD_DIM : (head + 1) * HEAD_DIM], kept)
        return kept

    states = dot(tokens[0], states_ref[:deep])
    for b in range(1, blocks):
        states += dot(tokens[b], states_ref[b * deep : (b + 1) * deep])
    states = states.astype(BF16)
    q, k, v = (own(states[:, i * inner : (i + 1) * inner]) for i in range(3))
    total = dot(weighted[0], wo_ref[:, :deep], COLS)
    for b in range(1, blocks):
        total += dot(weighted[b], wo_ref[:, b * deep : (b + 1) * deep], COLS)
    c = own(total.astype(BF16))
    passage_i = lax.broadcasted_iota(jnp.int32, (count, count), 0) // PLEN
    passage_j = lax.broadcasted_iota(jnp.int32, (count, count), 1) // PLEN
    logits = jnp.where(passage_i == passage_j, dot(q, k, COLS), -jnp.inf)
    exps = jnp.exp(logits - jnp.max(logits, axis=1, keepdims=True))
    probs = exps / jnp.sum(exps, axis=1, keepdims=True)
    attn = probs.astype(BF16)
    attn_grad = dot(c, v, COLS)
    mean = jnp.sum(attn_grad * probs, axis=1, keepdims=True)
    score_grad = (probs * (attn_grad - mean)).astype(BF16)
    query_grad = dot(score_grad, k).astype(BF16)
    key_grad = dot(score_grad, q, ROWS).astype(BF16)
    value_grad = dot(attn, c, ROWS).astype(BF16)
    context = dot(attn, v).astype(BF16)
    blank = jnp.zeros_like(context)
    token_side = jnp.concatenate([query_grad, key_grad, value_grad, blank], axis=1)
    weighted_side = jnp.concatenate([blank, context], axis=1)
    span = deep // rows
    for b in range(blocks):
        term = dot(tokens[b], token_side, ROWS)
        upper = term[:, : 2 * HEAD_DIM].astype(BF16)
        lower = (term[:, 2 * HEAD_DIM :] + dot(weighted[b], weighted_side, ROWS)).astype(BF16)
        out_ref[b * span : (b + 1) * span, :rows, :] = upper.reshape(span, rows, -1)
        out_ref[b * span : (b + 1) * span, rows:, :] = lower.reshape(span, rows, -1)


def reader(half, high, query, tokens, out_grad, weights, owners):
    width, inner = weights[0].shape
    passages = query.shape[1]
    vmem = pl.BlockSpec(memory_space=pltpu.VMEM)
    return pl.pallas_call(
        functools.partial(reader_kernel, inner // HEAD_DIM),
        out_shape=(
            jax.ShapeDtypeStruct((owners, 2 * width // owners, 2 * HEAD_DIM), BF16),
            jax.ShapeDtypeStruct((1, passages), F32),
        ),
        in_specs=[pl.BlockSpec(memory_space=pltpu.SMEM)]
        + [vmem] * 6
        + [pl.BlockSpec(memory_space=pl.ANY)] * 4,
        out_specs=(vmem, vmem),
        scratch_shapes=[
            pltpu.VMEM((width, 3 * inner), BF16),
            pltpu.VMEM((inner, width), BF16),
            pltpu.SemaphoreType.DMA((4,)),
        ],
        compiler_params=pltpu.CompilerParams(vmem_limit_bytes=40 * 1024 * 1024),
        name="reader",
    )(half, high, query, *tokens, *out_grad, *weights)


def exact(a, b):
    return dot(a.astype(BF16), b.astype(BF16))


def pack_kernel(
    at_ref, vocab_ref, index_ref, slab_ref, slab_ids_ref, ids_ref, owner_ref, row_ref, out_ref
):
    core, strip = at_ref[0], at_ref[1]
    peers, stride, deep = out_ref.shape
    vocab_rows = vocab_ref.shape[0]
    pass_rows = index_ref.shape[0]
    folded = pass_rows // 2
    asked = vocab_rows + folded
    held = asked + 16
    columns = pl.ds(pl.multiple_of(strip * LANES, LANES), LANES)
    index = index_ref[:, columns]
    slab, plen, npass = slab_ref.shape[0], ids_ref.shape[0], ids_ref.shape[1]

    def places(owner, core):
        z, y = owner // peers, lax.rem(owner, peers)
        return jnp.where(core == 0, z, y), jnp.where(core == 0, y, z)

    def coded(owner, row):
        first, second = places(owner, 1 - core)
        code = second * REACH + first * stride + row
        return (code // LANES).astype(F32), lax.rem(code, LANES).astype(F32)

    ids = ids_ref[...]
    high, low = coded(ids // vocab_rows, lax.rem(ids, vocab_rows))
    lane = lax.broadcasted_iota(jnp.int32, (npass, deep), 1)
    passage = lax.broadcasted_iota(jnp.int32, (npass, deep), 0)
    high_row, low_row = jnp.zeros((1, deep), F32), jnp.zeros((1, deep), F32)
    for i in range(plen):
        to = (lane == passage * plen + i).astype(F32)
        high_row += exact(high[i : i + 1], to)
        low_row += exact(low[i : i + 1], to)
    high, low = coded(owner_ref[...], vocab_rows + lax.rem(row_ref[...], folded))
    to = (lane == passage + plen * npass).astype(F32)
    high_row += exact(high, to)
    low_row += exact(low, to)
    lane = lax.broadcasted_iota(jnp.int32, (1, deep), 1)
    none = peers * REACH - 1
    high_row = jnp.where(lane < (plen + 1) * npass, high_row, float(none // LANES))
    low_row = jnp.where(lane < (plen + 1) * npass, low_row, float(none % LANES))
    line = lax.broadcasted_iota(jnp.int32, (16, deep), 0)
    wanted = jnp.where(line == 0, high_row, jnp.where(line == 1, low_row, 0.0)).astype(BF16)

    slab_ids = slab_ids_ref[...]
    owner, row = slab_ids // pass_rows, lax.rem(slab_ids, pass_rows)
    i = lax.broadcasted_iota(jnp.int32, (slab, slab), 0)
    j = lax.broadcasted_iota(jnp.int32, (slab, slab), 1)
    owner_column = jnp.sum(jnp.where(i == j, owner.astype(F32), 0.0), axis=1, keepdims=True)
    place_column = jnp.sum(jnp.where(i == j, (row + 1).astype(F32), 0.0), axis=1, keepdims=True)
    before = jnp.where((owner_column == owner.astype(F32)) & (i < j), 1.0, 0.0)
    first, second = places(owner, core)
    slot = ((first * peers + second) * CAPS).astype(F32) + jnp.sum(before, axis=0, keepdims=True)
    slots = lax.broadcasted_iota(jnp.int32, (peers * peers * CAPS, slab), 0).astype(F32)
    select = jnp.where(slots == slot, 1.0, 0.0).astype(BF16)
    place = jnp.broadcast_to(place_column, (slab, deep - LANES)).astype(BF16)
    slab_out = dot(select, jnp.concatenate([slab_ref[:, columns], place], axis=1)).astype(BF16)

    index = jnp.concatenate([index[:folded], index[folded:]], axis=1)
    for peer in range(peers):
        out_ref[peer, :vocab_rows, :] = vocab_ref[...]
        out_ref[peer, vocab_rows:asked, :] = index
        out_ref[peer, asked:held, :] = wanted
        out_ref[peer, held:, :] = slab_out[peer * peers * CAPS : (peer + 1) * peers * CAPS]


def pack(core, strip, vocab, index, slab, slab_ids, ids, owner, row, peers):
    vmem = pl.BlockSpec(memory_space=pltpu.VMEM)
    rows = vocab.shape[0] + index.shape[0] // 2 + 16 + peers * CAPS
    return pl.pallas_call(
        pack_kernel,
        out_shape=jax.ShapeDtypeStruct((peers, rows, vocab.shape[1]), BF16),
        in_specs=[pl.BlockSpec(memory_space=pltpu.SMEM)] + [vmem] * 7,
        out_specs=vmem,
        compiler_params=pltpu.CompilerParams(vmem_limit_bytes=32 * 1024 * 1024),
        name="pack",
    )(jnp.stack([core, strip]), vocab, index, slab, slab_ids, ids, owner, row)


def total_kernel(terms_ref, *out_refs):
    rows = terms_ref.shape[1] // 2
    sums = []
    for half in range(2):
        acc = terms_ref[half].astype(F32)
        for i in range(2 + half, terms_ref.shape[0], 2):
            acc += terms_ref[i].astype(F32)
        sums.append(acc)
    for i, out_ref in enumerate(out_refs):
        top, left = divmod(i, 2)
        out_ref[...] = jnp.concatenate(
            [
                acc[top * rows : (top + 1) * rows, left * HEAD_DIM : (left + 1) * HEAD_DIM]
                for acc in sums
            ],
            axis=1,
        )


def total(terms):
    rows, width = terms.shape[1] // 2, terms.shape[2]
    vmem = pl.BlockSpec(memory_space=pltpu.VMEM)
    return pl.pallas_call(
        total_kernel,
        out_shape=(jax.ShapeDtypeStruct((rows, width), F32),) * 4,
        in_specs=[vmem],
        out_specs=(vmem,) * 4,
        compiler_params=pltpu.CompilerParams(vmem_limit_bytes=32 * 1024 * 1024),
        name="total",
    )(terms)


def shards(
    index_emb,
    query_emb,
    passage_owner,
    passage_row,
    token_ids,
    vocab_table,
    w_query,
    w_key,
    w_value,
    w_out,
    out_grad,
    slab_emb,
    slab_ids,
):
    nz, nq = lax.axis_size("z"), lax.axis_size("q")
    ny = lax.axis_size("p") * nq
    owners = nz * ny
    swap = [(0, 1), (1, 0)]
    my_z = lax.axis_index("z")
    my_y = lax.axis_index(("p", "q"))
    my_half = lax.axis_index("q")
    pass_rows, width = index_emb.shape
    queries = query_emb.shape[0]
    npass, plen = token_ids.shape
    count = npass * plen
    vocab_rows = vocab_table.shape[0]
    strips = width // LANES
    strip = lax.rem(lax.axis_index(M), strips)

    def my_strip(array):
        return lax.dynamic_slice_in_dim(array, strip * LANES, LANES, axis=1)

    cores = lax.axis_size("c")
    my_core = lax.axis_index("c")
    at_z = [[(z * ny + y) * cores for z in range(nz)] for y in range(ny)]
    at_y = [[(z * ny + y) * cores for y in range(ny)] for z in range(nz)]
    first_groups = at_z + [[i + 1 for i in group] for group in at_y]
    second_groups = at_y + [[i + 1 for i in group] for group in at_z]
    second = jnp.where(my_core == 0, my_y, my_z)

    deep = vocab_table.shape[1]
    index_strip = my_strip(index_emb)
    folded = pass_rows // 2
    asked = vocab_rows + folded
    held = asked + 16
    stride = held + ny * CAPS
    spare = -npass % 16
    rows_here = count + npass + spare
    message = pack(
        my_core,
        strip,
        vocab_table,
        index_emb,
        slab_emb,
        slab_ids[None],
        token_ids.T,
        passage_owner.T,
        passage_row[None],
        nz,
    )
    got_first = lax.all_to_all(
        message,
        ALONG,
        0,
        0,
        axis_index_groups=first_groups,
        tiled=True,
    )
    query_strips = query_emb.reshape(queries, strips, LANES).transpose(1, 0, 2)
    extra = jnp.concatenate(
        [
            query_strips.reshape(strips, queries * LANES),
            jnp.pad(passage_row.astype(BF16)[None], ((0, 0), (0, deep - npass))),
        ],
        axis=0,
    )
    extra = jnp.pad(extra, ((0, -extra.shape[0] % 8), (0, 0)))
    other = lax.ppermute(jnp.concatenate([out_grad, extra], axis=0), "q", swap)
    got_first, other = lax.optimization_barrier((got_first, other))
    along_x = lax.all_gather(jnp.concatenate([out_grad, other[:count]], axis=0), "x", axis=0)
    other_strips = other[count : count + strips].reshape(strips, queries, LANES)
    def per_passage(some):
        some = jnp.repeat(jnp.concatenate([some, some], axis=2), K, axis=1)
        return jnp.pad(some, ((0, 0), (0, spare), (0, 0)))

    pair_query = jnp.concatenate([per_passage(query_strips), per_passage(other_strips)], axis=1)
    other_row = other[count + strips, :npass].astype(jnp.int32)
    high = jnp.concatenate([jnp.pad(passage_row, (0, spare)), jnp.pad(other_row, (0, spare))])
    high = (high[:, None] >= folded).astype(jnp.int32)

    wanted = lax.ppermute(got_first[:, asked : asked + 2], "c", [(0, 1), (1, 0)])
    wanted = wanted.astype(jnp.int32)[:, :, :rows_here]
    rows_at = wanted[:, 0] * LANES + wanted[:, 1] - second * REACH
    slab_at = (
        held
        + jnp.arange(ny)[:, None, None] * CAPS
        + jnp.arange(nz)[None, :, None] * stride
        + jnp.arange(CAPS)[None, None, :]
    ).reshape(ny, nz * CAPS)
    at = jnp.concatenate([rows_at, slab_at], axis=1)
    one_hot = (at.reshape(-1)[:, None] == jnp.arange(nz * stride)[None, :]).astype(BF16)
    served = dot(one_hot, got_first.reshape(nz * stride, deep)).astype(BF16)
    got_second = lax.all_to_all(
        served.reshape(*at.shape, deep),
        ALONG,
        0,
        0,
        axis_index_groups=second_groups,
        tiled=True,
    )
    got_second, along_x = lax.optimization_barrier((got_second, along_x))
    part = jnp.sum(got_second[:, :rows_here].astype(F32), axis=0).astype(BF16)

    nx = lax.axis_size("x")
    grads = [
        lax.all_gather(along_x[i * nx // 2 : (i + 1) * nx // 2], "c", axis=0) for i in range(2)
    ]
    near = lax.all_to_all(
        jnp.broadcast_to(part[None], (nq * nx, *part.shape)), ("q", "x"), 0, 0, tiled=True
    )
    near, grads = lax.optimization_barrier((near, grads))
    tokens = [lax.all_gather(near[i * nx : (i + 1) * nx], "c", axis=0) for i in range(nq)]

    got_slab = got_second[:, rows_here:].reshape(-1, deep)
    got_place = got_slab[:, LANES].astype(jnp.int32) - 1
    put = jnp.arange(pass_rows)[:, None] == got_place[None, :]
    placed = dot(put.astype(BF16), got_slab[:, :LANES]).astype(BF16)
    refreshed = jnp.where(jnp.any(put, axis=1)[:, None], placed, index_strip)

    terms, pair_relevance = reader(
        my_half.reshape(1), high, pair_query, tokens, grads, (w_query, w_key, w_value, w_out), owners
    )
    relevance = pair_relevance[0, :npass].reshape(queries, K)
    refreshed, terms = lax.optimization_barrier((refreshed, terms))
    refreshed = lax.all_gather(refreshed, M, axis=0)
    refreshed = jnp.concatenate([refreshed[i] for i in range(strips)], axis=1)
    terms = lax.all_to_all(terms, IDX, 0, 0, tiled=True)
    grad_query, grad_key, grad_value, grad_out = total(terms)
    return (relevance, grad_query, grad_key, grad_value, grad_out.T, refreshed)


def solution(mesh):
    devices = mesh.devices
    owners, columns = devices.shape
    fine = Mesh(devices.reshape(owners // 8, 4, 2, columns // 2, 2), (*IDX, *M))
    return jax.shard_map(
        shards,
        mesh=fine,
        in_specs=(
            P(IDX, None),
            P(IDX, None),
            P(IDX, None),
            P(IDX),
            P(IDX, None),
            P(IDX, M),
            P(None, M),
            P(None, M),
            P(None, M),
            P(M, None),
            P(IDX, M),
            P(IDX, None),
            P(IDX),
        ),
        out_specs=(
            P(IDX, None),
            P(IDX, M),
            P(IDX, M),
            P(IDX, M),
            P(M, IDX),
            P(IDX, None),
        ),
        check_vma=False,
    )
```

```python
import functools

import jax
import jax.numpy as jnp
from jax import lax
from jax.experimental import pallas as pl
from jax.experimental.pallas import tpu as pltpu
from jax.sharding import Mesh
from jax.sharding import PartitionSpec as P

HEAD_DIM = 64
K = 20
PLEN = 4
CAPS = 2
LANES = 128
REACH = 4096
IDX = ("z", "p", "q")
M = ("x", "c")
ALONG = ("z", "p", "q", "c")
F32 = jnp.float32
BF16 = jnp.bfloat16
ROWS = (((0,), (0,)), ((), ()))
COLS = (((1,), (1,)), ((), ()))


def dot(a, b, dims=None):
    if dims is None:
        return jnp.dot(a, b, preferred_element_type=F32)
    return lax.dot_general(a, b, dims, preferred_element_type=F32)


def reader_kernel(heads, half_ref, high_ref, query_ref, *refs):
    token_refs, grad_refs, weight_refs, wo_ref = refs[:2], refs[2:4], refs[4:7], refs[7]
    out_ref, rel_ref = refs[8:]
    nc, nx, count, deep = grad_refs[0].shape
    blocks = 2 * nx * nc
    strips, passages = query_ref.shape[:2]
    rows = out_ref.shape[1] // 2
    mine = half_ref[0]

    def grad_block(b):
        x, c = divmod(b, nc)
        return grad_refs[x // nx][c, x % nx]

    def token_block(b, low, high):
        x, c = divmod(b, nc)
        both = [ref[c, x, low:high, :] for ref in token_refs]
        ordered = [jnp.where(mine == 0, both[0], both[1]), jnp.where(mine == 0, both[1], both[0])]
        return jnp.concatenate(ordered, axis=0)

    acc = jnp.zeros((passages, deep), F32)
    for s in range(strips):
        fetched = token_block(s, count // 2, (count + passages) // 2)
        acc += fetched.astype(F32) * query_ref[s].astype(F32)
    low = jnp.sum(acc[:, :LANES], axis=1, keepdims=True)
    high = jnp.sum(acc[:, LANES:], axis=1, keepdims=True)
    scores = jnp.where(high_ref[...] > 0, high, low)
    each, valid = passages // 2, count // 2 // PLEN
    queries = valid // K
    p = lax.broadcasted_iota(jnp.int32, (passages, 2 * queries), 0)
    g = lax.broadcasted_iota(jnp.int32, (passages, 2 * queries), 1)
    first = jnp.where(g >= queries, each + (g - queries) * K, g * K)
    group = (p >= first) & (p < first + K)
    top = jnp.max(jnp.where(group, scores, -jnp.inf), axis=0, keepdims=True)
    exps = jnp.where(group, jnp.exp(scores - top), 0.0)
    rel_column = jnp.sum(exps / jnp.sum(exps, axis=0, keepdims=True), axis=1, keepdims=True)
    same = lax.broadcasted_iota(jnp.int32, (passages, passages), 0) == lax.broadcasted_iota(
        jnp.int32, (passages, passages), 1
    )
    rel_row = jnp.sum(jnp.where(same, rel_column, 0.0), axis=0, keepdims=True)
    rel_ref[...] = rel_row
    token = lax.broadcasted_iota(jnp.int32, (count, passages), 0)
    p = lax.broadcasted_iota(jnp.int32, (count, passages), 1)
    at = jnp.where(p >= each, p - each, p)
    begin = jnp.where(p >= each, count // 2, 0) + at * PLEN
    begin = jnp.where(at < valid, begin, count)
    of_token = (token >= begin) & (token < begin + PLEN)
    rel = jnp.sum(jnp.where(of_token, rel_row, 0.0), axis=1, keepdims=True)

    tokens = [token_block(b, 0, count // 2) for b in range(blocks)]
    weighted = [
        (grad_block(b).astype(F32) * rel).astype(BF16) for b in range(blocks)
    ]
    def own(states):
        kept = states[:, :HEAD_DIM]
        for head in range(1, heads):
            kept = jnp.where(mine == head, states[:, head * HEAD_DIM : (head + 1) * HEAD_DIM], kept)
        return kept

    def projected(weight_ref):
        states = dot(tokens[0], weight_ref[:deep])
        for b in range(1, blocks):
            states += dot(tokens[b], weight_ref[b * deep : (b + 1) * deep])
        return own(states.astype(BF16))

    q, k, v = (projected(weight_ref) for weight_ref in weight_refs)
    total = dot(weighted[0], wo_ref[:, :deep], COLS)
    for b in range(1, blocks):
        total += dot(weighted[b], wo_ref[:, b * deep : (b + 1) * deep], COLS)
    c = own(total.astype(BF16))
    passage_i = lax.broadcasted_iota(jnp.int32, (count, count), 0) // PLEN
    passage_j = lax.broadcasted_iota(jnp.int32, (count, count), 1) // PLEN
    logits = jnp.where(passage_i == passage_j, dot(q, k, COLS), -jnp.inf)
    exps = jnp.exp(logits - jnp.max(logits, axis=1, keepdims=True))
    probs = exps / jnp.sum(exps, axis=1, keepdims=True)
    attn = probs.astype(BF16)
    attn_grad = dot(c, v, COLS)
    mean = jnp.sum(attn_grad * probs, axis=1, keepdims=True)
    score_grad = (probs * (attn_grad - mean)).astype(BF16)
    query_grad = dot(score_grad, k).astype(BF16)
    key_grad = dot(score_grad, q, ROWS).astype(BF16)
    value_grad = dot(attn, c, ROWS).astype(BF16)
    context = dot(attn, v).astype(BF16)
    blank = jnp.zeros_like(context)
    token_side = jnp.concatenate([query_grad, key_grad, value_grad, blank], axis=1)
    weighted_side = jnp.concatenate([blank, context], axis=1)
    span = deep // rows
    for b in range(blocks):
        term = dot(tokens[b], token_side, ROWS)
        upper = term[:, : 2 * HEAD_DIM].astype(BF16)
        lower = (term[:, 2 * HEAD_DIM :] + dot(weighted[b], weighted_side, ROWS)).astype(BF16)
        out_ref[b * span : (b + 1) * span, :rows, :] = upper.reshape(span, rows, -1)
        out_ref[b * span : (b + 1) * span, rows:, :] = lower.reshape(span, rows, -1)


def reader(half, high, query, tokens, out_grad, weights, owners):
    width, inner = weights[0].shape
    passages = query.shape[1]
    vmem = pl.BlockSpec(memory_space=pltpu.VMEM)
    return pl.pallas_call(
        functools.partial(reader_kernel, inner // HEAD_DIM),
        out_shape=(
            jax.ShapeDtypeStruct((owners, 2 * width // owners, 2 * HEAD_DIM), BF16),
            jax.ShapeDtypeStruct((1, passages), F32),
        ),
        in_specs=[pl.BlockSpec(memory_space=pltpu.SMEM)]
        + [vmem] * 10,
        out_specs=(vmem, vmem),
        compiler_params=pltpu.CompilerParams(vmem_limit_bytes=40 * 1024 * 1024),
        name="reader",
    )(half, high, query, *tokens, *out_grad, *weights)


def exact(a, b):
    return dot(a.astype(BF16), b.astype(BF16))


def pack_kernel(at_ref, *refs):
    hbm, out_ref, vmem, sems = refs[:7], refs[7], refs[8:15], refs[15]
    copies = [pltpu.make_async_copy(hbm[i], vmem[i], sems.at[i]) for i in range(7)]
    for copy in copies:
        copy.start()
    vocab_ref, index_ref, slab_ref, slab_ids_ref, ids_ref, owner_ref, row_ref = vmem
    core, strip = at_ref[0], at_ref[1]
    for copy in copies:
        copy.wait()
    peers, stride, deep = out_ref.shape
    vocab_rows = vocab_ref.shape[0]
    pass_rows = index_ref.shape[0]
    folded = pass_rows // 2
    asked = vocab_rows + folded
    held = asked + 16
    columns = pl.ds(pl.multiple_of(strip * LANES, LANES), LANES)
    index = index_ref[:, columns]
    slab, plen, npass = slab_ref.shape[0], ids_ref.shape[0], ids_ref.shape[1]

    def places(owner, core):
        z, y = owner // peers, lax.rem(owner, peers)
        return jnp.where(core == 0, z, y), jnp.where(core == 0, y, z)

    def coded(owner, row):
        first, second = places(owner, 1 - core)
        code = second * REACH + first * stride + row
        return (code // LANES).astype(F32), lax.rem(code, LANES).astype(F32)

    ids = ids_ref[...]
    high, low = coded(ids // vocab_rows, lax.rem(ids, vocab_rows))
    lane = lax.broadcasted_iota(jnp.int32, (npass, deep), 1)
    passage = lax.broadcasted_iota(jnp.int32, (npass, deep), 0)
    high_row, low_row = jnp.zeros((1, deep), F32), jnp.zeros((1, deep), F32)
    for i in range(plen):
        to = (lane == passage * plen + i).astype(F32)
        high_row += exact(high[i : i + 1], to)
        low_row += exact(low[i : i + 1], to)
    high, low = coded(owner_ref[...], vocab_rows + lax.rem(row_ref[...], folded))
    to = (lane == passage + plen * npass).astype(F32)
    high_row += exact(high, to)
    low_row += exact(low, to)
    lane = lax.broadcasted_iota(jnp.int32, (1, deep), 1)
    none = peers * REACH - 1
    high_row = jnp.where(lane < (plen + 1) * npass, high_row, float(none // LANES))
    low_row = jnp.where(lane < (plen + 1) * npass, low_row, float(none % LANES))
    line = lax.broadcasted_iota(jnp.int32, (16, deep), 0)
    wanted = jnp.where(line == 0, high_row, jnp.where(line == 1, low_row, 0.0)).astype(BF16)

    slab_ids = slab_ids_ref[...]
    owner, row = slab_ids // pass_rows, lax.rem(slab_ids, pass_rows)
    i = lax.broadcasted_iota(jnp.int32, (slab, slab), 0)
    j = lax.broadcasted_iota(jnp.int32, (slab, slab), 1)
    owner_column = jnp.sum(jnp.where(i == j, owner.astype(F32), 0.0), axis=1, keepdims=True)
    place_column = jnp.sum(jnp.where(i == j, (row + 1).astype(F32), 0.0), axis=1, keepdims=True)
    before = jnp.where((owner_column == owner.astype(F32)) & (i < j), 1.0, 0.0)
    first, second = places(owner, core)
    slot = ((first * peers + second) * CAPS).astype(F32) + jnp.sum(before, axis=0, keepdims=True)
    slots = lax.broadcasted_iota(jnp.int32, (peers * peers * CAPS, slab), 0).astype(F32)
    select = jnp.where(slots == slot, 1.0, 0.0).astype(BF16)
    place = jnp.broadcast_to(place_column, (slab, deep - LANES)).astype(BF16)
    slab_out = dot(select, jnp.concatenate([slab_ref[:, columns], place], axis=1)).astype(BF16)

    index = jnp.concatenate([index[:folded], index[folded:]], axis=1)
    for peer in range(peers):
        out_ref[peer, :vocab_rows, :] = vocab_ref[...]
        out_ref[peer, vocab_rows:asked, :] = index
        out_ref[peer, asked:held, :] = wanted
        out_ref[peer, held:, :] = slab_out[peer * peers * CAPS : (peer + 1) * peers * CAPS]


def pack(core, strip, vocab, index, slab, slab_ids, ids, owner, row, peers):
    operands = (vocab, index, slab, slab_ids, ids, owner, row)
    rows = vocab.shape[0] + index.shape[0] // 2 + 16 + peers * CAPS
    return pl.pallas_call(
        pack_kernel,
        out_shape=jax.ShapeDtypeStruct((peers, rows, vocab.shape[1]), BF16),
        in_specs=[pl.BlockSpec(memory_space=pltpu.SMEM)]
        + [pl.BlockSpec(memory_space=pltpu.HBM)] * 7,
        out_specs=pl.BlockSpec(memory_space=pltpu.VMEM),
        scratch_shapes=[pltpu.VMEM(operand.shape, operand.dtype) for operand in operands]
        + [pltpu.SemaphoreType.DMA((7,))],
        compiler_params=pltpu.CompilerParams(vmem_limit_bytes=60 * 1024 * 1024),
        name="pack",
    )(jnp.stack([core, strip]), *operands)


def total_kernel(terms_ref, *out_refs):
    rows = terms_ref.shape[1] // 2
    sums = []
    for half in range(2):
        acc = terms_ref[half].astype(F32)
        for i in range(2 + half, terms_ref.shape[0], 2):
            acc += terms_ref[i].astype(F32)
        sums.append(acc)
    for i, out_ref in enumerate(out_refs):
        top, left = divmod(i, 2)
        out_ref[...] = jnp.concatenate(
            [
                acc[top * rows : (top + 1) * rows, left * HEAD_DIM : (left + 1) * HEAD_DIM]
                for acc in sums
            ],
            axis=1,
        )


def total(terms):
    rows, width = terms.shape[1] // 2, terms.shape[2]
    vmem = pl.BlockSpec(memory_space=pltpu.VMEM)
    return pl.pallas_call(
        total_kernel,
        out_shape=(jax.ShapeDtypeStruct((rows, width), F32),) * 4,
        in_specs=[vmem],
        out_specs=(vmem,) * 4,
        compiler_params=pltpu.CompilerParams(vmem_limit_bytes=32 * 1024 * 1024),
        name="total",
    )(terms)


def shards(
    index_emb,
    query_emb,
    passage_owner,
    passage_row,
    token_ids,
    vocab_table,
    w_query,
    w_key,
    w_value,
    w_out,
    out_grad,
    slab_emb,
    slab_ids,
):
    nz, nq = lax.axis_size("z"), lax.axis_size("q")
    ny = lax.axis_size("p") * nq
    owners = nz * ny
    swap = [(0, 1), (1, 0)]
    my_z = lax.axis_index("z")
    my_y = lax.axis_index(("p", "q"))
    my_half = lax.axis_index("q")
    pass_rows, width = index_emb.shape
    queries = query_emb.shape[0]
    npass, plen = token_ids.shape
    count = npass * plen
    vocab_rows = vocab_table.shape[0]
    strips = width // LANES
    strip = lax.rem(lax.axis_index(M), strips)

    def my_strip(array):
        return lax.dynamic_slice_in_dim(array, strip * LANES, LANES, axis=1)

    cores = lax.axis_size("c")
    my_core = lax.axis_index("c")
    at_z = [[(z * ny + y) * cores for z in range(nz)] for y in range(ny)]
    at_y = [[(z * ny + y) * cores for y in range(ny)] for z in range(nz)]
    first_groups = at_z + [[i + 1 for i in group] for group in at_y]
    second_groups = at_y + [[i + 1 for i in group] for group in at_z]
    second = jnp.where(my_core == 0, my_y, my_z)

    deep = vocab_table.shape[1]
    index_strip = my_strip(index_emb)
    folded = pass_rows // 2
    asked = vocab_rows + folded
    held = asked + 16
    stride = held + ny * CAPS
    spare = -npass % 16
    rows_here = count + npass + spare
    message = pack(
        my_core,
        strip,
        vocab_table,
        index_emb,
        slab_emb,
        slab_ids[None],
        token_ids.T,
        passage_owner.T,
        passage_row[None],
        nz,
    )
    got_first = lax.all_to_all(
        message,
        ALONG,
        0,
        0,
        axis_index_groups=first_groups,
        tiled=True,
    )
    query_strips = query_emb.reshape(queries, strips, LANES).transpose(1, 0, 2)
    extra = jnp.concatenate(
        [
            query_strips.reshape(strips, queries * LANES),
            jnp.pad(passage_row.astype(BF16)[None], ((0, 0), (0, deep - npass))),
        ],
        axis=0,
    )
    extra = jnp.pad(extra, ((0, -extra.shape[0] % 8), (0, 0)))
    other = lax.ppermute(jnp.concatenate([out_grad, extra], axis=0), "q", swap)
    got_first, other = lax.optimization_barrier((got_first, other))
    along_x = lax.all_gather(jnp.concatenate([out_grad, other[:count]], axis=0), "x", axis=0)
    other_strips = other[count : count + strips].reshape(strips, queries, LANES)
    def per_passage(some):
        some = jnp.repeat(jnp.concatenate([some, some], axis=2), K, axis=1)
        return jnp.pad(some, ((0, 0), (0, spare), (0, 0)))

    pair_query = jnp.concatenate([per_passage(query_strips), per_passage(other_strips)], axis=1)
    other_row = other[count + strips, :npass].astype(jnp.int32)
    high = jnp.concatenate([jnp.pad(passage_row, (0, spare)), jnp.pad(other_row, (0, spare))])
    high = (high[:, None] >= folded).astype(jnp.int32)

    wanted = lax.ppermute(got_first[:, asked : asked + 2], "c", [(0, 1), (1, 0)])
    wanted = wanted.astype(jnp.int32)[:, :, :rows_here]
    rows_at = wanted[:, 0] * LANES + wanted[:, 1] - second * REACH
    slab_at = (
        held
        + jnp.arange(ny)[:, None, None] * CAPS
        + jnp.arange(nz)[None, :, None] * stride
        + jnp.arange(CAPS)[None, None, :]
    ).reshape(ny, nz * CAPS)
    at = jnp.concatenate([rows_at, slab_at], axis=1)
    one_hot = (at.reshape(-1)[:, None] == jnp.arange(nz * stride)[None, :]).astype(BF16)
    served = dot(one_hot, got_first.reshape(nz * stride, deep)).astype(BF16)
    got_second = lax.all_to_all(
        served.reshape(*at.shape, deep),
        ALONG,
        0,
        0,
        axis_index_groups=second_groups,
        tiled=True,
    )
    got_second, along_x = lax.optimization_barrier((got_second, along_x))
    part = jnp.sum(got_second[:, :rows_here].astype(F32), axis=0).astype(BF16)

    nx = lax.axis_size("x")
    grads = [
        lax.all_gather(along_x[i * nx // 2 : (i + 1) * nx // 2], "c", axis=0) for i in range(2)
    ]
    near = lax.all_to_all(
        jnp.broadcast_to(part[None], (nq * nx, *part.shape)), ("q", "x"), 0, 0, tiled=True
    )
    near, grads = lax.optimization_barrier((near, grads))
    tokens = [lax.all_gather(near[i * nx : (i + 1) * nx], "c", axis=0) for i in range(nq)]

    got_slab = got_second[:, rows_here:].reshape(-1, deep)
    got_place = got_slab[:, LANES].astype(jnp.int32) - 1
    put = jnp.arange(pass_rows)[:, None] == got_place[None, :]
    placed = dot(put.astype(BF16), got_slab[:, :LANES]).astype(BF16)
    refreshed = jnp.where(jnp.any(put, axis=1)[:, None], placed, index_strip)

    terms, pair_relevance = reader(
        my_half.reshape(1), high, pair_query, tokens, grads, (w_query, w_key, w_value, w_out), owners
    )
    relevance = pair_relevance[0, :npass].reshape(queries, K)
    refreshed, terms = lax.optimization_barrier((refreshed, terms))
    refreshed = lax.all_gather(refreshed, M, axis=0)
    refreshed = jnp.concatenate([refreshed[i] for i in range(strips)], axis=1)
    terms = lax.all_to_all(terms, IDX, 0, 0, tiled=True)
    grad_query, grad_key, grad_value, grad_out = total(terms)
    return (relevance, grad_query, grad_key, grad_value, grad_out.T, refreshed)


def solution(mesh):
    devices = mesh.devices
    owners, columns = devices.shape
    fine = Mesh(devices.reshape(owners // 8, 4, 2, columns // 2, 2), (*IDX, *M))
    return jax.shard_map(
        shards,
        mesh=fine,
        in_specs=(
            P(IDX, None),
            P(IDX, None),
            P(IDX, None),
            P(IDX),
            P(IDX, None),
            P(IDX, M),
            P(None, M),
            P(None, M),
            P(None, M),
            P(M, None),
            P(IDX, M),
            P(IDX, None),
            P(IDX),
        ),
        out_specs=(
            P(IDX, None),
            P(IDX, M),
            P(IDX, M),
            P(IDX, M),
            P(M, IDX),
            P(IDX, None),
        ),
        check_vma=False,
    )
```

```python
import functools

import jax
import jax.numpy as jnp
from jax import lax
from jax.experimental import pallas as pl
from jax.experimental.pallas import tpu as pltpu
from jax.sharding import Mesh
from jax.sharding import PartitionSpec as P

HEAD_DIM = 64
K = 20
PLEN = 4
CAPS = 2
LANES = 128
REACH = 4096
IDX = ("z", "p", "q")
M = ("x", "c")
ALONG = ("z", "p", "q", "c")
F32 = jnp.float32
BF16 = jnp.bfloat16
ROWS = (((0,), (0,)), ((), ()))
COLS = (((1,), (1,)), ((), ()))


def dot(a, b, dims=None):
    if dims is None:
        return jnp.dot(a, b, preferred_element_type=F32)
    return lax.dot_general(a, b, dims, preferred_element_type=F32)


def reader_kernel(heads, strips, half_ref, *refs):
    token_refs, grad_refs, weight_refs, wo_ref = refs[:2], refs[2:4], refs[4:7], refs[7]
    out_ref, rel_ref = refs[8:]
    nc, nx, count, deep = grad_refs[0].shape
    blocks = 2 * nx * nc
    rows = out_ref.shape[1] // 2
    mine = half_ref[0]

    def grad_block(b):
        x, c = divmod(b, nc)
        return grad_refs[x // nx][c, x % nx]

    def token_block(b, low, high):
        x, c = divmod(b, nc)
        both = [ref[c, x, low:high, :] for ref in token_refs]
        ordered = [jnp.where(mine == 0, both[0], both[1]), jnp.where(mine == 0, both[1], both[0])]
        return jnp.concatenate(ordered, axis=0)

    valid = count // 2 // PLEN
    sums = []
    for ref in token_refs:
        acc = jnp.zeros((16, LANES), F32)
        for b in range(strips):
            x, c = divmod(b, nc)
            acc += ref[c, x, count // 2 :, :LANES].astype(F32)
        sums.append(jnp.sum(acc, axis=0, keepdims=True))
    lane = lax.broadcasted_iota(jnp.int32, (1, LANES), 1)
    token = lax.broadcasted_iota(jnp.int32, (count // 2, LANES), 0)
    begin = lax.broadcasted_iota(jnp.int32, (count // 2, LANES), 1) * PLEN
    of_token = (token >= begin) & (token < begin + PLEN)
    rel = []
    for scores in (
        jnp.where(mine == 0, sums[0], sums[1]),
        jnp.where(mine == 0, sums[1], sums[0]),
    ):
        share = jnp.zeros((1, LANES), F32)
        for first in range(0, valid, K):
            group = (lane >= first) & (lane < first + K)
            top = jnp.max(jnp.where(group, scores, -jnp.inf), axis=1, keepdims=True)
            exps = jnp.where(group, jnp.exp(scores - top), 0.0)
            share += exps / jnp.sum(exps, axis=1, keepdims=True)
        if not rel:
            rel_ref[...] = share
        rel.append(jnp.sum(jnp.where(of_token, share, 0.0), axis=1, keepdims=True))
    rel = jnp.concatenate(rel, axis=0)

    tokens = [token_block(b, 0, count // 2) for b in range(blocks)]
    weighted = [
        (grad_block(b).astype(F32) * rel).astype(BF16) for b in range(blocks)
    ]
    def own(states):
        kept = states[:, :HEAD_DIM]
        for head in range(1, heads):
            kept = jnp.where(mine == head, states[:, head * HEAD_DIM : (head + 1) * HEAD_DIM], kept)
        return kept

    def projected(weight_ref):
        states = dot(tokens[0], weight_ref[:deep])
        for b in range(1, blocks):
            states += dot(tokens[b], weight_ref[b * deep : (b + 1) * deep])
        return own(states.astype(BF16))

    q, k, v = (projected(weight_ref) for weight_ref in weight_refs)
    total = dot(weighted[0], wo_ref[:, :deep], COLS)
    for b in range(1, blocks):
        total += dot(weighted[b], wo_ref[:, b * deep : (b + 1) * deep], COLS)
    c = own(total.astype(BF16))
    passage_i = lax.broadcasted_iota(jnp.int32, (count, count), 0) // PLEN
    passage_j = lax.broadcasted_iota(jnp.int32, (count, count), 1) // PLEN
    logits = jnp.where(passage_i == passage_j, dot(q, k, COLS), -jnp.inf)
    exps = jnp.exp(logits - jnp.max(logits, axis=1, keepdims=True))
    probs = exps / jnp.sum(exps, axis=1, keepdims=True)
    attn = probs.astype(BF16)
    attn_grad = dot(c, v, COLS)
    mean = jnp.sum(attn_grad * probs, axis=1, keepdims=True)
    score_grad = (probs * (attn_grad - mean)).astype(BF16)
    query_grad = dot(score_grad, k).astype(BF16)
    key_grad = dot(score_grad, q, ROWS).astype(BF16)
    value_grad = dot(attn, c, ROWS).astype(BF16)
    context = dot(attn, v).astype(BF16)
    blank = jnp.zeros_like(context)
    token_side = jnp.concatenate([query_grad, key_grad, value_grad, blank], axis=1)
    weighted_side = jnp.concatenate([blank, context], axis=1)
    span = deep // rows
    for b in range(blocks):
        term = dot(tokens[b], token_side, ROWS)
        upper = term[:, : 2 * HEAD_DIM].astype(BF16)
        lower = (term[:, 2 * HEAD_DIM :] + dot(weighted[b], weighted_side, ROWS)).astype(BF16)
        out_ref[b * span : (b + 1) * span, :rows, :] = upper.reshape(span, rows, -1)
        out_ref[b * span : (b + 1) * span, rows:, :] = lower.reshape(span, rows, -1)


def reader(half, tokens, out_grad, weights, strips, owners):
    width, inner = weights[0].shape
    vmem = pl.BlockSpec(memory_space=pltpu.VMEM)
    return pl.pallas_call(
        functools.partial(reader_kernel, inner // HEAD_DIM, strips),
        out_shape=(
            jax.ShapeDtypeStruct((owners, 2 * width // owners, 2 * HEAD_DIM), BF16),
            jax.ShapeDtypeStruct((1, LANES), F32),
        ),
        in_specs=[pl.BlockSpec(memory_space=pltpu.SMEM)]
        + [vmem] * 8,
        out_specs=(vmem, vmem),
        compiler_params=pltpu.CompilerParams(vmem_limit_bytes=40 * 1024 * 1024),
        name="reader",
    )(half, *tokens, *out_grad, *weights)


def exact(a, b):
    return dot(a.astype(BF16), b.astype(BF16))


def pack_kernel(at_ref, *refs):
    hbm, out_ref, vmem, sems = refs[:7], refs[7], refs[8:15], refs[15]
    copies = [pltpu.make_async_copy(hbm[i], vmem[i], sems.at[i]) for i in range(7)]
    for copy in copies:
        copy.start()
    vocab_ref, index_ref, slab_ref, slab_ids_ref, ids_ref, owner_ref, row_ref = vmem
    core, strip = at_ref[0], at_ref[1]
    for copy in copies:
        copy.wait()
    peers, stride, deep = out_ref.shape
    vocab_rows = vocab_ref.shape[0]
    pass_rows = index_ref.shape[0]
    folded = pass_rows // 2
    asked = vocab_rows + folded
    held = asked + 16
    columns = pl.ds(pl.multiple_of(strip * LANES, LANES), LANES)
    index = index_ref[:, columns]
    slab, plen, npass = slab_ref.shape[0], ids_ref.shape[0], ids_ref.shape[1]

    def places(owner, core):
        z, y = owner // peers, lax.rem(owner, peers)
        return jnp.where(core == 0, z, y), jnp.where(core == 0, y, z)

    def coded(owner, row):
        first, second = places(owner, 1 - core)
        code = second * REACH + first * stride + row
        return (code // LANES).astype(F32), lax.rem(code, LANES).astype(F32)

    ids = ids_ref[...]
    high, low = coded(ids // vocab_rows, lax.rem(ids, vocab_rows))
    lane = lax.broadcasted_iota(jnp.int32, (npass, deep), 1)
    passage = lax.broadcasted_iota(jnp.int32, (npass, deep), 0)
    high_row, low_row = jnp.zeros((1, deep), F32), jnp.zeros((1, deep), F32)
    for i in range(plen):
        to = (lane == passage * plen + i).astype(F32)
        high_row += exact(high[i : i + 1], to)
        low_row += exact(low[i : i + 1], to)
    high, low = coded(owner_ref[...], vocab_rows + lax.rem(row_ref[...], folded))
    to = (lane == passage + plen * npass).astype(F32)
    high_row += exact(high, to)
    low_row += exact(low, to)
    lane = lax.broadcasted_iota(jnp.int32, (1, deep), 1)
    none = peers * REACH - 1
    high_row = jnp.where(lane < (plen + 1) * npass, high_row, float(none // LANES))
    low_row = jnp.where(lane < (plen + 1) * npass, low_row, float(none % LANES))
    line = lax.broadcasted_iota(jnp.int32, (16, deep), 0)
    wanted = jnp.where(line == 0, high_row, jnp.where(line == 1, low_row, 0.0)).astype(BF16)

    slab_ids = slab_ids_ref[...]
    owner, row = slab_ids // pass_rows, lax.rem(slab_ids, pass_rows)
    i = lax.broadcasted_iota(jnp.int32, (slab, slab), 0)
    j = lax.broadcasted_iota(jnp.int32, (slab, slab), 1)
    owner_column = jnp.sum(jnp.where(i == j, owner.astype(F32), 0.0), axis=1, keepdims=True)
    place_column = jnp.sum(jnp.where(i == j, (row + 1).astype(F32), 0.0), axis=1, keepdims=True)
    before = jnp.where((owner_column == owner.astype(F32)) & (i < j), 1.0, 0.0)
    first, second = places(owner, core)
    slot = ((first * peers + second) * CAPS).astype(F32) + jnp.sum(before, axis=0, keepdims=True)
    slots = lax.broadcasted_iota(jnp.int32, (peers * peers * CAPS, slab), 0).astype(F32)
    select = jnp.where(slots == slot, 1.0, 0.0).astype(BF16)
    place = jnp.broadcast_to(place_column, (slab, deep - LANES)).astype(BF16)
    slab_out = dot(select, jnp.concatenate([slab_ref[:, columns], place], axis=1)).astype(BF16)

    index = jnp.concatenate([index[:folded], index[folded:]], axis=1)
    for peer in range(peers):
        out_ref[peer, :vocab_rows, :] = vocab_ref[...]
        out_ref[peer, vocab_rows:asked, :] = index
        out_ref[peer, asked:held, :] = wanted
        out_ref[peer, held:, :] = slab_out[peer * peers * CAPS : (peer + 1) * peers * CAPS]


def pack(core, strip, vocab, index, slab, slab_ids, ids, owner, row, peers):
    operands = (vocab, index, slab, slab_ids, ids, owner, row)
    rows = vocab.shape[0] + index.shape[0] // 2 + 16 + peers * CAPS
    return pl.pallas_call(
        pack_kernel,
        out_shape=jax.ShapeDtypeStruct((peers, rows, vocab.shape[1]), BF16),
        in_specs=[pl.BlockSpec(memory_space=pltpu.SMEM)]
        + [pl.BlockSpec(memory_space=pltpu.HBM)] * 7,
        out_specs=pl.BlockSpec(memory_space=pltpu.VMEM),
        scratch_shapes=[pltpu.VMEM(operand.shape, operand.dtype) for operand in operands]
        + [pltpu.SemaphoreType.DMA((7,))],
        compiler_params=pltpu.CompilerParams(vmem_limit_bytes=60 * 1024 * 1024),
        name="pack",
    )(jnp.stack([core, strip]), *operands)


def spread_kernel(got_ref, query_ref, high_ref, out_ref):
    count, passages = out_ref.shape[1] - 16, query_ref.shape[0]

    def summed(low, high):
        acc = got_ref[0, low:high, :].astype(F32)
        for source in range(1, got_ref.shape[0]):
            acc += got_ref[source, low:high, :].astype(F32)
        return acc.astype(BF16)

    rows = summed(0, count)
    products = summed(count, count + passages).astype(F32) * query_ref[...].astype(F32)
    low = jnp.sum(products[:, :LANES], axis=1, keepdims=True)
    high = jnp.sum(products[:, LANES:], axis=1, keepdims=True)
    scores = jnp.where(high_ref[...] > 0, high, low)
    p = lax.broadcasted_iota(jnp.int32, (passages, out_ref.shape[2]), 0)
    lane = lax.broadcasted_iota(jnp.int32, (passages, out_ref.shape[2]), 1)
    scores = jnp.sum(jnp.where(p == lane, scores, 0.0), axis=0, keepdims=True)
    parts = []
    for _ in range(3):
        parts.append(scores.astype(BF16).astype(F32))
        scores = scores - parts[-1]
    line = lax.broadcasted_iota(jnp.int32, (16, out_ref.shape[2]), 0)
    block = jnp.zeros((16, out_ref.shape[2]), F32)
    for i, part in enumerate(parts):
        block = jnp.where(line == i, part, block)
    block = block.astype(BF16)
    for peer in range(out_ref.shape[0]):
        out_ref[peer, :count, :] = rows
        out_ref[peer, count:, :] = block


def spread(got, query, high, count, peers):
    vmem = pl.BlockSpec(memory_space=pltpu.VMEM)
    return pl.pallas_call(
        spread_kernel,
        out_shape=jax.ShapeDtypeStruct((peers, count + 16, got.shape[2]), BF16),
        in_specs=[vmem] * 3,
        out_specs=vmem,
        compiler_params=pltpu.CompilerParams(vmem_limit_bytes=32 * 1024 * 1024),
        name="spread",
    )(got, query, high)


def total_kernel(terms_ref, *out_refs):
    rows = terms_ref.shape[1] // 2
    sums = []
    for half in range(2):
        acc = terms_ref[half].astype(F32)
        for i in range(2 + half, terms_ref.shape[0], 2):
            acc += terms_ref[i].astype(F32)
        sums.append(acc)
    for i, out_ref in enumerate(out_refs):
        top, left = divmod(i, 2)
        out_ref[...] = jnp.concatenate(
            [
                acc[top * rows : (top + 1) * rows, left * HEAD_DIM : (left + 1) * HEAD_DIM]
                for acc in sums
            ],
            axis=1,
        )


def total(terms):
    rows, width = terms.shape[1] // 2, terms.shape[2]
    vmem = pl.BlockSpec(memory_space=pltpu.VMEM)
    return pl.pallas_call(
        total_kernel,
        out_shape=(jax.ShapeDtypeStruct((rows, width), F32),) * 4,
        in_specs=[vmem],
        out_specs=(vmem,) * 4,
        compiler_params=pltpu.CompilerParams(vmem_limit_bytes=32 * 1024 * 1024),
        name="total",
    )(terms)


def shards(
    index_emb,
    query_emb,
    passage_owner,
    passage_row,
    token_ids,
    vocab_table,
    w_query,
    w_key,
    w_value,
    w_out,
    out_grad,
    slab_emb,
    slab_ids,
):
    nz, nq = lax.axis_size("z"), lax.axis_size("q")
    ny = lax.axis_size("p") * nq
    owners = nz * ny
    swap = [(0, 1), (1, 0)]
    my_z = lax.axis_index("z")
    my_y = lax.axis_index(("p", "q"))
    my_half = lax.axis_index("q")
    pass_rows, width = index_emb.shape
    queries = query_emb.shape[0]
    npass, plen = token_ids.shape
    count = npass * plen
    vocab_rows = vocab_table.shape[0]
    strips = width // LANES
    strip = lax.rem(lax.axis_index(M), strips)

    def my_strip(array):
        return lax.dynamic_slice_in_dim(array, strip * LANES, LANES, axis=1)

    cores = lax.axis_size("c")
    my_core = lax.axis_index("c")
    at_z = [[(z * ny + y) * cores for z in range(nz)] for y in range(ny)]
    at_y = [[(z * ny + y) * cores for y in range(ny)] for z in range(nz)]
    first_groups = at_z + [[i + 1 for i in group] for group in at_y]
    second_groups = at_y + [[i + 1 for i in group] for group in at_z]
    second = jnp.where(my_core == 0, my_y, my_z)

    deep = vocab_table.shape[1]
    index_strip = my_strip(index_emb)
    folded = pass_rows // 2
    asked = vocab_rows + folded
    held = asked + 16
    stride = held + ny * CAPS
    spare = -npass % 16
    rows_here = count + npass + spare
    message = pack(
        my_core,
        strip,
        vocab_table,
        index_emb,
        slab_emb,
        slab_ids[None],
        token_ids.T,
        passage_owner.T,
        passage_row[None],
        nz,
    )
    got_first = lax.all_to_all(
        message,
        ALONG,
        0,
        0,
        axis_index_groups=first_groups,
        tiled=True,
    )
    other = lax.ppermute(out_grad, "q", swap)
    got_first, other = lax.optimization_barrier((got_first, other))
    along_x = lax.all_gather(jnp.concatenate([out_grad, other], axis=0), "x", axis=0)
    wanted = lax.ppermute(got_first[:, asked : asked + 2], "c", [(0, 1), (1, 0)])
    wanted = wanted.astype(jnp.int32)[:, :, :rows_here]
    rows_at = wanted[:, 0] * LANES + wanted[:, 1] - second * REACH
    slab_at = (
        held
        + jnp.arange(ny)[:, None, None] * CAPS
        + jnp.arange(nz)[None, :, None] * stride
        + jnp.arange(CAPS)[None, None, :]
    ).reshape(ny, nz * CAPS)
    at = jnp.concatenate([rows_at, slab_at], axis=1)
    one_hot = (at.reshape(-1)[:, None] == jnp.arange(nz * stride)[None, :]).astype(BF16)
    served = dot(one_hot, got_first.reshape(nz * stride, deep)).astype(BF16)
    got_second = lax.all_to_all(
        served.reshape(*at.shape, deep),
        ALONG,
        0,
        0,
        axis_index_groups=second_groups,
        tiled=True,
    )
    got_second, along_x = lax.optimization_barrier((got_second, along_x))

    query = my_strip(query_emb)
    query = jnp.repeat(jnp.concatenate([query, query], axis=1), K, axis=0)
    query = jnp.pad(query, ((0, spare), (0, 0)))
    high = jnp.pad((passage_row >= folded).astype(jnp.int32), (0, spare))[:, None]
    nx = lax.axis_size("x")
    part = spread(got_second, query, high, count, nq * nx)
    grads = [
        lax.all_gather(along_x[i * nx // 2 : (i + 1) * nx // 2], "c", axis=0) for i in range(2)
    ]
    near = lax.all_to_all(part, ("q", "x"), 0, 0, tiled=True)
    near, grads = lax.optimization_barrier((near, grads))
    tokens = [lax.all_gather(near[i * nx : (i + 1) * nx], "c", axis=0) for i in range(nq)]

    got_slab = got_second[:, rows_here:].reshape(-1, deep)
    got_place = got_slab[:, LANES].astype(jnp.int32) - 1
    put = jnp.arange(pass_rows)[:, None] == got_place[None, :]
    placed = dot(put.astype(BF16), got_slab[:, :LANES]).astype(BF16)
    refreshed = jnp.where(jnp.any(put, axis=1)[:, None], placed, index_strip)

    terms, pair_relevance = reader(
        my_half.reshape(1), tokens, grads, (w_query, w_key, w_value, w_out), strips, owners
    )
    relevance = pair_relevance[0, :npass].reshape(queries, K)
    refreshed, terms = lax.optimization_barrier((refreshed, terms))
    refreshed = lax.all_gather(refreshed, M, axis=0)
    refreshed = jnp.concatenate([refreshed[i] for i in range(strips)], axis=1)
    terms = lax.all_to_all(terms, IDX, 0, 0, tiled=True)
    grad_query, grad_key, grad_value, grad_out = total(terms)
    return (relevance, grad_query, grad_key, grad_value, grad_out.T, refreshed)


def solution(mesh):
    devices = mesh.devices
    owners, columns = devices.shape
    fine = Mesh(devices.reshape(owners // 8, 4, 2, columns // 2, 2), (*IDX, *M))
    return jax.shard_map(
        shards,
        mesh=fine,
        in_specs=(
            P(IDX, None),
            P(IDX, None),
            P(IDX, None),
            P(IDX),
            P(IDX, None),
            P(IDX, M),
            P(None, M),
            P(None, M),
            P(None, M),
            P(M, None),
            P(IDX, M),
            P(IDX, None),
            P(IDX),
        ),
        out_specs=(
            P(IDX, None),
            P(IDX, M),
            P(IDX, M),
            P(IDX, M),
            P(M, IDX),
            P(IDX, None),
        ),
        check_vma=False,
    )
```

```python
import functools

import jax
import jax.numpy as jnp
from jax import lax
from jax.experimental import pallas as pl
from jax.experimental.pallas import tpu as pltpu
from jax.sharding import Mesh
from jax.sharding import PartitionSpec as P

HEAD_DIM = 64
K = 20
PLEN = 4
CAPS = 2
LANES = 128
REACH = 4096
IDX = ("z", "p", "q")
M = ("x", "c")
ALONG = ("z", "p", "q", "c")
F32 = jnp.float32
BF16 = jnp.bfloat16
ROWS = (((0,), (0,)), ((), ()))
COLS = (((1,), (1,)), ((), ()))


def dot(a, b, dims=None):
    if dims is None:
        return jnp.dot(a, b, preferred_element_type=F32)
    return lax.dot_general(a, b, dims, preferred_element_type=F32)


def reader_kernel(heads, strips, half_ref, *refs):
    token_refs, grad_refs, weight_refs, wo_ref = refs[:2], refs[2:4], refs[4:7], refs[7]
    out_ref, rel_ref = refs[8:]
    nc, nx, count, deep = grad_refs[0].shape
    blocks = 2 * nx * nc
    rows = out_ref.shape[1] // 2
    mine = half_ref[0]

    def grad_block(b):
        x, c = divmod(b, nc)
        return grad_refs[x // nx][c, x % nx]

    def token_block(b, low, high):
        x, c = divmod(b, nc)
        both = [ref[c, x, low:high, :] for ref in token_refs]
        ordered = [jnp.where(mine == 0, both[0], both[1]), jnp.where(mine == 0, both[1], both[0])]
        return jnp.concatenate(ordered, axis=0)

    valid = count // 2 // PLEN
    sums = []
    for ref in token_refs:
        acc = jnp.zeros((16, LANES), F32)
        for b in range(strips):
            x, c = divmod(b, nc)
            acc += ref[c, x, count // 2 :, :LANES].astype(F32)
        sums.append(jnp.sum(acc, axis=0, keepdims=True))
    lane = lax.broadcasted_iota(jnp.int32, (1, LANES), 1)
    token = lax.broadcasted_iota(jnp.int32, (count // 2, LANES), 0)
    begin = lax.broadcasted_iota(jnp.int32, (count // 2, LANES), 1) * PLEN
    of_token = (token >= begin) & (token < begin + PLEN)
    rel = []
    for scores in (
        jnp.where(mine == 0, sums[0], sums[1]),
        jnp.where(mine == 0, sums[1], sums[0]),
    ):
        share = jnp.zeros((1, LANES), F32)
        for first in range(0, valid, K):
            group = (lane >= first) & (lane < first + K)
            top = jnp.max(jnp.where(group, scores, -jnp.inf), axis=1, keepdims=True)
            exps = jnp.where(group, jnp.exp(scores - top), 0.0)
            share += exps / jnp.sum(exps, axis=1, keepdims=True)
        if not rel:
            rel_ref[...] = share
        rel.append(jnp.sum(jnp.where(of_token, share, 0.0), axis=1, keepdims=True))
    rel = jnp.concatenate(rel, axis=0)

    tokens = [token_block(b, 0, count // 2) for b in range(blocks)]
    weighted = [
        (grad_block(b).astype(F32) * rel).astype(BF16) for b in range(blocks)
    ]
    def own(states):
        kept = states[:, :HEAD_DIM]
        for head in range(1, heads):
            kept = jnp.where(mine == head, states[:, head * HEAD_DIM : (head + 1) * HEAD_DIM], kept)
        return kept

    def projected(weight_ref):
        states = dot(tokens[0], weight_ref[:deep])
        for b in range(1, blocks):
            states += dot(tokens[b], weight_ref[b * deep : (b + 1) * deep])
        return own(states.astype(BF16))

    q, k, v = (projected(weight_ref) for weight_ref in weight_refs)
    total = dot(weighted[0], wo_ref[:, :deep], COLS)
    for b in range(1, blocks):
        total += dot(weighted[b], wo_ref[:, b * deep : (b + 1) * deep], COLS)
    c = own(total.astype(BF16))
    passage_i = lax.broadcasted_iota(jnp.int32, (count, count), 0) // PLEN
    passage_j = lax.broadcasted_iota(jnp.int32, (count, count), 1) // PLEN
    logits = jnp.where(passage_i == passage_j, dot(q, k, COLS), -jnp.inf)
    exps = jnp.exp(logits - jnp.max(logits, axis=1, keepdims=True))
    probs = exps / jnp.sum(exps, axis=1, keepdims=True)
    attn = probs.astype(BF16)
    attn_grad = dot(c, v, COLS)
    mean = jnp.sum(attn_grad * probs, axis=1, keepdims=True)
    score_grad = (probs * (attn_grad - mean)).astype(BF16)
    query_grad = dot(score_grad, k).astype(BF16)
    key_grad = dot(score_grad, q, ROWS).astype(BF16)
    value_grad = dot(attn, c, ROWS).astype(BF16)
    context = dot(attn, v).astype(BF16)
    blank = jnp.zeros_like(context)
    token_side = jnp.concatenate([query_grad, key_grad, value_grad, blank], axis=1)
    weighted_side = jnp.concatenate([blank, blank, blank, context], axis=1)
    sides = jnp.concatenate([token_side, weighted_side], axis=0)
    span = deep // rows
    for b in range(blocks):
        term = dot(jnp.concatenate([tokens[b], weighted[b]], axis=0), sides, ROWS).astype(BF16)
        upper, lower = term[:, : 2 * HEAD_DIM], term[:, 2 * HEAD_DIM :]
        out_ref[b * span : (b + 1) * span, :rows, :] = upper.reshape(span, rows, -1)
        out_ref[b * span : (b + 1) * span, rows:, :] = lower.reshape(span, rows, -1)


def reader(half, tokens, out_grad, weights, strips, owners):
    width, inner = weights[0].shape
    vmem = pl.BlockSpec(memory_space=pltpu.VMEM)
    return pl.pallas_call(
        functools.partial(reader_kernel, inner // HEAD_DIM, strips),
        out_shape=(
            jax.ShapeDtypeStruct((owners, 2 * width // owners, 2 * HEAD_DIM), BF16),
            jax.ShapeDtypeStruct((1, LANES), F32),
        ),
        in_specs=[pl.BlockSpec(memory_space=pltpu.SMEM)]
        + [vmem] * 8,
        out_specs=(vmem, vmem),
        compiler_params=pltpu.CompilerParams(vmem_limit_bytes=40 * 1024 * 1024),
        name="reader",
    )(half, *tokens, *out_grad, *weights)


def exact(a, b):
    return dot(a.astype(BF16), b.astype(BF16))


def pack_kernel(at_ref, *refs):
    hbm, out_ref, vmem, rest_ref, sems = refs[:7], refs[7], refs[8:15], refs[15], refs[16]
    copies = [pltpu.make_async_copy(hbm[i], vmem[i], sems.at[i]) for i in range(7)]
    for copy in copies:
        copy.start()
    vocab_ref, index_ref, slab_ref, slab_ids_ref, ids_ref, owner_ref, row_ref = vmem
    core, strip = at_ref[0], at_ref[1]
    peers, stride, deep = out_ref.shape
    vocab_rows = vocab_ref.shape[0]
    copies[0].wait()
    sends = [
        pltpu.make_async_copy(vocab_ref, out_ref.at[peer, :vocab_rows, :], sems.at[7 + peer])
        for peer in range(peers)
    ]
    for send in sends:
        send.start()
    for copy in copies[1:]:
        copy.wait()
    pass_rows = index_ref.shape[0]
    folded = pass_rows // 2
    asked = vocab_rows + folded
    columns = pl.ds(pl.multiple_of(strip * LANES, LANES), LANES)
    index = index_ref[:, columns]
    slab, plen, npass = slab_ref.shape[0], ids_ref.shape[0], ids_ref.shape[1]

    def places(owner, core):
        z, y = owner // peers, lax.rem(owner, peers)
        return jnp.where(core == 0, z, y), jnp.where(core == 0, y, z)

    def coded(owner, row):
        first, second = places(owner, 1 - core)
        code = second * REACH + first * stride + row
        return (code // LANES).astype(F32), lax.rem(code, LANES).astype(F32)

    ids = ids_ref[...]
    high, low = coded(ids // vocab_rows, lax.rem(ids, vocab_rows))
    lane = lax.broadcasted_iota(jnp.int32, (npass, deep), 1)
    passage = lax.broadcasted_iota(jnp.int32, (npass, deep), 0)
    high_row, low_row = jnp.zeros((1, deep), F32), jnp.zeros((1, deep), F32)
    for i in range(plen):
        to = (lane == passage * plen + i).astype(F32)
        high_row += exact(high[i : i + 1], to)
        low_row += exact(low[i : i + 1], to)
    high, low = coded(owner_ref[...], vocab_rows + lax.rem(row_ref[...], folded))
    to = (lane == passage + plen * npass).astype(F32)
    high_row += exact(high, to)
    low_row += exact(low, to)
    lane = lax.broadcasted_iota(jnp.int32, (1, deep), 1)
    none = peers * REACH - 1
    high_row = jnp.where(lane < (plen + 1) * npass, high_row, float(none // LANES))
    low_row = jnp.where(lane < (plen + 1) * npass, low_row, float(none % LANES))
    line = lax.broadcasted_iota(jnp.int32, (16, deep), 0)
    wanted = jnp.where(line == 0, high_row, jnp.where(line == 1, low_row, 0.0)).astype(BF16)

    slab_ids = slab_ids_ref[...]
    owner, row = slab_ids // pass_rows, lax.rem(slab_ids, pass_rows)
    i = lax.broadcasted_iota(jnp.int32, (slab, slab), 0)
    j = lax.broadcasted_iota(jnp.int32, (slab, slab), 1)
    owner_column = jnp.sum(jnp.where(i == j, owner.astype(F32), 0.0), axis=1, keepdims=True)
    place_column = jnp.sum(jnp.where(i == j, (row + 1).astype(F32), 0.0), axis=1, keepdims=True)
    before = jnp.where((owner_column == owner.astype(F32)) & (i < j), 1.0, 0.0)
    first, second = places(owner, core)
    slot = ((first * peers + second) * CAPS).astype(F32) + jnp.sum(before, axis=0, keepdims=True)
    slots = lax.broadcasted_iota(jnp.int32, (peers * peers * CAPS, slab), 0).astype(F32)
    select = jnp.where(slots == slot, 1.0, 0.0).astype(BF16)
    place = jnp.broadcast_to(place_column, (slab, deep - LANES)).astype(BF16)
    slab_out = dot(select, jnp.concatenate([slab_ref[:, columns], place], axis=1)).astype(BF16)

    index = jnp.concatenate([index[:folded], index[folded:]], axis=1)
    for peer in range(peers):
        rest_ref[peer, :folded, :] = index
        rest_ref[peer, folded : folded + 16, :] = wanted
        rest_ref[peer, folded + 16 :, :] = slab_out[
            peer * peers * CAPS : (peer + 1) * peers * CAPS
        ]
    last = pltpu.make_async_copy(rest_ref, out_ref.at[:, vocab_rows:, :], sems.at[7 + peers])
    last.start()
    for send in sends:
        send.wait()
    last.wait()


def pack(core, strip, vocab, index, slab, slab_ids, ids, owner, row, peers):
    operands = (vocab, index, slab, slab_ids, ids, owner, row)
    rows = vocab.shape[0] + index.shape[0] // 2 + 16 + peers * CAPS
    return pl.pallas_call(
        pack_kernel,
        out_shape=jax.ShapeDtypeStruct((peers, rows, vocab.shape[1]), BF16),
        in_specs=[pl.BlockSpec(memory_space=pltpu.SMEM)]
        + [pl.BlockSpec(memory_space=pltpu.HBM)] * 7,
        out_specs=pl.BlockSpec(memory_space=pltpu.HBM),
        scratch_shapes=[pltpu.VMEM(operand.shape, operand.dtype) for operand in operands]
        + [
            pltpu.VMEM((peers, rows - vocab.shape[0], vocab.shape[1]), BF16),
            pltpu.SemaphoreType.DMA((8 + peers,)),
        ],
        compiler_params=pltpu.CompilerParams(vmem_limit_bytes=60 * 1024 * 1024),
        name="pack",
    )(jnp.stack([core, strip]), *operands)


def spread_kernel(got_ref, query_ref, high_ref, out_ref):
    count, passages = out_ref.shape[1] - 16, query_ref.shape[0]

    def summed(low, high):
        acc = got_ref[0, low:high, :].astype(F32)
        for source in range(1, got_ref.shape[0]):
            acc += got_ref[source, low:high, :].astype(F32)
        return acc.astype(BF16)

    rows = summed(0, count)
    products = summed(count, count + passages).astype(F32) * query_ref[...].astype(F32)
    low = jnp.sum(products[:, :LANES], axis=1, keepdims=True)
    high = jnp.sum(products[:, LANES:], axis=1, keepdims=True)
    scores = jnp.where(high_ref[...] > 0, high, low)
    p = lax.broadcasted_iota(jnp.int32, (passages, out_ref.shape[2]), 0)
    lane = lax.broadcasted_iota(jnp.int32, (passages, out_ref.shape[2]), 1)
    scores = jnp.sum(jnp.where(p == lane, scores, 0.0), axis=0, keepdims=True)
    parts = []
    for _ in range(3):
        parts.append(scores.astype(BF16).astype(F32))
        scores = scores - parts[-1]
    line = lax.broadcasted_iota(jnp.int32, (16, out_ref.shape[2]), 0)
    block = jnp.zeros((16, out_ref.shape[2]), F32)
    for i, part in enumerate(parts):
        block = jnp.where(line == i, part, block)
    block = block.astype(BF16)
    for peer in range(out_ref.shape[0]):
        out_ref[peer, :count, :] = rows
        out_ref[peer, count:, :] = block


def spread(got, query, high, count, peers):
    vmem = pl.BlockSpec(memory_space=pltpu.VMEM)
    return pl.pallas_call(
        spread_kernel,
        out_shape=jax.ShapeDtypeStruct((peers, count + 16, got.shape[2]), BF16),
        in_specs=[vmem] * 3,
        out_specs=vmem,
        compiler_params=pltpu.CompilerParams(vmem_limit_bytes=32 * 1024 * 1024),
        name="spread",
    )(got, query, high)


def total_kernel(terms_ref, *out_refs):
    rows = terms_ref.shape[1] // 2
    sums = []
    for half in range(2):
        acc = terms_ref[half].astype(F32)
        for i in range(2 + half, terms_ref.shape[0], 2):
            acc += terms_ref[i].astype(F32)
        sums.append(acc)
    for i, out_ref in enumerate(out_refs):
        top, left = divmod(i, 2)
        out_ref[...] = jnp.concatenate(
            [
                acc[top * rows : (top + 1) * rows, left * HEAD_DIM : (left + 1) * HEAD_DIM]
                for acc in sums
            ],
            axis=1,
        )


def total(terms):
    rows, width = terms.shape[1] // 2, terms.shape[2]
    vmem = pl.BlockSpec(memory_space=pltpu.VMEM)
    return pl.pallas_call(
        total_kernel,
        out_shape=(jax.ShapeDtypeStruct((rows, width), F32),) * 4,
        in_specs=[vmem],
        out_specs=(vmem,) * 4,
        compiler_params=pltpu.CompilerParams(vmem_limit_bytes=32 * 1024 * 1024),
        name="total",
    )(terms)


def shards(
    index_emb,
    query_emb,
    passage_owner,
    passage_row,
    token_ids,
    vocab_table,
    w_query,
    w_key,
    w_value,
    w_out,
    out_grad,
    slab_emb,
    slab_ids,
):
    nz, nq = lax.axis_size("z"), lax.axis_size("q")
    ny = lax.axis_size("p") * nq
    owners = nz * ny
    swap = [(0, 1), (1, 0)]
    my_z = lax.axis_index("z")
    my_y = lax.axis_index(("p", "q"))
    my_half = lax.axis_index("q")
    pass_rows, width = index_emb.shape
    queries = query_emb.shape[0]
    npass, plen = token_ids.shape
    count = npass * plen
    vocab_rows = vocab_table.shape[0]
    strips = width // LANES
    strip = lax.rem(lax.axis_index(M), strips)

    def my_strip(array):
        return lax.dynamic_slice_in_dim(array, strip * LANES, LANES, axis=1)

    cores = lax.axis_size("c")
    my_core = lax.axis_index("c")
    at_z = [[(z * ny + y) * cores for z in range(nz)] for y in range(ny)]
    at_y = [[(z * ny + y) * cores for y in range(ny)] for z in range(nz)]
    first_groups = at_z + [[i + 1 for i in group] for group in at_y]
    second_groups = at_y + [[i + 1 for i in group] for group in at_z]
    second = jnp.where(my_core == 0, my_y, my_z)

    deep = vocab_table.shape[1]
    index_strip = my_strip(index_emb)
    folded = pass_rows // 2
    asked = vocab_rows + folded
    held = asked + 16
    stride = held + ny * CAPS
    spare = -npass % 16
    rows_here = count + npass + spare
    message = pack(
        my_core,
        strip,
        vocab_table,
        index_emb,
        slab_emb,
        slab_ids[None],
        token_ids.T,
        passage_owner.T,
        passage_row[None],
        nz,
    )
    got_first = lax.all_to_all(
        message,
        ALONG,
        0,
        0,
        axis_index_groups=first_groups,
        tiled=True,
    )
    other = lax.ppermute(out_grad, "q", swap)
    got_first, other = lax.optimization_barrier((got_first, other))
    along_x = lax.all_gather(jnp.concatenate([out_grad, other], axis=0), "x", axis=0)
    wanted = lax.all_gather(got_first[:, asked : asked + 2].reshape(1, -1, deep), "c", axis=0, tiled=True)
    wanted = lax.dynamic_index_in_dim(wanted, 1 - my_core, axis=0, keepdims=False)
    wanted = wanted.reshape(ny, 2, deep).astype(jnp.int32)[:, :, :rows_here]
    rows_at = wanted[:, 0] * LANES + wanted[:, 1] - second * REACH
    slab_at = (
        held
        + jnp.arange(ny)[:, None, None] * CAPS
        + jnp.arange(nz)[None, :, None] * stride
        + jnp.arange(CAPS)[None, None, :]
    ).reshape(ny, nz * CAPS)
    at = jnp.concatenate([rows_at, slab_at], axis=1)
    one_hot = (at.reshape(-1)[:, None] == jnp.arange(nz * stride)[None, :]).astype(BF16)
    served = dot(one_hot, got_first.reshape(nz * stride, deep)).astype(BF16)
    got_second = lax.all_to_all(
        served.reshape(*at.shape, deep),
        ALONG,
        0,
        0,
        axis_index_groups=second_groups,
        tiled=True,
    )
    got_second, along_x = lax.optimization_barrier((got_second, along_x))

    query = my_strip(query_emb)
    query = jnp.repeat(jnp.concatenate([query, query], axis=1), K, axis=0)
    query = jnp.pad(query, ((0, spare), (0, 0)))
    high = jnp.pad((passage_row >= folded).astype(jnp.int32), (0, spare))[:, None]
    nx = lax.axis_size("x")
    part = spread(got_second, query, high, count, nq * nx)
    grads = [
        lax.all_gather(along_x[i * nx // 2 : (i + 1) * nx // 2], "c", axis=0) for i in range(2)
    ]
    near = lax.all_to_all(part, ("q", "x"), 0, 0, tiled=True)
    near, grads = lax.optimization_barrier((near, grads))
    tokens = [lax.all_gather(near[i * nx : (i + 1) * nx], "c", axis=0) for i in range(nq)]

    got_slab = got_second[:, rows_here:].reshape(-1, deep)
    got_place = got_slab[:, LANES].astype(jnp.int32) - 1
    put = jnp.arange(pass_rows)[:, None] == got_place[None, :]
    placed = dot(put.astype(BF16), got_slab[:, :LANES]).astype(BF16)
    refreshed = jnp.where(jnp.any(put, axis=1)[:, None], placed, index_strip)

    terms, pair_relevance = reader(
        my_half.reshape(1), tokens, grads, (w_query, w_key, w_value, w_out), strips, owners
    )
    relevance = pair_relevance[0, :npass].reshape(queries, K)
    refreshed, terms = lax.optimization_barrier((refreshed, terms))
    refreshed = lax.all_gather(refreshed, M, axis=0)
    refreshed = jnp.concatenate([refreshed[i] for i in range(strips)], axis=1)
    terms = lax.all_to_all(terms, IDX, 0, 0, tiled=True)
    grad_query, grad_key, grad_value, grad_out = total(terms)
    return (relevance, grad_query, grad_key, grad_value, grad_out.T, refreshed)


def solution(mesh):
    devices = mesh.devices
    owners, columns = devices.shape
    fine = Mesh(devices.reshape(owners // 8, 4, 2, columns // 2, 2), (*IDX, *M))
    return jax.shard_map(
        shards,
        mesh=fine,
        in_specs=(
            P(IDX, None),
            P(IDX, None),
            P(IDX, None),
            P(IDX),
            P(IDX, None),
            P(IDX, M),
            P(None, M),
            P(None, M),
            P(None, M),
            P(M, None),
            P(IDX, M),
            P(IDX, None),
            P(IDX),
        ),
        out_specs=(
            P(IDX, None),
            P(IDX, M),
            P(IDX, M),
            P(IDX, M),
            P(M, IDX),
            P(IDX, None),
        ),
        check_vma=False,
    )
```

```python
import functools

import jax
import jax.numpy as jnp
from jax import lax
from jax.experimental import pallas as pl
from jax.experimental.pallas import tpu as pltpu
from jax.sharding import Mesh
from jax.sharding import PartitionSpec as P

HEAD_DIM = 64
K = 20
PLEN = 4
CAPS = 2
LANES = 128
REACH = 4096
IDX = ("z", "p", "q")
M = ("x", "c")
ALONG = ("z", "p", "q", "c")
F32 = jnp.float32
BF16 = jnp.bfloat16
ROWS = (((0,), (0,)), ((), ()))
COLS = (((1,), (1,)), ((), ()))


def dot(a, b, dims=None):
    if dims is None:
        return jnp.dot(a, b, preferred_element_type=F32)
    return lax.dot_general(a, b, dims, preferred_element_type=F32)


def reader_kernel(heads, strips, half_ref, *refs):
    token_refs, grad_refs, weight_refs, wo_ref = refs[:2], refs[2:4], refs[4:7], refs[7]
    out_ref, rel_ref = refs[8:]
    nc, nx, count, deep = grad_refs[0].shape
    blocks = 2 * nx * nc
    rows = out_ref.shape[1] // 2
    mine = half_ref[0]

    def grad_block(b):
        x, c = divmod(b, nc)
        return grad_refs[x // nx][c, x % nx]

    def token_block(b, low, high):
        x, c = divmod(b, nc)
        both = [ref[c, x, low:high, :] for ref in token_refs]
        ordered = [jnp.where(mine == 0, both[0], both[1]), jnp.where(mine == 0, both[1], both[0])]
        return jnp.concatenate(ordered, axis=0)

    valid = count // 2 // PLEN
    sums = []
    for ref in token_refs:
        acc = jnp.zeros((16, LANES), F32)
        for b in range(strips):
            x, c = divmod(b, nc)
            acc += ref[c, x, count // 2 :, :LANES].astype(F32)
        sums.append(jnp.sum(acc, axis=0, keepdims=True))
    lane = lax.broadcasted_iota(jnp.int32, (1, LANES), 1)
    token = lax.broadcasted_iota(jnp.int32, (count // 2, LANES), 0)
    begin = lax.broadcasted_iota(jnp.int32, (count // 2, LANES), 1) * PLEN
    of_token = (token >= begin) & (token < begin + PLEN)
    rel = []
    for scores in (
        jnp.where(mine == 0, sums[0], sums[1]),
        jnp.where(mine == 0, sums[1], sums[0]),
    ):
        share = jnp.zeros((1, LANES), F32)
        for first in range(0, valid, K):
            group = (lane >= first) & (lane < first + K)
            top = jnp.max(jnp.where(group, scores, -jnp.inf), axis=1, keepdims=True)
            exps = jnp.where(group, jnp.exp(scores - top), 0.0)
            share += exps / jnp.sum(exps, axis=1, keepdims=True)
        if not rel:
            rel_ref[...] = share
        rel.append(jnp.sum(jnp.where(of_token, share, 0.0), axis=1, keepdims=True))
    rel = jnp.concatenate(rel, axis=0)

    tokens = [token_block(b, 0, count // 2) for b in range(blocks)]
    weighted = [
        (grad_block(b).astype(F32) * rel).astype(BF16) for b in range(blocks)
    ]
    def own(states):
        kept = states[:, :HEAD_DIM]
        for head in range(1, heads):
            kept = jnp.where(mine == head, states[:, head * HEAD_DIM : (head + 1) * HEAD_DIM], kept)
        return kept

    def projected(weight_ref):
        states = dot(tokens[0], weight_ref[:deep])
        for b in range(1, blocks):
            states += dot(tokens[b], weight_ref[b * deep : (b + 1) * deep])
        return own(states.astype(BF16))

    q, k, v = (projected(weight_ref) for weight_ref in weight_refs)
    total = dot(weighted[0], wo_ref[:, :deep], COLS)
    for b in range(1, blocks):
        total += dot(weighted[b], wo_ref[:, b * deep : (b + 1) * deep], COLS)
    c = own(total.astype(BF16))
    passage_i = lax.broadcasted_iota(jnp.int32, (count, count), 0) // PLEN
    passage_j = lax.broadcasted_iota(jnp.int32, (count, count), 1) // PLEN
    logits = jnp.where(passage_i == passage_j, dot(q, k, COLS), -jnp.inf)
    exps = jnp.exp(logits - jnp.max(logits, axis=1, keepdims=True))
    probs = exps / jnp.sum(exps, axis=1, keepdims=True)
    attn = probs.astype(BF16)
    attn_grad = dot(c, v, COLS)
    mean = jnp.sum(attn_grad * probs, axis=1, keepdims=True)
    score_grad = (probs * (attn_grad - mean)).astype(BF16)
    query_grad = dot(score_grad, k).astype(BF16)
    key_grad = dot(score_grad, q, ROWS).astype(BF16)
    value_grad = dot(attn, c, ROWS).astype(BF16)
    context = dot(attn, v).astype(BF16)
    blank = jnp.zeros_like(context)
    token_side = jnp.concatenate([query_grad, key_grad, value_grad, blank], axis=1)
    weighted_side = jnp.concatenate([blank, blank, blank, context], axis=1)
    sides = jnp.concatenate([token_side, weighted_side], axis=0)
    span = deep // rows
    for b in range(blocks):
        term = dot(jnp.concatenate([tokens[b], weighted[b]], axis=0), sides, ROWS).astype(BF16)
        upper, lower = term[:, : 2 * HEAD_DIM], term[:, 2 * HEAD_DIM :]
        out_ref[b * span : (b + 1) * span, :rows, :] = upper.reshape(span, rows, -1)
        out_ref[b * span : (b + 1) * span, rows:, :] = lower.reshape(span, rows, -1)


def reader(half, tokens, out_grad, weights, strips, owners):
    width, inner = weights[0].shape
    vmem = pl.BlockSpec(memory_space=pltpu.VMEM)
    return pl.pallas_call(
        functools.partial(reader_kernel, inner // HEAD_DIM, strips),
        out_shape=(
            jax.ShapeDtypeStruct((owners, 2 * width // owners, 2 * HEAD_DIM), BF16),
            jax.ShapeDtypeStruct((1, LANES), F32),
        ),
        in_specs=[pl.BlockSpec(memory_space=pltpu.SMEM)]
        + [vmem] * 8,
        out_specs=(vmem, vmem),
        compiler_params=pltpu.CompilerParams(vmem_limit_bytes=40 * 1024 * 1024),
        name="reader",
    )(half, *tokens, *out_grad, *weights)


def exact(a, b):
    return dot(a.astype(BF16), b.astype(BF16))


def pack_kernel(at_ref, *refs):
    hbm, out_ref, vmem, rest_ref, sems = refs[:7], refs[7], refs[8:15], refs[15], refs[16]
    copies = [pltpu.make_async_copy(hbm[i], vmem[i], sems.at[i]) for i in range(7)]
    for copy in copies:
        copy.start()
    vocab_ref, index_ref, slab_ref, slab_ids_ref, ids_ref, owner_ref, row_ref = vmem
    core, strip = at_ref[0], at_ref[1]
    peers, stride, deep = out_ref.shape
    vocab_rows = vocab_ref.shape[0]
    copies[0].wait()
    sends = [
        pltpu.make_async_copy(vocab_ref, out_ref.at[peer, :vocab_rows, :], sems.at[7 + peer])
        for peer in range(peers)
    ]
    for send in sends:
        send.start()
    for copy in copies[1:]:
        copy.wait()
    pass_rows = index_ref.shape[0]
    folded = pass_rows // 2
    asked = vocab_rows + folded
    columns = pl.ds(pl.multiple_of(strip * LANES, LANES), LANES)
    index = index_ref[:, columns]
    slab, plen, npass = slab_ref.shape[0], ids_ref.shape[0], ids_ref.shape[1]

    def places(owner, core):
        z, y = owner // peers, lax.rem(owner, peers)
        return jnp.where(core == 0, z, y), jnp.where(core == 0, y, z)

    def coded(owner, row):
        first, second = places(owner, 1 - core)
        code = second * REACH + first * stride + row
        return (code // LANES).astype(F32), lax.rem(code, LANES).astype(F32)

    ids = ids_ref[...]
    high, low = coded(ids // vocab_rows, lax.rem(ids, vocab_rows))
    lane = lax.broadcasted_iota(jnp.int32, (npass, deep), 1)
    passage = lax.broadcasted_iota(jnp.int32, (npass, deep), 0)
    high_row, low_row = jnp.zeros((1, deep), F32), jnp.zeros((1, deep), F32)
    for i in range(plen):
        to = (lane == passage * plen + i).astype(F32)
        high_row += exact(high[i : i + 1], to)
        low_row += exact(low[i : i + 1], to)
    high, low = coded(owner_ref[...], vocab_rows + lax.rem(row_ref[...], folded))
    to = (lane == passage + plen * npass).astype(F32)
    high_row += exact(high, to)
    low_row += exact(low, to)
    lane = lax.broadcasted_iota(jnp.int32, (1, deep), 1)
    none = peers * REACH - 1
    high_row = jnp.where(lane < (plen + 1) * npass, high_row, float(none // LANES))
    low_row = jnp.where(lane < (plen + 1) * npass, low_row, float(none % LANES))
    line = lax.broadcasted_iota(jnp.int32, (16, deep), 0)
    wanted = jnp.where(line == 0, high_row, jnp.where(line == 1, low_row, 0.0)).astype(BF16)

    slab_ids = slab_ids_ref[...]
    owner, row = slab_ids // pass_rows, lax.rem(slab_ids, pass_rows)
    i = lax.broadcasted_iota(jnp.int32, (slab, slab), 0)
    j = lax.broadcasted_iota(jnp.int32, (slab, slab), 1)
    owner_column = jnp.sum(jnp.where(i == j, owner.astype(F32), 0.0), axis=1, keepdims=True)
    place_column = jnp.sum(jnp.where(i == j, (row + 1).astype(F32), 0.0), axis=1, keepdims=True)
    before = jnp.where((owner_column == owner.astype(F32)) & (i < j), 1.0, 0.0)
    first, second = places(owner, core)
    slot = ((first * peers + second) * CAPS).astype(F32) + jnp.sum(before, axis=0, keepdims=True)
    slots = lax.broadcasted_iota(jnp.int32, (peers * peers * CAPS, slab), 0).astype(F32)
    select = jnp.where(slots == slot, 1.0, 0.0).astype(BF16)
    place = jnp.broadcast_to(place_column, (slab, deep - LANES)).astype(BF16)
    slab_out = dot(select, jnp.concatenate([slab_ref[:, columns], place], axis=1)).astype(BF16)

    index = jnp.concatenate([index[:folded], index[folded:]], axis=1)
    for peer in range(peers):
        rest_ref[peer, :folded, :] = index
        rest_ref[peer, folded : folded + 16, :] = wanted
        rest_ref[peer, folded + 16 :, :] = slab_out[
            peer * peers * CAPS : (peer + 1) * peers * CAPS
        ]
    last = pltpu.make_async_copy(rest_ref, out_ref.at[:, vocab_rows:, :], sems.at[7 + peers])
    last.start()
    for send in sends:
        send.wait()
    last.wait()


def pack(core, strip, vocab, index, slab, slab_ids, ids, owner, row, peers):
    operands = (vocab, index, slab, slab_ids, ids, owner, row)
    rows = vocab.shape[0] + index.shape[0] // 2 + 16 + peers * CAPS
    return pl.pallas_call(
        pack_kernel,
        out_shape=jax.ShapeDtypeStruct((peers, rows, vocab.shape[1]), BF16),
        in_specs=[pl.BlockSpec(memory_space=pltpu.SMEM)]
        + [pl.BlockSpec(memory_space=pltpu.HBM)] * 7,
        out_specs=pl.BlockSpec(memory_space=pltpu.HBM),
        scratch_shapes=[pltpu.VMEM(operand.shape, operand.dtype) for operand in operands]
        + [
            pltpu.VMEM((peers, rows - vocab.shape[0], vocab.shape[1]), BF16),
            pltpu.SemaphoreType.DMA((8 + peers,)),
        ],
        compiler_params=pltpu.CompilerParams(vmem_limit_bytes=60 * 1024 * 1024),
        name="pack",
    )(jnp.stack([core, strip]), *operands)


def spread_kernel(got_ref, query_ref, high_ref, out_ref):
    count, passages = out_ref.shape[1] - 16, query_ref.shape[0]

    def summed(low, high):
        acc = got_ref[0, low:high, :].astype(F32)
        for source in range(1, got_ref.shape[0]):
            acc += got_ref[source, low:high, :].astype(F32)
        return acc.astype(BF16)

    rows = summed(0, count)
    products = summed(count, count + passages).astype(F32) * query_ref[...].astype(F32)
    low = jnp.sum(products[:, :LANES], axis=1, keepdims=True)
    high = jnp.sum(products[:, LANES:], axis=1, keepdims=True)
    scores = jnp.where(high_ref[...] > 0, high, low)
    p = lax.broadcasted_iota(jnp.int32, (passages, out_ref.shape[2]), 0)
    lane = lax.broadcasted_iota(jnp.int32, (passages, out_ref.shape[2]), 1)
    scores = jnp.sum(jnp.where(p == lane, scores, 0.0), axis=0, keepdims=True)
    parts = []
    for _ in range(3):
        parts.append(scores.astype(BF16).astype(F32))
        scores = scores - parts[-1]
    line = lax.broadcasted_iota(jnp.int32, (16, out_ref.shape[2]), 0)
    block = jnp.zeros((16, out_ref.shape[2]), F32)
    for i, part in enumerate(parts):
        block = jnp.where(line == i, part, block)
    block = block.astype(BF16)
    for peer in range(out_ref.shape[0]):
        out_ref[peer, :count, :] = rows
        out_ref[peer, count:, :] = block


def spread(got, query, high, count, peers):
    vmem = pl.BlockSpec(memory_space=pltpu.VMEM)
    return pl.pallas_call(
        spread_kernel,
        out_shape=jax.ShapeDtypeStruct((peers, count + 16, got.shape[2]), BF16),
        in_specs=[vmem] * 3,
        out_specs=vmem,
        compiler_params=pltpu.CompilerParams(vmem_limit_bytes=32 * 1024 * 1024),
        name="spread",
    )(got, query, high)


def total_kernel(terms_ref, *out_refs):
    rows = terms_ref.shape[1] // 2
    sums = []
    for half in range(2):
        acc = terms_ref[half].astype(F32)
        for i in range(2 + half, terms_ref.shape[0], 2):
            acc += terms_ref[i].astype(F32)
        sums.append(acc)
    for i, out_ref in enumerate(out_refs):
        top, left = divmod(i, 2)
        out_ref[...] = jnp.concatenate(
            [
                acc[top * rows : (top + 1) * rows, left * HEAD_DIM : (left + 1) * HEAD_DIM]
                for acc in sums
            ],
            axis=1,
        )


def total(terms):
    rows, width = terms.shape[1] // 2, terms.shape[2]
    vmem = pl.BlockSpec(memory_space=pltpu.VMEM)
    return pl.pallas_call(
        total_kernel,
        out_shape=(jax.ShapeDtypeStruct((rows, width), F32),) * 4,
        in_specs=[vmem],
        out_specs=(vmem,) * 4,
        compiler_params=pltpu.CompilerParams(vmem_limit_bytes=32 * 1024 * 1024),
        name="total",
    )(terms)


def shards(
    index_emb,
    query_emb,
    passage_owner,
    passage_row,
    token_ids,
    vocab_table,
    w_query,
    w_key,
    w_value,
    w_out,
    out_grad,
    slab_emb,
    slab_ids,
):
    nz, nq = lax.axis_size("z"), lax.axis_size("q")
    ny = lax.axis_size("p") * nq
    owners = nz * ny
    swap = [(0, 1), (1, 0)]
    my_z = lax.axis_index("z")
    my_y = lax.axis_index(("p", "q"))
    my_half = lax.axis_index("q")
    pass_rows, width = index_emb.shape
    queries = query_emb.shape[0]
    npass, plen = token_ids.shape
    count = npass * plen
    vocab_rows = vocab_table.shape[0]
    strips = width // LANES
    strip = lax.rem(lax.axis_index(M), strips)

    def my_strip(array):
        return lax.dynamic_slice_in_dim(array, strip * LANES, LANES, axis=1)

    cores = lax.axis_size("c")
    my_core = lax.axis_index("c")
    at_z = [[(z * ny + y) * cores for z in range(nz)] for y in range(ny)]
    at_y = [[(z * ny + y) * cores for y in range(ny)] for z in range(nz)]
    first_groups = at_z + [[i + 1 for i in group] for group in at_y]
    second_groups = at_y + [[i + 1 for i in group] for group in at_z]
    second = jnp.where(my_core == 0, my_y, my_z)

    deep = vocab_table.shape[1]
    index_strip = my_strip(index_emb)
    folded = pass_rows // 2
    asked = vocab_rows + folded
    held = asked + 16
    stride = held + ny * CAPS
    spare = -npass % 16
    rows_here = count + npass
    message = pack(
        my_core,
        strip,
        vocab_table,
        index_emb,
        slab_emb,
        slab_ids[None],
        token_ids.T,
        passage_owner.T,
        passage_row[None],
        nz,
    )
    got_first = lax.all_to_all(
        message,
        ALONG,
        0,
        0,
        axis_index_groups=first_groups,
        tiled=True,
    )
    other = lax.ppermute(out_grad, "q", swap)
    got_first, other = lax.optimization_barrier((got_first, other))
    along_x = lax.all_gather(jnp.concatenate([out_grad, other], axis=0), "x", axis=0)
    wanted = lax.all_gather(got_first[:, asked : asked + 2].reshape(1, -1, deep), "c", axis=0, tiled=True)
    wanted = lax.dynamic_index_in_dim(wanted, 1 - my_core, axis=0, keepdims=False)
    wanted = wanted.reshape(ny, 2, deep).astype(jnp.int32)[:, :, :rows_here]
    rows_at = wanted[:, 0] * LANES + wanted[:, 1] - second * REACH
    slab_at = (
        held
        + jnp.arange(ny)[:, None, None] * CAPS
        + jnp.arange(nz)[None, :, None] * stride
        + jnp.arange(CAPS)[None, None, :]
    ).reshape(ny, nz * CAPS)
    at = jnp.concatenate([rows_at, slab_at], axis=1)
    one_hot = (at.reshape(-1)[:, None] == jnp.arange(nz * stride)[None, :]).astype(BF16)
    served = dot(one_hot, got_first.reshape(nz * stride, deep)).astype(BF16)
    got_second = lax.all_to_all(
        served.reshape(*at.shape, deep),
        ALONG,
        0,
        0,
        axis_index_groups=second_groups,
        tiled=True,
    )
    got_second, along_x = lax.optimization_barrier((got_second, along_x))

    query = my_strip(query_emb)
    query = jnp.repeat(jnp.concatenate([query, query], axis=1), K, axis=0)
    query = jnp.pad(query, ((0, spare), (0, 0)))
    high = jnp.pad((passage_row >= folded).astype(jnp.int32), (0, spare))[:, None]
    nx = lax.axis_size("x")
    part = spread(got_second, query, high, count, nq * nx)
    grads = [
        lax.all_gather(along_x[i * nx // 2 : (i + 1) * nx // 2], "c", axis=0) for i in range(2)
    ]
    near = lax.all_to_all(part, ("q", "x"), 0, 0, tiled=True)
    near, grads = lax.optimization_barrier((near, grads))
    tokens = [lax.all_gather(near[i * nx : (i + 1) * nx], "c", axis=0) for i in range(nq)]

    got_slab = got_second[:, rows_here:].reshape(-1, deep)
    got_place = got_slab[:, LANES].astype(jnp.int32) - 1
    put = jnp.arange(pass_rows)[:, None] == got_place[None, :]
    placed = dot(put.astype(BF16), got_slab[:, :LANES]).astype(BF16)
    refreshed = jnp.where(jnp.any(put, axis=1)[:, None], placed, index_strip)

    terms, pair_relevance = reader(
        my_half.reshape(1), tokens, grads, (w_query, w_key, w_value, w_out), strips, owners
    )
    relevance = pair_relevance[0, :npass].reshape(queries, K)
    refreshed, terms = lax.optimization_barrier((refreshed, terms))
    refreshed = lax.all_gather(refreshed, M, axis=0)
    refreshed = jnp.concatenate([refreshed[i] for i in range(strips)], axis=1)
    terms = lax.all_to_all(terms, IDX, 0, 0, tiled=True)
    grad_query, grad_key, grad_value, grad_out = total(terms)
    return (relevance, grad_query, grad_key, grad_value, grad_out.T, refreshed)


def solution(mesh):
    devices = mesh.devices
    owners, columns = devices.shape
    fine = Mesh(devices.reshape(owners // 8, 4, 2, columns // 2, 2), (*IDX, *M))
    return jax.shard_map(
        shards,
        mesh=fine,
        in_specs=(
            P(IDX, None),
            P(IDX, None),
            P(IDX, None),
            P(IDX),
            P(IDX, None),
            P(IDX, M),
            P(None, M),
            P(None, M),
            P(None, M),
            P(M, None),
            P(IDX, M),
            P(IDX, None),
            P(IDX),
        ),
        out_specs=(
            P(IDX, None),
            P(IDX, M),
            P(IDX, M),
            P(IDX, M),
            P(M, IDX),
            P(IDX, None),
        ),
        check_vma=False,
    )
```

```python
import functools

import jax
import jax.numpy as jnp
from jax import lax
from jax.experimental import pallas as pl
from jax.experimental.pallas import tpu as pltpu
from jax.sharding import Mesh
from jax.sharding import PartitionSpec as P

HEAD_DIM = 64
K = 20
PLEN = 4
CAPS = 2
LANES = 128
REACH = 4096
IDX = ("z", "p", "q")
M = ("x", "c")
ALONG = ("z", "p", "q", "c")
F32 = jnp.float32
BF16 = jnp.bfloat16
ROWS = (((0,), (0,)), ((), ()))
COLS = (((1,), (1,)), ((), ()))


def dot(a, b, dims=None):
    if dims is None:
        return jnp.dot(a, b, preferred_element_type=F32)
    return lax.dot_general(a, b, dims, preferred_element_type=F32)


def reader_kernel(heads, strips, half_ref, *refs):
    token_refs, grad_refs, weight_refs, wo_ref = refs[:2], refs[2:4], refs[4:7], refs[7]
    out_ref, rel_ref = refs[8:]
    nc, nx, count, deep = grad_refs[0].shape
    blocks = 2 * nx * nc
    rows = out_ref.shape[1] // 2
    mine = half_ref[0]

    def grad_block(b):
        x, c = divmod(b, nc)
        return grad_refs[x // nx][c, x % nx]

    def token_block(b, low, high):
        x, c = divmod(b, nc)
        both = [ref[c, x, low:high, :] for ref in token_refs]
        ordered = [jnp.where(mine == 0, both[0], both[1]), jnp.where(mine == 0, both[1], both[0])]
        return jnp.concatenate(ordered, axis=0)

    valid = count // 2 // PLEN
    sums = []
    for ref in token_refs:
        acc = jnp.zeros((16, LANES), F32)
        for b in range(strips):
            x, c = divmod(b, nc)
            acc += ref[c, x, count // 2 :, :LANES].astype(F32)
        sums.append(jnp.sum(acc, axis=0, keepdims=True))
    lane = lax.broadcasted_iota(jnp.int32, (1, LANES), 1)
    token = lax.broadcasted_iota(jnp.int32, (count // 2, LANES), 0)
    begin = lax.broadcasted_iota(jnp.int32, (count // 2, LANES), 1) * PLEN
    of_token = (token >= begin) & (token < begin + PLEN)
    rel = []
    for scores in (
        jnp.where(mine == 0, sums[0], sums[1]),
        jnp.where(mine == 0, sums[1], sums[0]),
    ):
        share = jnp.zeros((1, LANES), F32)
        for first in range(0, valid, K):
            group = (lane >= first) & (lane < first + K)
            top = jnp.max(jnp.where(group, scores, -jnp.inf), axis=1, keepdims=True)
            exps = jnp.where(group, jnp.exp(scores - top), 0.0)
            share += exps / jnp.sum(exps, axis=1, keepdims=True)
        if not rel:
            rel_ref[...] = share
        rel.append(jnp.sum(jnp.where(of_token, share, 0.0), axis=1, keepdims=True))
    rel = jnp.concatenate(rel, axis=0)

    tokens = [token_block(b, 0, count // 2) for b in range(blocks)]
    weighted = [
        (grad_block(b).astype(F32) * rel).astype(BF16) for b in range(blocks)
    ]
    def own(states):
        kept = states[:, :HEAD_DIM]
        for head in range(1, heads):
            kept = jnp.where(mine == head, states[:, head * HEAD_DIM : (head + 1) * HEAD_DIM], kept)
        return kept

    def projected(weight_ref):
        states = dot(tokens[0], weight_ref[:deep])
        for b in range(1, blocks):
            states += dot(tokens[b], weight_ref[b * deep : (b + 1) * deep])
        return own(states.astype(BF16))

    q, k, v = (projected(weight_ref) for weight_ref in weight_refs)
    total = dot(weighted[0], wo_ref[:, :deep], COLS)
    for b in range(1, blocks):
        total += dot(weighted[b], wo_ref[:, b * deep : (b + 1) * deep], COLS)
    c = own(total.astype(BF16))
    passage_i = lax.broadcasted_iota(jnp.int32, (count, count), 0) // PLEN
    passage_j = lax.broadcasted_iota(jnp.int32, (count, count), 1) // PLEN
    logits = jnp.where(passage_i == passage_j, dot(q, k, COLS), -jnp.inf)
    exps = jnp.exp(logits - jnp.max(logits, axis=1, keepdims=True))
    probs = exps / jnp.sum(exps, axis=1, keepdims=True)
    attn = probs.astype(BF16)
    attn_grad = dot(c, v, COLS)
    mean = jnp.sum(attn_grad * probs, axis=1, keepdims=True)
    score_grad = (probs * (attn_grad - mean)).astype(BF16)
    query_grad = dot(score_grad, k).astype(BF16)
    key_grad = dot(score_grad, q, ROWS).astype(BF16)
    value_grad = dot(attn, c, ROWS).astype(BF16)
    context = dot(attn, v).astype(BF16)
    blank = jnp.zeros_like(context)
    token_side = jnp.concatenate([query_grad, key_grad, value_grad, blank], axis=1)
    weighted_side = jnp.concatenate([blank, blank, blank, context], axis=1)
    sides = jnp.concatenate([token_side, weighted_side], axis=0)
    span = deep // rows
    for b in range(blocks):
        term = dot(jnp.concatenate([tokens[b], weighted[b]], axis=0), sides, ROWS).astype(BF16)
        upper, lower = term[:, : 2 * HEAD_DIM], term[:, 2 * HEAD_DIM :]
        out_ref[b * span : (b + 1) * span, :rows, :] = upper.reshape(span, rows, -1)
        out_ref[b * span : (b + 1) * span, rows:, :] = lower.reshape(span, rows, -1)


def reader(half, tokens, out_grad, weights, strips, owners):
    width, inner = weights[0].shape
    vmem = pl.BlockSpec(memory_space=pltpu.VMEM)
    return pl.pallas_call(
        functools.partial(reader_kernel, inner // HEAD_DIM, strips),
        out_shape=(
            jax.ShapeDtypeStruct((owners, 2 * width // owners, 2 * HEAD_DIM), BF16),
            jax.ShapeDtypeStruct((1, LANES), F32),
        ),
        in_specs=[pl.BlockSpec(memory_space=pltpu.SMEM)]
        + [vmem] * 8,
        out_specs=(vmem, vmem),
        compiler_params=pltpu.CompilerParams(vmem_limit_bytes=40 * 1024 * 1024),
        name="reader",
    )(half, *tokens, *out_grad, *weights)


def exact(a, b):
    return dot(a.astype(BF16), b.astype(BF16))


def pack_kernel(at_ref, *refs):
    hbm, out_ref, vmem, rest_ref, sems = refs[:7], refs[7], refs[8:15], refs[15], refs[16]
    copies = [pltpu.make_async_copy(hbm[i], vmem[i], sems.at[i]) for i in range(7)]
    for copy in copies:
        copy.start()
    vocab_ref, index_ref, slab_ref, slab_ids_ref, ids_ref, owner_ref, row_ref = vmem
    core, strip = at_ref[0], at_ref[1]
    peers, stride, deep = out_ref.shape
    vocab_rows = vocab_ref.shape[0]
    copies[0].wait()
    sends = [
        pltpu.make_async_copy(vocab_ref, out_ref.at[peer, :vocab_rows, :], sems.at[7 + peer])
        for peer in range(peers)
    ]
    for send in sends:
        send.start()
    for copy in copies[1:]:
        copy.wait()
    pass_rows = index_ref.shape[0]
    folded = pass_rows // 2
    asked = vocab_rows + folded
    columns = pl.ds(pl.multiple_of(strip * LANES, LANES), LANES)
    index = index_ref[:, columns]
    slab, plen, npass = slab_ref.shape[0], ids_ref.shape[0], ids_ref.shape[1]

    def places(owner, core):
        z, y = owner // peers, lax.rem(owner, peers)
        return jnp.where(core == 0, z, y), jnp.where(core == 0, y, z)

    def coded(owner, row):
        first, second = places(owner, 1 - core)
        code = second * REACH + first * stride + row
        return (code // LANES).astype(F32), lax.rem(code, LANES).astype(F32)

    ids = ids_ref[...]
    high, low = coded(ids // vocab_rows, lax.rem(ids, vocab_rows))
    lane = lax.broadcasted_iota(jnp.int32, (npass, deep), 1)
    passage = lax.broadcasted_iota(jnp.int32, (npass, deep), 0)
    high_row, low_row = jnp.zeros((1, deep), F32), jnp.zeros((1, deep), F32)
    for i in range(plen):
        to = (lane == passage * plen + i).astype(F32)
        high_row += exact(high[i : i + 1], to)
        low_row += exact(low[i : i + 1], to)
    high, low = coded(owner_ref[...], vocab_rows + lax.rem(row_ref[...], folded))
    to = (lane == passage + plen * npass).astype(F32)
    high_row += exact(high, to)
    low_row += exact(low, to)
    lane = lax.broadcasted_iota(jnp.int32, (1, deep), 1)
    none = peers * REACH - 1
    high_row = jnp.where(lane < (plen + 1) * npass, high_row, float(none // LANES))
    low_row = jnp.where(lane < (plen + 1) * npass, low_row, float(none % LANES))
    line = lax.broadcasted_iota(jnp.int32, (16, deep), 0)
    wanted = jnp.where(line == 0, high_row, jnp.where(line == 1, low_row, 0.0)).astype(BF16)

    slab_ids = slab_ids_ref[...]
    owner, row = slab_ids // pass_rows, lax.rem(slab_ids, pass_rows)
    i = lax.broadcasted_iota(jnp.int32, (slab, slab), 0)
    j = lax.broadcasted_iota(jnp.int32, (slab, slab), 1)
    owner_column = jnp.sum(jnp.where(i == j, owner.astype(F32), 0.0), axis=1, keepdims=True)
    place_column = jnp.sum(jnp.where(i == j, (row + 1).astype(F32), 0.0), axis=1, keepdims=True)
    before = jnp.where((owner_column == owner.astype(F32)) & (i < j), 1.0, 0.0)
    first, second = places(owner, core)
    slot = ((first * peers + second) * CAPS).astype(F32) + jnp.sum(before, axis=0, keepdims=True)
    slots = lax.broadcasted_iota(jnp.int32, (peers * peers * CAPS, slab), 0).astype(F32)
    select = jnp.where(slots == slot, 1.0, 0.0).astype(BF16)
    place = jnp.broadcast_to(place_column, (slab, deep - LANES)).astype(BF16)
    slab_out = dot(select, jnp.concatenate([slab_ref[:, columns], place], axis=1)).astype(BF16)

    index = jnp.concatenate([index[:folded], index[folded:]], axis=1)
    for peer in range(peers):
        rest_ref[peer, :folded, :] = index
        rest_ref[peer, folded : folded + 16, :] = wanted
        rest_ref[peer, folded + 16 :, :] = slab_out[
            peer * peers * CAPS : (peer + 1) * peers * CAPS
        ]
    last = pltpu.make_async_copy(rest_ref, out_ref.at[:, vocab_rows:, :], sems.at[7 + peers])
    last.start()
    for send in sends:
        send.wait()
    last.wait()


def pack(core, strip, vocab, index, slab, slab_ids, ids, owner, row, peers):
    operands = (vocab, index, slab, slab_ids, ids, owner, row)
    rows = vocab.shape[0] + index.shape[0] // 2 + 16 + peers * CAPS
    return pl.pallas_call(
        pack_kernel,
        out_shape=jax.ShapeDtypeStruct((peers, rows, vocab.shape[1]), BF16),
        in_specs=[pl.BlockSpec(memory_space=pltpu.SMEM)]
        + [pl.BlockSpec(memory_space=pltpu.HBM)] * 7,
        out_specs=pl.BlockSpec(memory_space=pltpu.HBM),
        scratch_shapes=[pltpu.VMEM(operand.shape, operand.dtype) for operand in operands]
        + [
            pltpu.VMEM((peers, rows - vocab.shape[0], vocab.shape[1]), BF16),
            pltpu.SemaphoreType.DMA((8 + peers,)),
        ],
        compiler_params=pltpu.CompilerParams(vmem_limit_bytes=60 * 1024 * 1024),
        name="pack",
    )(jnp.stack([core, strip]), *operands)


def spread_kernel(got_ref, query_ref, high_ref, out_ref):
    count, passages = out_ref.shape[1] - 16, query_ref.shape[0]

    def summed(low, high):
        acc = got_ref[0, low:high, :].astype(F32)
        for source in range(1, got_ref.shape[0]):
            acc += got_ref[source, low:high, :].astype(F32)
        return acc.astype(BF16)

    rows = summed(0, count)
    products = summed(count, count + passages).astype(F32) * query_ref[...].astype(F32)
    low = jnp.sum(products[:, :LANES], axis=1, keepdims=True)
    high = jnp.sum(products[:, LANES:], axis=1, keepdims=True)
    scores = jnp.where(high_ref[...] > 0, high, low)
    p = lax.broadcasted_iota(jnp.int32, (passages, out_ref.shape[2]), 0)
    lane = lax.broadcasted_iota(jnp.int32, (passages, out_ref.shape[2]), 1)
    scores = jnp.sum(jnp.where(p == lane, scores, 0.0), axis=0, keepdims=True)
    parts = []
    for _ in range(3):
        parts.append(scores.astype(BF16).astype(F32))
        scores = scores - parts[-1]
    line = lax.broadcasted_iota(jnp.int32, (16, out_ref.shape[2]), 0)
    block = jnp.zeros((16, out_ref.shape[2]), F32)
    for i, part in enumerate(parts):
        block = jnp.where(line == i, part, block)
    block = block.astype(BF16)
    for peer in range(out_ref.shape[0]):
        out_ref[peer, :count, :] = rows
        out_ref[peer, count:, :] = block


def spread(got, query, high, count, peers):
    vmem = pl.BlockSpec(memory_space=pltpu.VMEM)
    return pl.pallas_call(
        spread_kernel,
        out_shape=jax.ShapeDtypeStruct((peers, count + 16, got.shape[2]), BF16),
        in_specs=[vmem] * 3,
        out_specs=vmem,
        compiler_params=pltpu.CompilerParams(vmem_limit_bytes=32 * 1024 * 1024),
        name="spread",
    )(got, query, high)


def total_kernel(terms_ref, *out_refs):
    rows = terms_ref.shape[1] // 2
    sums = []
    for half in range(2):
        acc = terms_ref[half].astype(F32)
        for i in range(2 + half, terms_ref.shape[0], 2):
            acc += terms_ref[i].astype(F32)
        sums.append(acc)
    for i, out_ref in enumerate(out_refs):
        top, left = divmod(i, 2)
        out_ref[...] = jnp.concatenate(
            [
                acc[top * rows : (top + 1) * rows, left * HEAD_DIM : (left + 1) * HEAD_DIM]
                for acc in sums
            ],
            axis=1,
        )


def total(terms):
    rows, width = terms.shape[1] // 2, terms.shape[2]
    vmem = pl.BlockSpec(memory_space=pltpu.VMEM)
    return pl.pallas_call(
        total_kernel,
        out_shape=(jax.ShapeDtypeStruct((rows, width), F32),) * 4,
        in_specs=[vmem],
        out_specs=(vmem,) * 4,
        compiler_params=pltpu.CompilerParams(vmem_limit_bytes=32 * 1024 * 1024),
        name="total",
    )(terms)


def shards(
    index_emb,
    query_emb,
    passage_owner,
    passage_row,
    token_ids,
    vocab_table,
    w_query,
    w_key,
    w_value,
    w_out,
    out_grad,
    slab_emb,
    slab_ids,
):
    nz, nq = lax.axis_size("z"), lax.axis_size("q")
    ny = lax.axis_size("p") * nq
    owners = nz * ny
    swap = [(0, 1), (1, 0)]
    my_z = lax.axis_index("z")
    my_y = lax.axis_index(("p", "q"))
    my_half = lax.axis_index("q")
    pass_rows, width = index_emb.shape
    queries = query_emb.shape[0]
    npass, plen = token_ids.shape
    count = npass * plen
    vocab_rows = vocab_table.shape[0]
    strips = width // LANES
    strip = lax.rem(lax.axis_index(M), strips)

    def my_strip(array):
        return lax.dynamic_slice_in_dim(array, strip * LANES, LANES, axis=1)

    cores = lax.axis_size("c")
    my_core = lax.axis_index("c")
    at_z = [[(z * ny + y) * cores for z in range(nz)] for y in range(ny)]
    at_y = [[(z * ny + y) * cores for y in range(ny)] for z in range(nz)]
    first_groups = at_y + [[i + 1 for i in group] for group in at_z]
    second_groups = at_z + [[i + 1 for i in group] for group in at_y]
    second = jnp.where(my_core == 0, my_z, my_y)

    deep = vocab_table.shape[1]
    index_strip = my_strip(index_emb)
    folded = pass_rows // 2
    asked = vocab_rows + folded
    held = asked + 16
    stride = held + ny * CAPS
    spare = -npass % 16
    rows_here = count + npass + spare
    message = pack(
        1 - my_core,
        strip,
        vocab_table,
        index_emb,
        slab_emb,
        slab_ids[None],
        token_ids.T,
        passage_owner.T,
        passage_row[None],
        nz,
    )
    got_first = lax.all_to_all(
        message,
        ALONG,
        0,
        0,
        axis_index_groups=first_groups,
        tiled=True,
    )
    other = lax.ppermute(out_grad, "q", swap)
    got_first, other = lax.optimization_barrier((got_first, other))
    along_x = lax.all_gather(jnp.concatenate([out_grad, other], axis=0), "x", axis=0)
    wanted = lax.all_gather(got_first[:, asked : asked + 2].reshape(1, -1, deep), "c", axis=0, tiled=True)
    wanted = lax.dynamic_index_in_dim(wanted, 1 - my_core, axis=0, keepdims=False)
    wanted = wanted.reshape(ny, 2, deep).astype(jnp.int32)[:, :, :rows_here]
    rows_at = wanted[:, 0] * LANES + wanted[:, 1] - second * REACH
    slab_at = (
        held
        + jnp.arange(ny)[:, None, None] * CAPS
        + jnp.arange(nz)[None, :, None] * stride
        + jnp.arange(CAPS)[None, None, :]
    ).reshape(ny, nz * CAPS)
    at = jnp.concatenate([rows_at, slab_at], axis=1)
    one_hot = (at.reshape(-1)[:, None] == jnp.arange(nz * stride)[None, :]).astype(BF16)
    served = dot(one_hot, got_first.reshape(nz * stride, deep)).astype(BF16)
    got_second = lax.all_to_all(
        served.reshape(*at.shape, deep),
        ALONG,
        0,
        0,
        axis_index_groups=second_groups,
        tiled=True,
    )
    got_second, along_x = lax.optimization_barrier((got_second, along_x))

    query = my_strip(query_emb)
    query = jnp.repeat(jnp.concatenate([query, query], axis=1), K, axis=0)
    query = jnp.pad(query, ((0, spare), (0, 0)))
    high = jnp.pad((passage_row >= folded).astype(jnp.int32), (0, spare))[:, None]
    nx = lax.axis_size("x")
    part = spread(got_second, query, high, count, nq * nx)
    grads = [
        lax.all_gather(along_x[i * nx // 2 : (i + 1) * nx // 2], "c", axis=0) for i in range(2)
    ]
    near = lax.all_to_all(part, ("q", "x"), 0, 0, tiled=True)
    near, grads = lax.optimization_barrier((near, grads))
    tokens = [lax.all_gather(near[i * nx : (i + 1) * nx], "c", axis=0) for i in range(nq)]

    got_slab = got_second[:, rows_here:].reshape(-1, deep)
    got_place = got_slab[:, LANES].astype(jnp.int32) - 1
    put = jnp.arange(pass_rows)[:, None] == got_place[None, :]
    placed = dot(put.astype(BF16), got_slab[:, :LANES]).astype(BF16)
    refreshed = jnp.where(jnp.any(put, axis=1)[:, None], placed, index_strip)

    terms, pair_relevance = reader(
        my_half.reshape(1), tokens, grads, (w_query, w_key, w_value, w_out), strips, owners
    )
    relevance = pair_relevance[0, :npass].reshape(queries, K)
    refreshed, terms = lax.optimization_barrier((refreshed, terms))
    refreshed = lax.all_gather(refreshed, M, axis=0)
    refreshed = jnp.concatenate([refreshed[i] for i in range(strips)], axis=1)
    terms = lax.all_to_all(terms, IDX, 0, 0, tiled=True)
    grad_query, grad_key, grad_value, grad_out = total(terms)
    return (relevance, grad_query, grad_key, grad_value, grad_out.T, refreshed)


def solution(mesh):
    devices = mesh.devices
    owners, columns = devices.shape
    fine = Mesh(devices.reshape(owners // 8, 4, 2, columns // 2, 2), (*IDX, *M))
    return jax.shard_map(
        shards,
        mesh=fine,
        in_specs=(
            P(IDX, None),
            P(IDX, None),
            P(IDX, None),
            P(IDX),
            P(IDX, None),
            P(IDX, M),
            P(None, M),
            P(None, M),
            P(None, M),
            P(M, None),
            P(IDX, M),
            P(IDX, None),
            P(IDX),
        ),
        out_specs=(
            P(IDX, None),
            P(IDX, M),
            P(IDX, M),
            P(IDX, M),
            P(M, IDX),
            P(IDX, None),
        ),
        check_vma=False,
    )
```
